32 devices in a mesh: video: 4 (over y, core), frame: 8 (over z, x).
Axes of the slice: x: 2, y: 2, z: 4, core: 2. Of those that a mesh axis runs over, the one named last changes fastest.
Arguments:
- hidden: bfloat16 [64, 256, 320], P(('video', 'frame')), parts along dimension 0, may hold values from -6 to 6
- ref_feats: bfloat16 [1024, 320], P(('video', 'frame')), parts along dimension 0, may hold values from -6 to 6
- frame_index: int32 [64], P(('video', 'frame')), parts along dimension 0, may hold values from 0 to 31
- step_index: int32 [1], replicated, may hold values from 0 to 999
- temb_table: bfloat16 [1000, 320], replicated, may hold values from -3 to 3
- norm_gain_1: float32 [320], replicated, may hold values from 0.1 to 1.9
- norm_gain_2: float32 [320], replicated, may hold values from 0.1 to 1.9
- sp_query: bfloat16 [320, 320], replicated, as said below
- sp_key: bfloat16 [320, 320], replicated, as said below
- sp_value: bfloat16 [320, 320], replicated, may hold values from -0.3125 to 0.3125
- sp_out: bfloat16 [320, 320], replicated, may hold values from -0.625 to 0.625
- tm_query: bfloat16 [320, 320], replicated, as said below
- tm_key: bfloat16 [320, 320], replicated, as said below
- tm_value: bfloat16 [320, 320], replicated, may hold values from -0.3125 to 0.3125
- tm_out: bfloat16 [320, 320], replicated, may hold values from -0.625 to 0.625
Outputs:
- mixed: bfloat16 [64, 256, 320], P(('video', 'frame')), parts along dimension 0
The draws below stay inside these ranges and needn't reach their ends.
There are 4 independent parts, one for each index of `video`. The reference program is written for one: setup_inputs(seed, part) draws one part's arguments, and reference() takes and returns one part's arrays. A program takes and returns all parts, laid end to end along the dimension named above; an argument that names none is the same for every part. Nothing has to cross between parts.
Inputs may be any that keep to these rules, and one draw needn't show every extreme that they name: `sp_query`: a projection matrix. `sp_key`: a projection matrix. `tm_query`: a projection matrix. `tm_key`: a projection matrix.
All inputs are finite; a program needn't handle non-finite values.
Results may differ from the reference program's by a relative error of at most 0.015.
The reference program's roundings to bfloat16 on the way count: a program that leaves them out, or rounds other values in their place, can miss the bound.
Values may be sent and summed in bfloat16 or wider, within the bound.
A program may use at most 64 MiB of HBM per device.

```python
import math
import jax
import jax.numpy as jnp
from jax import lax

C = 320
HEADS = 8
POS = 256
FRAMES = 16
STEPS = 1000


def paired_draw(key, own_tag):
    key = jax.random.fold_in(key, own_tag)
    own = jax.random.normal(key, (C, C), jnp.float32)
    matrix = jnp.clip(own, -6.0, 6.0) * (4.0 / C) ** 0.5
    return matrix.astype(jnp.bfloat16)


def draw_sp_query(key, part):
    return paired_draw(key, 1)


def draw_sp_key(key, part):
    return paired_draw(key, 2)


def draw_tm_query(key, part):
    return paired_draw(key, 3)


def draw_tm_key(key, part):
    return paired_draw(key, 4)


def touch_ends(result, own_key, least, largest):
    shape = result.shape
    spot = [jax.random.randint(jax.random.fold_in(own_key, axis), (), 0, shape[axis]) for axis in range(len(shape))]
    result = result.at[tuple(spot)].set(least)
    longest = shape.index(max(shape))
    spot[longest] = (spot[longest] + 1) % shape[longest]
    return result.at[tuple(spot)].set(largest)


def levels(own_key, dims, split, smallest, top_value):
    loudness, own = 1.0, jax.random.fold_in(own_key, 6)
    for position, parts in split:
        draws = jnp.exp(jax.random.uniform(jax.random.fold_in(own, position), (parts,), jnp.float32, smallest / len(split), top_value / len(split)))
        loudness = loudness * jnp.repeat(draws, dims[position] // parts).reshape([-1 if axis == position else 1 for axis in range(len(dims))])
    return loudness


def bell_draw(rng, extent, spread, most, shards=(), held_as=jnp.bfloat16):
    factor_of = levels(rng, extent, shards, -0.22, 0.18) if shards else 1.0
    drawn = jax.random.normal(rng, extent, jnp.float32) * spread * factor_of
    return jnp.minimum(jnp.maximum(drawn, -most), most).astype(held_as)


def setup_inputs(seed: int = 0, part: int = 0) -> dict:
    key_list = jax.random.split(jax.random.key(seed), 16)
    part_splits = jax.random.split(jax.random.fold_in(key_list[15], part), 16)
    hidden = bell_draw(part_splits[0], (FRAMES, POS, C), 1.0, 6.0, ((0, 8),))
    ref_feats = bell_draw(part_splits[1], (POS, C), 1.0, 6.0, ((0, 8),))
    frame_index = touch_ends(jax.random.randint(part_splits[2], (FRAMES,), 0, 2 * FRAMES), jax.random.fold_in(part_splits[2], 1), 0, (2 * FRAMES) - 1).astype(jnp.int32)
    step_index = jax.random.randint(key_list[3], (1,), 0, STEPS).astype(jnp.int32)
    temb_table = bell_draw(key_list[4], (STEPS, C), 0.5, 3.0)
    norm_gain_1 = jnp.clip(1.0 + 0.18 * jax.random.normal(key_list[5], (C,), jnp.float32), 0.1, 1.9)
    norm_gain_2 = jnp.clip(1.0 + 0.18 * jax.random.normal(key_list[6], (C,), jnp.float32), 0.1, 1.9)
    sp_query = draw_sp_query(jax.random.fold_in(key_list[15], 71), part)
    sp_key = draw_sp_key(jax.random.fold_in(key_list[15], 71), part)
    sp_value = bell_draw(key_list[9], (C, C), C ** -0.5, 0.3125)
    sp_out = bell_draw(key_list[10], (C, C), (C // 4) ** -0.5, 0.625)
    tm_query = draw_tm_query(jax.random.fold_in(key_list[15], 71), part)
    tm_key = draw_tm_key(jax.random.fold_in(key_list[15], 71), part)
    tm_value = bell_draw(key_list[13], (C, C), C ** -0.5, 0.3125)
    tm_out = bell_draw(key_list[14], (C, C), (C // 4) ** -0.5, 0.625)
    return dict(hidden=hidden, ref_feats=ref_feats, frame_index=frame_index, step_index=step_index, temb_table=temb_table, norm_gain_1=norm_gain_1, norm_gain_2=norm_gain_2, sp_query=sp_query, sp_key=sp_key, sp_value=sp_value, sp_out=sp_out, tm_query=tm_query, tm_key=tm_key, tm_value=tm_value, tm_out=tm_out)


def layer_norm(values, gain):
    mean = lax.optimization_barrier(jnp.mean(values, axis=-1, keepdims=True))
    centered = values - mean
    var = lax.optimization_barrier(jnp.mean(centered * centered, axis=-1, keepdims=True))
    return centered * lax.rsqrt(var + 1e-05) * gain

def positional(frame_index):
    chan = jnp.arange(C)
    freq = jnp.exp(-(chan // 2 * 2).astype(jnp.float32) / C * math.log(10000.0))
    phase = (chan % 2).astype(jnp.float32) * (math.pi / 2)
    return jnp.sin(frame_index.astype(jnp.float32)[:, None] * freq[None, :] + phase[None, :])

def attend(query, keys, values):
    count = query.shape[0]
    q = query.astype(jnp.float32).reshape(count, HEADS, C // HEADS)
    k = keys.astype(jnp.float32).reshape(keys.shape[0], HEADS, C // HEADS)
    v = values.astype(jnp.float32).reshape(values.shape[0], HEADS, C // HEADS)
    scores = jnp.einsum('qhd,khd->hqk', q, k) / math.sqrt(C // HEADS)
    probs = jax.nn.softmax(scores, axis=-1).astype(jnp.bfloat16)
    out = jnp.einsum('hqk,khd->qhd', probs.astype(jnp.float32), v)
    return out.astype(jnp.bfloat16).reshape(count, C)

def reference(hidden, ref_feats, frame_index, step_index, temb_table, norm_gain_1, norm_gain_2, sp_query, sp_key, sp_value, sp_out, tm_query, tm_key, tm_value, tm_out):
    temb = lax.dynamic_slice_in_dim(temb_table, step_index[0], 1, 0).astype(jnp.float32)
    base = hidden.astype(jnp.float32) + temb[None, :, :]
    normed_1 = layer_norm(base, norm_gain_1).astype(jnp.bfloat16)
    ref_normed = layer_norm(ref_feats.astype(jnp.float32), norm_gain_1).astype(jnp.bfloat16)
    ref_k = jnp.dot(ref_normed, sp_key, preferred_element_type=jnp.float32).astype(jnp.bfloat16)
    ref_v = jnp.dot(ref_normed, sp_value, preferred_element_type=jnp.float32).astype(jnp.bfloat16)

    def spatial(frame_rows):
        q1 = jnp.dot(frame_rows, sp_query, preferred_element_type=jnp.float32).astype(jnp.bfloat16)
        k1 = jnp.dot(frame_rows, sp_key, preferred_element_type=jnp.float32).astype(jnp.bfloat16)
        v1 = jnp.dot(frame_rows, sp_value, preferred_element_type=jnp.float32).astype(jnp.bfloat16)
        attn = attend(q1, jnp.concatenate([k1, ref_k], axis=0), jnp.concatenate([v1, ref_v], axis=0))
        return jnp.dot(attn, sp_out, preferred_element_type=jnp.float32)
    mid = base + lax.map(spatial, normed_1)
    pe = positional(frame_index)
    normed_2 = (layer_norm(mid, norm_gain_2) + pe[:, None, :]).astype(jnp.bfloat16)
    q2 = jnp.dot(normed_2, tm_query, preferred_element_type=jnp.float32).astype(jnp.bfloat16)
    k2 = jnp.dot(normed_2, tm_key, preferred_element_type=jnp.float32).astype(jnp.bfloat16)
    v2 = jnp.dot(normed_2, tm_value, preferred_element_type=jnp.float32).astype(jnp.bfloat16)

    def temporal(triple):
        return attend(triple[0], triple[1], triple[2])
    attn_2 = lax.map(temporal, (jnp.transpose(q2, (1, 0, 2)), jnp.transpose(k2, (1, 0, 2)), jnp.transpose(v2, (1, 0, 2))))
    attn_2 = jnp.transpose(attn_2, (1, 0, 2))
    return (mid + jnp.dot(attn_2, tm_out, preferred_element_type=jnp.float32)).astype(jnp.bfloat16)
```

```python
import functools
import math

import jax
import jax.numpy as jnp
from jax import lax
from jax.experimental import pallas as pl
from jax.experimental.pallas import tpu as pltpu
from jax.sharding import PartitionSpec as P

HEADS = 8


def layer_norm(values, gain):
    mean = jnp.mean(values, axis=-1, keepdims=True)
    centered = values - mean
    var = jnp.mean(centered * centered, axis=-1, keepdims=True)
    return centered * lax.rsqrt(var + 1e-05) * gain


def positional(frame_index, width):
    chan = jnp.arange(width)
    freq = jnp.exp(-(chan // 2 * 2).astype(jnp.float32) / width * math.log(10000.0))
    phase = (chan % 2).astype(jnp.float32) * (math.pi / 2)
    return jnp.sin(frame_index.astype(jnp.float32)[:, None] * freq[None, :] + phase[None, :])


def project(rows, weight):
    return jnp.dot(rows, weight, preferred_element_type=jnp.float32).astype(jnp.bfloat16)


def temporal_attend(query, keys, values):
    frames, count, width = query.shape
    head_dim = width // HEADS
    q = query.reshape(frames, count, HEADS, head_dim)
    k = keys.reshape(frames, count, HEADS, head_dim)
    v = values.reshape(frames, count, HEADS, head_dim)
    scores = jnp.einsum("fnhd,gnhd->nhfg", q, k, preferred_element_type=jnp.float32) / math.sqrt(
        head_dim
    )
    probs = jax.nn.softmax(scores, axis=-1).astype(jnp.bfloat16)
    out = jnp.einsum("nhfg,gnhd->fnhd", probs, v, preferred_element_type=jnp.float32)
    return out.astype(jnp.bfloat16).reshape(frames, count, width)


def flatten_block(block):
    return block.reshape(block.shape[0], block.shape[2], block.shape[3])


def on_device_plain(
    hidden,
    ref_feats,
    frame_index,
    step_index,
    temb_table,
    norm_gain_1,
    norm_gain_2,
    sp_query,
    sp_key,
    sp_value,
    sp_out,
    tm_query,
    tm_key,
    tm_value,
    tm_out,
):
    frames_here, positions, width = hidden.shape
    head_dim = width // HEADS
    blocks = lax.axis_size("frame")
    share = positions // blocks
    temb = lax.dynamic_slice_in_dim(temb_table, step_index[0], 1, 0).astype(jnp.float32)
    base = hidden.astype(jnp.float32) + temb[None, :, :]
    normed_1 = layer_norm(base, norm_gain_1).astype(jnp.bfloat16)
    ref_local = layer_norm(ref_feats.astype(jnp.float32), norm_gain_1).astype(jnp.bfloat16)
    ref_all = lax.all_gather(ref_local, "frame", axis=0, tiled=True)
    ref_k = project(ref_all, sp_key)
    ref_v = project(ref_all, sp_value)
    q1 = project(normed_1, sp_query).reshape(frames_here, positions, HEADS, head_dim)
    k1 = project(normed_1, sp_key).reshape(frames_here, positions, HEADS, head_dim)
    v1 = project(normed_1, sp_value).reshape(frames_here, positions, HEADS, head_dim)
    ref_kh = ref_k.reshape(positions, HEADS, head_dim)
    ref_vh = ref_v.reshape(positions, HEADS, head_dim)
    scale = 1.0 / math.sqrt(head_dim)
    self_scores = jnp.einsum("fqhd,fkhd->fhqk", q1, k1, preferred_element_type=jnp.float32) * scale
    ref_scores = (
        jnp.einsum("fqhd,khd->fhqk", q1, ref_kh, preferred_element_type=jnp.float32) * scale
    )
    top = jnp.maximum(
        jnp.max(self_scores, axis=-1, keepdims=True), jnp.max(ref_scores, axis=-1, keepdims=True)
    )
    self_exp = jnp.exp(self_scores - top)
    ref_exp = jnp.exp(ref_scores - top)
    total = jnp.sum(self_exp, axis=-1, keepdims=True) + jnp.sum(ref_exp, axis=-1, keepdims=True)
    self_probs = (self_exp / total).astype(jnp.bfloat16)
    ref_probs = (ref_exp / total).astype(jnp.bfloat16)
    attn_1 = jnp.einsum("fhqk,fkhd->fqhd", self_probs, v1, preferred_element_type=jnp.float32)
    attn_1 = attn_1 + jnp.einsum(
        "fhqk,khd->fqhd", ref_probs, ref_vh, preferred_element_type=jnp.float32
    )
    attn_1 = attn_1.astype(jnp.bfloat16).reshape(frames_here, positions, width)
    mid = base + jnp.dot(attn_1, sp_out, preferred_element_type=jnp.float32)
    encoding = positional(frame_index, width)
    normed_2 = (layer_norm(mid, norm_gain_2) + encoding[:, None, :]).astype(jnp.bfloat16)
    moved = (
        project(normed_2, tm_query).reshape(frames_here, blocks, share, width),
        project(normed_2, tm_key).reshape(frames_here, blocks, share, width),
        project(normed_2, tm_value).reshape(frames_here, blocks, share, width),
    )
    result = temporal_attend(
        flatten_block(lax.all_to_all(moved[0], "frame", split_axis=1, concat_axis=0, tiled=True)),
        flatten_block(lax.all_to_all(moved[1], "frame", split_axis=1, concat_axis=0, tiled=True)),
        flatten_block(lax.all_to_all(moved[2], "frame", split_axis=1, concat_axis=0, tiled=True)),
    )
    attn_2 = result.reshape(result.shape[0], 1, result.shape[1], result.shape[2])
    returned = lax.all_to_all(attn_2, "frame", split_axis=0, concat_axis=1, tiled=True).reshape(
        frames_here, positions, width
    )
    return (mid + jnp.dot(returned, tm_out, preferred_element_type=jnp.float32)).astype(
        jnp.bfloat16
    )


def head_span(head, head_dim, width):
    low = head * head_dim
    high = low + head_dim
    return low, high, low // 128 * 128, min(width, -(-high // 128) * 128)


def lane_mask(low, high, first, last):
    lane = lax.broadcasted_iota(jnp.int32, (1, last - first), 1) + first
    return jnp.where((lane >= low) & (lane < high), 1.0, 0.0).astype(jnp.bfloat16)


def attend_heads(q, key_parts, value_parts, width, allowed=None):
    head_dim = width // HEADS
    factor = math.log2(math.e) / math.sqrt(head_dim)
    columns = [None] * (-(-width // 128))
    for head in range(HEADS):
        low, high, first, last = head_span(head, head_dim, width)
        picked = q[:, first:last] * lane_mask(low, high, first, last)
        scores = [
            lax.dot_general(
                picked,
                keys(first, last),
                (((1,), (1,)), ((), ())),
                preferred_element_type=jnp.float32,
            )
            for keys in key_parts
        ]
        if allowed is not None:
            scores = [jnp.where(allowed, s, -1e30) for s in scores]
        top = functools.reduce(jnp.maximum, [jnp.max(s, axis=-1, keepdims=True) for s in scores])
        exps = [jnp.exp2((s - top) * factor) for s in scores]
        total = sum(jnp.sum(e, axis=-1, keepdims=True) for e in exps)
        inverse = 1.0 / total
        result = None
        for e, values in zip(exps, value_parts):
            probs = (e * inverse).astype(jnp.bfloat16)
            part = jnp.dot(probs, values(first, last), preferred_element_type=jnp.float32)
            result = part if result is None else result + part
        for block in range(first // 128, -(-last // 128)):
            start, end = block * 128, min(width, block * 128 + 128)
            piece = result[:, start - first : end - first]
            if columns[block] is not None:
                lane = lax.broadcasted_iota(jnp.int32, (1, end - start), 1) + start
                piece = jnp.where(lane >= low, piece, columns[block])
            columns[block] = piece
    return jnp.concatenate(columns, axis=-1)


def fused_kernel(
    blocks,
    step_ref,
    frame_ref,
    hidden_ref,
    ref_ref,
    temb_ref,
    gain1_ref,
    gain2_ref,
    spq_ref,
    spk_ref,
    spv_ref,
    spo_ref,
    tmq_ref,
    tmk_ref,
    tmv_ref,
    tmo_ref,
    out_ref,
    ref_buf,
    q_buf,
    k_buf,
    v_buf,
    rk_buf,
    rv_buf,
    mid_buf,
    pe_buf,
    fwd_out,
    fwd_in,
    bwd_out,
    bwd_in,
    ref_send,
    ref_recv,
    fwd_send,
    fwd_recv,
    bwd_send,
    bwd_recv,
):
    me = lax.axis_index("frame")
    frames_here, _, halves, rows, width = hidden_ref.shape
    count = blocks * rows
    frames = frames_here * blocks
    bf16 = jnp.bfloat16

    def peer(shift):
        return lax.rem(me + shift, blocks)

    barrier = pltpu.get_barrier_semaphore()
    for shift in range(1, blocks):
        pl.semaphore_signal(
            barrier, inc=1, device_id={"frame": peer(shift)}, device_id_type=pl.DeviceIdType.MESH
        )

    gain1 = gain1_ref[...]
    ref_buf[me] = layer_norm(ref_ref[...].astype(jnp.float32), gain1).astype(bf16)
    pl.semaphore_wait(barrier, blocks - 1)

    def ref_copy(shift):
        return pltpu.make_async_remote_copy(
            src_ref=ref_buf.at[me],
            dst_ref=ref_buf.at[me],
            send_sem=ref_send.at[shift - 1],
            recv_sem=ref_recv.at[shift - 1],
            device_id={"frame": peer(shift)},
            device_id_type=pl.DeviceIdType.MESH,
        )

    def fwd_copy(half, shift):
        return pltpu.make_async_remote_copy(
            src_ref=fwd_out.at[half, peer(shift)],
            dst_ref=fwd_in.at[half, me],
            send_sem=fwd_send.at[half, shift - 1],
            recv_sem=fwd_recv.at[half, shift - 1],
            device_id={"frame": peer(shift)},
            device_id_type=pl.DeviceIdType.MESH,
        )

    def bwd_copy(half, shift):
        return pltpu.make_async_remote_copy(
            src_ref=bwd_out.at[half, peer(shift)],
            dst_ref=bwd_in.at[half, me],
            send_sem=bwd_send.at[half, shift - 1],
            recv_sem=bwd_recv.at[half, shift - 1],
            device_id={"frame": peer(shift)},
            device_id_type=pl.DeviceIdType.MESH,
        )

    for shift in range(1, blocks):
        ref_copy(shift).start()

    step = step_ref[0]
    rows8 = temb_ref[step // 8].astype(jnp.float32)
    row_id = lax.broadcasted_iota(jnp.int32, rows8.shape, 0)
    temb = jnp.sum(jnp.where(row_id == step % 8, rows8, 0.0), axis=0, keepdims=True)

    chan = lax.broadcasted_iota(jnp.int32, (1, width), 1)
    freq = jnp.exp(-(chan // 2 * 2).astype(jnp.float32) / width * math.log(10000.0))
    phase = (chan % 2).astype(jnp.float32) * (math.pi / 2)
    for f in range(frames_here):
        pe_buf[f] = jnp.sin(frame_ref[f].astype(jnp.float32) * freq + phase)

    for f in range(frames_here):
        normed = []
        for half in range(halves):
            base = hidden_ref[f, :, half].reshape(count, width).astype(jnp.float32) + temb
            mid_buf[half, f] = base
            normed.append(layer_norm(base, gain1).astype(bf16))
        normed = jnp.concatenate(normed, axis=0)
        query = project(normed, spq_ref[...])
        for half in range(halves):
            q_buf[half, f] = query[half * count : (half + 1) * count]
        k_buf[f] = project(normed, spk_ref[...])
        v_buf[f] = project(normed, spv_ref[...])

    for shift in range(1, blocks):
        ref_copy(shift).wait_recv()
    ref_all = ref_buf[...].reshape(-1, width)
    rk_buf[...] = project(ref_all, spk_ref[...])
    rv_buf[...] = project(ref_all, spv_ref[...])

    gain2 = gain2_ref[...]

    def spatial(half, carry):
        for f in range(frames_here):
            attn = attend_heads(
                q_buf[half, f],
                [lambda a, b: k_buf[f, :, a:b], lambda a, b: rk_buf[:, a:b]],
                [lambda a, b: v_buf[f, :, a:b], lambda a, b: rv_buf[:, a:b]],
                width,
            ).astype(bf16)
            mid = mid_buf[half, f] + jnp.dot(
                attn, spo_ref[...], preferred_element_type=jnp.float32
            )
            mid_buf[half, f] = mid
            normed = (layer_norm(mid, gain2) + pe_buf[f]).astype(bf16)
            fwd_out[half, :, f] = normed.reshape(blocks, rows, width)
        for shift in range(1, blocks):
            fwd_copy(half, shift).start()
        fwd_in[half, me] = fwd_out[half, me]
        return carry

    lax.fori_loop(0, halves, spatial, 0)

    group = 8
    size = frames * group
    row_pos = lax.broadcasted_iota(jnp.int32, (size, size), 0) % group
    col_pos = lax.broadcasted_iota(jnp.int32, (size, size), 1) % group
    same = row_pos == col_pos

    def temporal(half, carry):
        for shift in range(1, blocks):
            fwd_copy(half, shift).wait_recv()
        normed = fwd_in[half].reshape(frames * rows, width)

        def grouped(weight_ref):
            full = jnp.dot(normed, weight_ref[...], preferred_element_type=jnp.float32)
            full = full.reshape(frames, rows // group, group, width)
            return [full[:, g].reshape(size, width).astype(bf16) for g in range(rows // group)]

        q2, k2, v2 = grouped(tmq_ref), grouped(tmk_ref), grouped(tmv_ref)
        done = []
        for g in range(rows // group):
            attn = attend_heads(
                q2[g],
                [lambda a, b: k2[g][:, a:b]],
                [lambda a, b: v2[g][:, a:b]],
                width,
                same,
            )
            done.append(attn.reshape(frames, 1, group, width))
        attn = jnp.concatenate(done, axis=1).reshape(blocks, frames_here, rows, width)
        bwd_out[half] = attn.astype(bf16)
        for shift in range(1, blocks):
            bwd_copy(half, shift).start()
        bwd_in[half, me] = bwd_out[half, me]
        return carry

    lax.fori_loop(0, halves, temporal, 0)

    def finish(half, carry):
        for shift in range(1, blocks):
            bwd_copy(half, shift).wait_recv()
        for f in range(frames_here):
            attn = bwd_in[half, :, f].reshape(count, width)
            mixed = mid_buf[half, f] + jnp.dot(
                attn, tmo_ref[...], preferred_element_type=jnp.float32
            )
            out_ref[f, :, half] = mixed.astype(bf16).reshape(blocks, rows, width)
        return carry

    lax.fori_loop(0, halves, finish, 0)

    for shift in range(1, blocks):
        ref_copy(shift).wait_send()
        for half in range(halves):
            fwd_copy(half, shift).wait_send()
            bwd_copy(half, shift).wait_send()


def on_device_fused(
    hidden,
    ref_feats,
    frame_index,
    step_index,
    temb_table,
    norm_gain_1,
    norm_gain_2,
    *weights,
):
    frames_here, positions, width = hidden.shape
    blocks = lax.axis_size("frame")
    share = positions // blocks
    halves = 2
    rows = share // halves
    count = blocks * rows
    ref_rows = ref_feats.shape[0]
    bf16 = jnp.bfloat16
    dma = pltpu.SemaphoreType.DMA
    smem = pl.BlockSpec(memory_space=pltpu.SMEM)
    vmem = pl.BlockSpec(memory_space=pltpu.VMEM)
    moved = (halves, blocks, frames_here, rows, width)
    out = pl.pallas_call(
        functools.partial(fused_kernel, blocks),
        out_shape=jax.ShapeDtypeStruct((frames_here, blocks, halves, rows, width), bf16),
        in_specs=[smem, smem] + [vmem] * 13,
        out_specs=vmem,
        scratch_shapes=[
            pltpu.VMEM((blocks, ref_rows, width), bf16),
            pltpu.VMEM((halves, frames_here, count, width), bf16),
            pltpu.VMEM((frames_here, positions, width), bf16),
            pltpu.VMEM((frames_here, positions, width), bf16),
            pltpu.VMEM((blocks * ref_rows, width), bf16),
            pltpu.VMEM((blocks * ref_rows, width), bf16),
            pltpu.VMEM((halves, frames_here, count, width), jnp.float32),
            pltpu.VMEM((frames_here, 1, width), jnp.float32),
            pltpu.VMEM(moved, bf16),
            pltpu.VMEM(moved, bf16),
            pltpu.VMEM(moved, bf16),
            pltpu.VMEM(moved, bf16),
            dma((blocks - 1,)),
            dma((blocks - 1,)),
            dma((halves, blocks - 1)),
            dma((halves, blocks - 1)),
            dma((halves, blocks - 1)),
            dma((halves, blocks - 1)),
        ],
        compiler_params=pltpu.CompilerParams(
            collective_id=0, has_side_effects=True, vmem_limit_bytes=32 * 1024 * 1024
        ),
    )(
        step_index,
        frame_index,
        hidden.reshape(frames_here, blocks, halves, rows, width),
        ref_feats,
        temb_table.reshape(-1, 8, width),
        norm_gain_1.reshape(1, width),
        norm_gain_2.reshape(1, width),
        *weights,
    )
    return out.reshape(frames_here, positions, width)


def on_device(hidden, ref_feats, frame_index, step_index, temb_table, *rest):
    blocks = lax.axis_size("frame")
    frames_here, positions, width = hidden.shape
    fits = (
        positions % (32 * blocks) == 0
        and blocks * ref_feats.shape[0] == positions
        and ref_feats.shape[0] % 16 == 0
        and temb_table.shape[0] % 8 == 0
        and frames_here * blocks * 8 <= 128
    )
    body = on_device_fused if fits else on_device_plain
    return body(hidden, ref_feats, frame_index, step_index, temb_table, *rest)


def solution(mesh):
    in_specs = (
        P(("video", "frame"), None, None),
        P(("video", "frame"), None),
        P(("video", "frame")),
        P(),
        P(),
        P(),
        P(),
        P(),
        P(),
        P(),
        P(),
        P(),
        P(),
        P(),
        P(),
    )
    out_specs = P(("video", "frame"), None, None)
    return jax.shard_map(
        on_device, mesh=mesh, in_specs=in_specs, out_specs=out_specs, check_vma=False
    )
```

```python
import functools
import math

import jax
import jax.numpy as jnp
from jax import lax
from jax.experimental import pallas as pl
from jax.experimental.pallas import tpu as pltpu
from jax.sharding import PartitionSpec as P

HEADS = 8


def layer_norm(values, gain):
    mean = jnp.mean(values, axis=-1, keepdims=True)
    centered = values - mean
    var = jnp.mean(centered * centered, axis=-1, keepdims=True)
    return centered * lax.rsqrt(var + 1e-05) * gain


def positional(frame_index, width):
    chan = jnp.arange(width)
    freq = jnp.exp(-(chan // 2 * 2).astype(jnp.float32) / width * math.log(10000.0))
    phase = (chan % 2).astype(jnp.float32) * (math.pi / 2)
    return jnp.sin(frame_index.astype(jnp.float32)[:, None] * freq[None, :] + phase[None, :])


def project(rows, weight):
    return jnp.dot(rows, weight, preferred_element_type=jnp.float32).astype(jnp.bfloat16)


def temporal_attend(query, keys, values):
    frames, count, width = query.shape
    head_dim = width // HEADS
    q = query.reshape(frames, count, HEADS, head_dim)
    k = keys.reshape(frames, count, HEADS, head_dim)
    v = values.reshape(frames, count, HEADS, head_dim)
    scores = jnp.einsum("fnhd,gnhd->nhfg", q, k, preferred_element_type=jnp.float32) / math.sqrt(
        head_dim
    )
    probs = jax.nn.softmax(scores, axis=-1).astype(jnp.bfloat16)
    out = jnp.einsum("nhfg,gnhd->fnhd", probs, v, preferred_element_type=jnp.float32)
    return out.astype(jnp.bfloat16).reshape(frames, count, width)


def flatten_block(block):
    return block.reshape(block.shape[0], block.shape[2], block.shape[3])


def on_device_plain(
    hidden,
    ref_feats,
    frame_index,
    step_index,
    temb_table,
    norm_gain_1,
    norm_gain_2,
    sp_query,
    sp_key,
    sp_value,
    sp_out,
    tm_query,
    tm_key,
    tm_value,
    tm_out,
):
    frames_here, positions, width = hidden.shape
    head_dim = width // HEADS
    blocks = lax.axis_size("frame")
    share = positions // blocks
    temb = lax.dynamic_slice_in_dim(temb_table, step_index[0], 1, 0).astype(jnp.float32)
    base = hidden.astype(jnp.float32) + temb[None, :, :]
    normed_1 = layer_norm(base, norm_gain_1).astype(jnp.bfloat16)
    ref_local = layer_norm(ref_feats.astype(jnp.float32), norm_gain_1).astype(jnp.bfloat16)
    ref_all = lax.all_gather(ref_local, "frame", axis=0, tiled=True)
    ref_k = project(ref_all, sp_key)
    ref_v = project(ref_all, sp_value)
    q1 = project(normed_1, sp_query).reshape(frames_here, positions, HEADS, head_dim)
    k1 = project(normed_1, sp_key).reshape(frames_here, positions, HEADS, head_dim)
    v1 = project(normed_1, sp_value).reshape(frames_here, positions, HEADS, head_dim)
    ref_kh = ref_k.reshape(positions, HEADS, head_dim)
    ref_vh = ref_v.reshape(positions, HEADS, head_dim)
    scale = 1.0 / math.sqrt(head_dim)
    self_scores = jnp.einsum("fqhd,fkhd->fhqk", q1, k1, preferred_element_type=jnp.float32) * scale
    ref_scores = (
        jnp.einsum("fqhd,khd->fhqk", q1, ref_kh, preferred_element_type=jnp.float32) * scale
    )
    top = jnp.maximum(
        jnp.max(self_scores, axis=-1, keepdims=True), jnp.max(ref_scores, axis=-1, keepdims=True)
    )
    self_exp = jnp.exp(self_scores - top)
    ref_exp = jnp.exp(ref_scores - top)
    total = jnp.sum(self_exp, axis=-1, keepdims=True) + jnp.sum(ref_exp, axis=-1, keepdims=True)
    self_probs = (self_exp / total).astype(jnp.bfloat16)
    ref_probs = (ref_exp / total).astype(jnp.bfloat16)
    attn_1 = jnp.einsum("fhqk,fkhd->fqhd", self_probs, v1, preferred_element_type=jnp.float32)
    attn_1 = attn_1 + jnp.einsum(
        "fhqk,khd->fqhd", ref_probs, ref_vh, preferred_element_type=jnp.float32
    )
    attn_1 = attn_1.astype(jnp.bfloat16).reshape(frames_here, positions, width)
    mid = base + jnp.dot(attn_1, sp_out, preferred_element_type=jnp.float32)
    encoding = positional(frame_index, width)
    normed_2 = (layer_norm(mid, norm_gain_2) + encoding[:, None, :]).astype(jnp.bfloat16)
    moved = (
        project(normed_2, tm_query).reshape(frames_here, blocks, share, width),
        project(normed_2, tm_key).reshape(frames_here, blocks, share, width),
        project(normed_2, tm_value).reshape(frames_here, blocks, share, width),
    )
    result = temporal_attend(
        flatten_block(lax.all_to_all(moved[0], "frame", split_axis=1, concat_axis=0, tiled=True)),
        flatten_block(lax.all_to_all(moved[1], "frame", split_axis=1, concat_axis=0, tiled=True)),
        flatten_block(lax.all_to_all(moved[2], "frame", split_axis=1, concat_axis=0, tiled=True)),
    )
    attn_2 = result.reshape(result.shape[0], 1, result.shape[1], result.shape[2])
    returned = lax.all_to_all(attn_2, "frame", split_axis=0, concat_axis=1, tiled=True).reshape(
        frames_here, positions, width
    )
    return (mid + jnp.dot(returned, tm_out, preferred_element_type=jnp.float32)).astype(
        jnp.bfloat16
    )


def layer_norm_down(values, gain):
    mean = jnp.mean(values, axis=0, keepdims=True)
    centered = values - mean
    var = jnp.mean(centered * centered, axis=0, keepdims=True)
    return centered * lax.rsqrt(var + 1e-05) * gain


def project_down(weight, rows, contract):
    return lax.dot_general(
        weight, rows, (((0,), (contract,)), ((), ())), preferred_element_type=jnp.float32
    )


def head_span(head, head_dim, width):
    low = head * head_dim
    high = low + head_dim
    return low, high, low // 128 * 128, min(width, -(-high // 128) * 128)


def lane_mask(low, high, first, last):
    lane = lax.broadcasted_iota(jnp.int32, (1, last - first), 1) + first
    return jnp.where((lane >= low) & (lane < high), 1.0, 0.0).astype(jnp.bfloat16)


def attend_heads(q, key_parts, value_parts, width, allowed=None):
    head_dim = width // HEADS
    factor = math.log2(math.e) / math.sqrt(head_dim)
    columns = [None] * (-(-width // 128))
    for head in range(HEADS):
        low, high, first, last = head_span(head, head_dim, width)
        picked = q[:, first:last] * lane_mask(low, high, first, last)
        scores = [
            lax.dot_general(
                picked,
                keys(first, last),
                (((1,), (1,)), ((), ())),
                preferred_element_type=jnp.float32,
            )
            for keys in key_parts
        ]
        if allowed is not None:
            scores = [jnp.where(allowed, s, -1e30) for s in scores]
        top = functools.reduce(jnp.maximum, [jnp.max(s, axis=-1, keepdims=True) for s in scores])
        exps = [jnp.exp2((s - top) * factor) for s in scores]
        total = sum(jnp.sum(e, axis=-1, keepdims=True) for e in exps)
        inverse = 1.0 / total
        result = None
        for e, values in zip(exps, value_parts):
            probs = (e * inverse).astype(jnp.bfloat16)
            part = jnp.dot(probs, values(first, last), preferred_element_type=jnp.float32)
            result = part if result is None else result + part
        for block in range(first // 128, -(-last // 128)):
            start, end = block * 128, min(width, block * 128 + 128)
            piece = result[:, start - first : end - first]
            if columns[block] is not None:
                lane = lax.broadcasted_iota(jnp.int32, (1, end - start), 1) + start
                piece = jnp.where(lane >= low, piece, columns[block])
            columns[block] = piece
    return jnp.concatenate(columns, axis=-1)


def fused_kernel(
    blocks,
    step_ref,
    frame_ref,
    hidden_ref,
    ref_ref,
    temb_ref,
    gain1_ref,
    gain2_ref,
    spq_ref,
    spk_ref,
    spv_ref,
    spo_ref,
    tmq_ref,
    tmk_ref,
    tmv_ref,
    tmo_ref,
    out_ref,
    ref_buf,
    q_buf,
    k_buf,
    v_buf,
    mid_buf,
    pe_buf,
    gain2_buf,
    fwd_out,
    fwd_in,
    bwd_out,
    bwd_in,
    ref_send,
    ref_recv,
    fwd_send,
    fwd_recv,
    bwd_send,
    bwd_recv,
):
    me = lax.axis_index("frame")
    frames_here, width, positions = hidden_ref.shape
    halves, rows = fwd_out.shape[0], fwd_out.shape[3]
    count = blocks * rows
    frames = frames_here * blocks
    head_dim = width // HEADS
    bf16 = jnp.bfloat16

    def peer(shift):
        return lax.rem(me + shift, blocks)

    barrier = pltpu.get_barrier_semaphore()
    for shift in range(1, blocks):
        pl.semaphore_signal(
            barrier, inc=1, device_id={"frame": peer(shift)}, device_id_type=pl.DeviceIdType.MESH
        )

    gain1 = gain1_ref[...].reshape(1, width)
    ref_buf[me] = layer_norm(ref_ref[...].astype(jnp.float32), gain1).astype(bf16)
    pl.semaphore_wait(barrier, blocks - 1)

    def ref_copy(shift):
        return pltpu.make_async_remote_copy(
            src_ref=ref_buf.at[me],
            dst_ref=ref_buf.at[me],
            send_sem=ref_send.at[shift - 1],
            recv_sem=ref_recv.at[shift - 1],
            device_id={"frame": peer(shift)},
            device_id_type=pl.DeviceIdType.MESH,
        )

    def fwd_copy(half, shift):
        return pltpu.make_async_remote_copy(
            src_ref=fwd_out.at[half, peer(shift)],
            dst_ref=fwd_in.at[half, me],
            send_sem=fwd_send.at[half, shift - 1],
            recv_sem=fwd_recv.at[half, shift - 1],
            device_id={"frame": peer(shift)},
            device_id_type=pl.DeviceIdType.MESH,
        )

    def bwd_copy(half, shift):
        return pltpu.make_async_remote_copy(
            src_ref=bwd_out.at[half, peer(shift)],
            dst_ref=bwd_in.at[half, me],
            send_sem=bwd_send.at[half, shift - 1],
            recv_sem=bwd_recv.at[half, shift - 1],
            device_id={"frame": peer(shift)},
            device_id_type=pl.DeviceIdType.MESH,
        )

    for shift in range(1, blocks):
        ref_copy(shift).start()

    def column(row):
        return jnp.broadcast_to(row, (count, width)).T

    steps = temb_ref.shape[1]
    chosen = lax.broadcasted_iota(jnp.int32, (steps, count), 0) == step_ref[0]
    temb = jnp.dot(
        temb_ref[...],
        jnp.where(chosen, 1.0, 0.0).astype(bf16),
        preferred_element_type=jnp.float32,
    )

    chan = lax.broadcasted_iota(jnp.int32, (1, width), 1)
    freq = jnp.exp(-(chan // 2 * 2).astype(jnp.float32) / width * math.log(10000.0))
    phase = (chan % 2).astype(jnp.float32) * (math.pi / 2)
    for f in range(frames_here):
        pe_buf[f] = column(jnp.sin(frame_ref[f].astype(jnp.float32) * freq + phase))

    gain1 = column(gain1)
    for f in range(frames_here):
        normed = []
        for half in range(halves):
            base = hidden_ref[f, :, half * count : (half + 1) * count].astype(jnp.float32) + temb
            mid_buf[half, f] = base
            normed.append(layer_norm_down(base, gain1).astype(bf16))
        normed = jnp.concatenate(normed, axis=1)
        query = project_down(spq_ref[...], normed, 0)
        for half in range(halves):
            for head in range(HEADS):
                low, high, first, last = head_span(head, head_dim, width)
                piece = query[first:last, half * count : (half + 1) * count]
                row = lax.broadcasted_iota(jnp.int32, piece.shape, 0) + first
                piece = jnp.where((row >= low) & (row < high), piece, 0.0)
                q_buf[half, f, head, : last - first] = piece.astype(bf16)
        k_buf[f, :positions] = project(normed.T, spk_ref[...])
        value = project_down(spv_ref[...], normed, 0)
        v_buf[f, :, :, :positions] = value.reshape(HEADS, head_dim, positions).astype(bf16)

    for shift in range(1, blocks):
        ref_copy(shift).wait_recv()
    ref_all = ref_buf[...].reshape(-1, width)
    ref_key = project(ref_all, spk_ref[...])
    ref_value = project_down(spv_ref[...], ref_all, 1)
    ref_value = ref_value.reshape(HEADS, head_dim, positions).astype(bf16)
    for f in range(frames_here):
        k_buf[f, positions:] = ref_key
        v_buf[f, :, :, positions:] = ref_value

    gain2_buf[...] = column(gain2_ref[...].reshape(1, width))
    factor = math.log2(math.e) / math.sqrt(head_dim)

    def spatial(half, carry):
        for f in range(frames_here):
            done = []
            for head in range(HEADS):
                low, high, first, last = head_span(head, head_dim, width)
                scores = jnp.dot(
                    k_buf[f, :, first:last],
                    q_buf[half, f, head, : last - first],
                    preferred_element_type=jnp.float32,
                )
                top = jnp.max(scores, axis=0, keepdims=True)
                exps = jnp.exp2((scores - top) * factor)
                inverse = 1.0 / jnp.sum(exps, axis=0, keepdims=True)
                probs = (exps * inverse).astype(bf16)
                done.append(jnp.dot(v_buf[f, head], probs, preferred_element_type=jnp.float32))
            attn = jnp.concatenate(done, axis=0).astype(bf16)
            mid = mid_buf[half, f] + project_down(spo_ref[...], attn, 0)
            mid_buf[half, f] = mid
            normed = layer_norm_down(mid, gain2_buf[...]) + pe_buf[f]
            fwd_out[half, :, f] = normed.T.astype(bf16).reshape(blocks, rows, width)
        for shift in range(1, blocks):
            fwd_copy(half, shift).start()
        fwd_in[half, me] = fwd_out[half, me]
        return carry

    lax.fori_loop(0, halves, spatial, 0)

    group = 8
    size = frames * group
    row_pos = lax.broadcasted_iota(jnp.int32, (size, size), 0) % group
    col_pos = lax.broadcasted_iota(jnp.int32, (size, size), 1) % group
    same = row_pos == col_pos

    def temporal(half, carry):
        for shift in range(1, blocks):
            fwd_copy(half, shift).wait_recv()
        normed = fwd_in[half].reshape(frames * rows, width)

        def grouped(weight_ref):
            full = jnp.dot(normed, weight_ref[...], preferred_element_type=jnp.float32)
            full = full.reshape(frames, rows // group, group, width)
            return [full[:, g].reshape(size, width).astype(bf16) for g in range(rows // group)]

        q2, k2, v2 = grouped(tmq_ref), grouped(tmk_ref), grouped(tmv_ref)
        done = []
        for g in range(rows // group):
            attn = attend_heads(
                q2[g],
                [lambda a, b: k2[g][:, a:b]],
                [lambda a, b: v2[g][:, a:b]],
                width,
                same,
            )
            done.append(attn.reshape(frames, 1, group, width))
        attn = jnp.concatenate(done, axis=1).reshape(blocks, frames_here, rows, width)
        bwd_out[half] = attn.astype(bf16)
        for shift in range(1, blocks):
            bwd_copy(half, shift).start()
        bwd_in[half, me] = bwd_out[half, me]
        return carry

    lax.fori_loop(0, halves, temporal, 0)

    for half in range(halves):
        for shift in range(1, blocks):
            bwd_copy(half, shift).wait_recv()
        for f in range(frames_here):
            attn = bwd_in[half, :, f].reshape(count, width)
            mixed = mid_buf[half, f] + project_down(tmo_ref[...], attn, 1)
            out_ref[f, :, half * count : (half + 1) * count] = mixed.astype(bf16)

    for shift in range(1, blocks):
        ref_copy(shift).wait_send()
        for half in range(halves):
            fwd_copy(half, shift).wait_send()
            bwd_copy(half, shift).wait_send()


def on_device_fused(
    hidden,
    ref_feats,
    frame_index,
    step_index,
    temb_table,
    norm_gain_1,
    norm_gain_2,
    *weights,
):
    frames_here, positions, width = hidden.shape
    blocks = lax.axis_size("frame")
    share = positions // blocks
    halves = 2
    rows = share // halves
    count = blocks * rows
    ref_rows = ref_feats.shape[0]
    bf16 = jnp.bfloat16
    dma = pltpu.SemaphoreType.DMA
    smem = pl.BlockSpec(memory_space=pltpu.SMEM)
    vmem = pl.BlockSpec(memory_space=pltpu.VMEM)
    moved = (halves, blocks, frames_here, rows, width)
    out = pl.pallas_call(
        functools.partial(fused_kernel, blocks),
        out_shape=jax.ShapeDtypeStruct((frames_here, width, positions), bf16),
        in_specs=[smem, smem] + [vmem] * 13,
        out_specs=vmem,
        scratch_shapes=[
            pltpu.VMEM((blocks, ref_rows, width), bf16),
            pltpu.VMEM((halves, frames_here, HEADS, 256, count), bf16),
            pltpu.VMEM((frames_here, 2 * positions, width), bf16),
            pltpu.VMEM((frames_here, HEADS, width // HEADS, 2 * positions), bf16),
            pltpu.VMEM((halves, frames_here, width, count), jnp.float32),
            pltpu.VMEM((frames_here, width, count), jnp.float32),
            pltpu.VMEM((width, count), jnp.float32),
            pltpu.VMEM(moved, bf16),
            pltpu.VMEM(moved, bf16),
            pltpu.VMEM(moved, bf16),
            pltpu.VMEM(moved, bf16),
            dma((blocks - 1,)),
            dma((blocks - 1,)),
            dma((halves, blocks - 1)),
            dma((halves, blocks - 1)),
            dma((halves, blocks - 1)),
            dma((halves, blocks - 1)),
        ],
        compiler_params=pltpu.CompilerParams(
            collective_id=0, has_side_effects=True, vmem_limit_bytes=32 * 1024 * 1024
        ),
    )(
        step_index,
        frame_index,
        hidden.transpose(0, 2, 1),
        ref_feats,
        temb_table.T,
        norm_gain_1,
        norm_gain_2,
        *weights,
    )
    return out.transpose(0, 2, 1)


def on_device(hidden, ref_feats, frame_index, step_index, temb_table, *rest):
    blocks = lax.axis_size("frame")
    frames_here, positions, width = hidden.shape
    fits = (
        positions == 256 and positions % (32 * blocks) == 0
        and blocks * ref_feats.shape[0] == positions
        and ref_feats.shape[0] % 16 == 0
        and frames_here * blocks * 8 <= 128
    )
    body = on_device_fused if fits else on_device_plain
    return body(hidden, ref_feats, frame_index, step_index, temb_table, *rest)


def solution(mesh):
    in_specs = (
        P(("video", "frame"), None, None),
        P(("video", "frame"), None),
        P(("video", "frame")),
        P(),
        P(),
        P(),
        P(),
        P(),
        P(),
        P(),
        P(),
        P(),
        P(),
        P(),
        P(),
    )
    out_specs = P(("video", "frame"), None, None)
    return jax.shard_map(
        on_device, mesh=mesh, in_specs=in_specs, out_specs=out_specs, check_vma=False
    )
```

```python
import functools
import math

import jax
import jax.numpy as jnp
from jax import lax
from jax.experimental import pallas as pl
from jax.experimental.pallas import tpu as pltpu
from jax.sharding import PartitionSpec as P

HEADS = 8


def layer_norm(values, gain):
    mean = jnp.mean(values, axis=-1, keepdims=True)
    centered = values - mean
    var = jnp.mean(centered * centered, axis=-1, keepdims=True)
    return centered * lax.rsqrt(var + 1e-05) * gain


def positional(frame_index, width):
    chan = jnp.arange(width)
    freq = jnp.exp(-(chan // 2 * 2).astype(jnp.float32) / width * math.log(10000.0))
    phase = (chan % 2).astype(jnp.float32) * (math.pi / 2)
    return jnp.sin(frame_index.astype(jnp.float32)[:, None] * freq[None, :] + phase[None, :])


def project(rows, weight):
    return jnp.dot(rows, weight, preferred_element_type=jnp.float32).astype(jnp.bfloat16)


def temporal_attend(query, keys, values):
    frames, count, width = query.shape
    head_dim = width // HEADS
    q = query.reshape(frames, count, HEADS, head_dim)
    k = keys.reshape(frames, count, HEADS, head_dim)
    v = values.reshape(frames, count, HEADS, head_dim)
    scores = jnp.einsum("fnhd,gnhd->nhfg", q, k, preferred_element_type=jnp.float32) / math.sqrt(
        head_dim
    )
    probs = jax.nn.softmax(scores, axis=-1).astype(jnp.bfloat16)
    out = jnp.einsum("nhfg,gnhd->fnhd", probs, v, preferred_element_type=jnp.float32)
    return out.astype(jnp.bfloat16).reshape(frames, count, width)


def flatten_block(block):
    return block.reshape(block.shape[0], block.shape[2], block.shape[3])


def on_device_plain(
    hidden,
    ref_feats,
    frame_index,
    step_index,
    temb_table,
    norm_gain_1,
    norm_gain_2,
    sp_query,
    sp_key,
    sp_value,
    sp_out,
    tm_query,
    tm_key,
    tm_value,
    tm_out,
):
    frames_here, positions, width = hidden.shape
    head_dim = width // HEADS
    blocks = lax.axis_size("frame")
    share = positions // blocks
    temb = lax.dynamic_slice_in_dim(temb_table, step_index[0], 1, 0).astype(jnp.float32)
    base = hidden.astype(jnp.float32) + temb[None, :, :]
    normed_1 = layer_norm(base, norm_gain_1).astype(jnp.bfloat16)
    ref_local = layer_norm(ref_feats.astype(jnp.float32), norm_gain_1).astype(jnp.bfloat16)
    ref_all = lax.all_gather(ref_local, "frame", axis=0, tiled=True)
    ref_k = project(ref_all, sp_key)
    ref_v = project(ref_all, sp_value)
    q1 = project(normed_1, sp_query).reshape(frames_here, positions, HEADS, head_dim)
    k1 = project(normed_1, sp_key).reshape(frames_here, positions, HEADS, head_dim)
    v1 = project(normed_1, sp_value).reshape(frames_here, positions, HEADS, head_dim)
    ref_kh = ref_k.reshape(positions, HEADS, head_dim)
    ref_vh = ref_v.reshape(positions, HEADS, head_dim)
    scale = 1.0 / math.sqrt(head_dim)
    self_scores = jnp.einsum("fqhd,fkhd->fhqk", q1, k1, preferred_element_type=jnp.float32) * scale
    ref_scores = (
        jnp.einsum("fqhd,khd->fhqk", q1, ref_kh, preferred_element_type=jnp.float32) * scale
    )
    top = jnp.maximum(
        jnp.max(self_scores, axis=-1, keepdims=True), jnp.max(ref_scores, axis=-1, keepdims=True)
    )
    self_exp = jnp.exp(self_scores - top)
    ref_exp = jnp.exp(ref_scores - top)
    total = jnp.sum(self_exp, axis=-1, keepdims=True) + jnp.sum(ref_exp, axis=-1, keepdims=True)
    self_probs = (self_exp / total).astype(jnp.bfloat16)
    ref_probs = (ref_exp / total).astype(jnp.bfloat16)
    attn_1 = jnp.einsum("fhqk,fkhd->fqhd", self_probs, v1, preferred_element_type=jnp.float32)
    attn_1 = attn_1 + jnp.einsum(
        "fhqk,khd->fqhd", ref_probs, ref_vh, preferred_element_type=jnp.float32
    )
    attn_1 = attn_1.astype(jnp.bfloat16).reshape(frames_here, positions, width)
    mid = base + jnp.dot(attn_1, sp_out, preferred_element_type=jnp.float32)
    encoding = positional(frame_index, width)
    normed_2 = (layer_norm(mid, norm_gain_2) + encoding[:, None, :]).astype(jnp.bfloat16)
    moved = (
        project(normed_2, tm_query).reshape(frames_here, blocks, share, width),
        project(normed_2, tm_key).reshape(frames_here, blocks, share, width),
        project(normed_2, tm_value).reshape(frames_here, blocks, share, width),
    )
    result = temporal_attend(
        flatten_block(lax.all_to_all(moved[0], "frame", split_axis=1, concat_axis=0, tiled=True)),
        flatten_block(lax.all_to_all(moved[1], "frame", split_axis=1, concat_axis=0, tiled=True)),
        flatten_block(lax.all_to_all(moved[2], "frame", split_axis=1, concat_axis=0, tiled=True)),
    )
    attn_2 = result.reshape(result.shape[0], 1, result.shape[1], result.shape[2])
    returned = lax.all_to_all(attn_2, "frame", split_axis=0, concat_axis=1, tiled=True).reshape(
        frames_here, positions, width
    )
    return (mid + jnp.dot(returned, tm_out, preferred_element_type=jnp.float32)).astype(
        jnp.bfloat16
    )


def layer_norm_down(values, gain):
    mean = jnp.mean(values, axis=0, keepdims=True)
    centered = values - mean
    var = jnp.mean(centered * centered, axis=0, keepdims=True)
    return centered * lax.rsqrt(var + 1e-05) * gain


def project_down(weight, rows, contract):
    return lax.dot_general(
        weight, rows, (((0,), (contract,)), ((), ())), preferred_element_type=jnp.float32
    )


def head_span(head, head_dim, width):
    low = head * head_dim
    high = low + head_dim
    return low, high, low // 128 * 128, min(width, -(-high // 128) * 128)


def lane_mask(low, high, first, last):
    lane = lax.broadcasted_iota(jnp.int32, (1, last - first), 1) + first
    return jnp.where((lane >= low) & (lane < high), 1.0, 0.0).astype(jnp.bfloat16)


def attend_heads(q, key_parts, value_parts, width, allowed=None):
    head_dim = width // HEADS
    factor = math.log2(math.e) / math.sqrt(head_dim)
    columns = [None] * (-(-width // 128))
    for head in range(HEADS):
        low, high, first, last = head_span(head, head_dim, width)
        picked = q[:, first:last] * lane_mask(low, high, first, last)
        scores = [
            lax.dot_general(
                picked,
                keys(first, last),
                (((1,), (1,)), ((), ())),
                preferred_element_type=jnp.float32,
            )
            for keys in key_parts
        ]
        if allowed is not None:
            scores = [jnp.where(allowed, s, -1e30) for s in scores]
        top = functools.reduce(jnp.maximum, [jnp.max(s, axis=-1, keepdims=True) for s in scores])
        exps = [jnp.exp2((s - top) * factor) for s in scores]
        total = sum(jnp.sum(e, axis=-1, keepdims=True) for e in exps)
        inverse = 1.0 / total
        result = None
        for e, values in zip(exps, value_parts):
            probs = (e * inverse).astype(jnp.bfloat16)
            part = jnp.dot(probs, values(first, last), preferred_element_type=jnp.float32)
            result = part if result is None else result + part
        for block in range(first // 128, -(-last // 128)):
            start, end = block * 128, min(width, block * 128 + 128)
            piece = result[:, start - first : end - first]
            if columns[block] is not None:
                lane = lax.broadcasted_iota(jnp.int32, (1, end - start), 1) + start
                piece = jnp.where(lane >= low, piece, columns[block])
            columns[block] = piece
    return jnp.concatenate(columns, axis=-1)


def fused_kernel(
    blocks,
    step_hbm,
    frame_hbm,
    hidden_hbm,
    ref_hbm,
    temb_hbm,
    gain1_hbm,
    gain2_hbm,
    spq_hbm,
    spk_hbm,
    spv_hbm,
    spo_hbm,
    tmq_hbm,
    tmk_hbm,
    tmv_hbm,
    tmo_hbm,
    out_ref,
    step_ref,
    frame_ref,
    hidden_ref,
    ref_ref,
    temb_ref,
    gain1_ref,
    gain2_ref,
    spq_ref,
    spk_ref,
    spv_ref,
    spo_ref,
    tmq_ref,
    tmk_ref,
    tmv_ref,
    tmo_ref,
    load_sem,
    ref_buf,
    q_buf,
    k_buf,
    v_buf,
    mid_buf,
    pe_buf,
    gain2_buf,
    fwd_out,
    fwd_in,
    bwd_out,
    bwd_in,
    ref_send,
    ref_recv,
    fwd_send,
    fwd_recv,
    bwd_send,
    bwd_recv,
):
    me = lax.axis_index("frame")
    frames_here, width, positions = hidden_ref.shape
    halves, rows = fwd_out.shape[0], fwd_out.shape[3]
    count = blocks * rows
    frames = frames_here * blocks
    head_dim = width // HEADS
    bf16 = jnp.bfloat16

    def peer(shift):
        return lax.rem(me + shift, blocks)

    loads = [
        pltpu.make_async_copy(source, target, load_sem.at[place])
        for place, (source, target) in enumerate(
            (
                (ref_hbm, ref_ref),
                (gain1_hbm, gain1_ref),
                (step_hbm, step_ref),
                (frame_hbm, frame_ref),
                (temb_hbm, temb_ref),
                (hidden_hbm, hidden_ref),
                (spq_hbm, spq_ref),
                (spk_hbm, spk_ref),
                (spv_hbm, spv_ref),
                (gain2_hbm, gain2_ref),
                (spo_hbm, spo_ref),
                (tmq_hbm, tmq_ref),
                (tmk_hbm, tmk_ref),
                (tmv_hbm, tmv_ref),
                (tmo_hbm, tmo_ref),
            )
        )
    ]
    for load in loads:
        load.start()

    barrier = pltpu.get_barrier_semaphore()
    for shift in range(1, blocks):
        pl.semaphore_signal(
            barrier, inc=1, device_id={"frame": peer(shift)}, device_id_type=pl.DeviceIdType.MESH
        )

    for load in loads[:2]:
        load.wait()
    gain1 = gain1_ref[...].reshape(1, width)
    ref_buf[me] = layer_norm(ref_ref[...].astype(jnp.float32), gain1).astype(bf16)
    pl.semaphore_wait(barrier, blocks - 1)

    def ref_copy(shift):
        return pltpu.make_async_remote_copy(
            src_ref=ref_buf.at[me],
            dst_ref=ref_buf.at[me],
            send_sem=ref_send.at[shift - 1],
            recv_sem=ref_recv.at[shift - 1],
            device_id={"frame": peer(shift)},
            device_id_type=pl.DeviceIdType.MESH,
        )

    def fwd_copy(half, shift):
        return pltpu.make_async_remote_copy(
            src_ref=fwd_out.at[half, peer(shift)],
            dst_ref=fwd_in.at[half, me],
            send_sem=fwd_send.at[half, shift - 1],
            recv_sem=fwd_recv.at[half, shift - 1],
            device_id={"frame": peer(shift)},
            device_id_type=pl.DeviceIdType.MESH,
        )

    def bwd_copy(half, shift):
        return pltpu.make_async_remote_copy(
            src_ref=bwd_out.at[half, peer(shift)],
            dst_ref=bwd_in.at[half, me],
            send_sem=bwd_send.at[half, shift - 1],
            recv_sem=bwd_recv.at[half, shift - 1],
            device_id={"frame": peer(shift)},
            device_id_type=pl.DeviceIdType.MESH,
        )

    for shift in range(1, blocks):
        ref_copy(shift).start()

    def column(row):
        return jnp.broadcast_to(row, (count, width)).T

    for load in loads[2:]:
        load.wait()
    steps = temb_ref.shape[1]
    chosen = lax.broadcasted_iota(jnp.int32, (steps, count), 0) == step_ref[0]
    temb = jnp.dot(
        temb_ref[...],
        jnp.where(chosen, 1.0, 0.0).astype(bf16),
        preferred_element_type=jnp.float32,
    )

    chan = lax.broadcasted_iota(jnp.int32, (1, width), 1)
    freq = jnp.exp(-(chan // 2 * 2).astype(jnp.float32) / width * math.log(10000.0))
    phase = (chan % 2).astype(jnp.float32) * (math.pi / 2)
    for f in range(frames_here):
        pe_buf[f] = column(jnp.sin(frame_ref[f].astype(jnp.float32) * freq + phase))

    gain1 = column(gain1)
    for f in range(frames_here):
        normed = []
        for half in range(halves):
            base = hidden_ref[f, :, half * count : (half + 1) * count].astype(jnp.float32) + temb
            mid_buf[half, f] = base
            normed.append(layer_norm_down(base, gain1).astype(bf16))
        normed = jnp.concatenate(normed, axis=1)
        query = project_down(spq_ref[...], normed, 0)
        for half in range(halves):
            for head in range(HEADS):
                low, high, first, last = head_span(head, head_dim, width)
                piece = query[first:last, half * count : (half + 1) * count]
                row = lax.broadcasted_iota(jnp.int32, piece.shape, 0) + first
                piece = jnp.where((row >= low) & (row < high), piece, 0.0)
                q_buf[half, f, head, : last - first] = piece.astype(bf16)
        k_buf[f, :positions] = project(normed.T, spk_ref[...])
        value = project_down(spv_ref[...], normed, 0)
        v_buf[f, :, :, :positions] = value.reshape(HEADS, head_dim, positions).astype(bf16)

    for shift in range(1, blocks):
        ref_copy(shift).wait_recv()
    ref_all = ref_buf[...].reshape(-1, width)
    ref_key = project(ref_all, spk_ref[...])
    ref_value = project_down(spv_ref[...], ref_all, 1)
    ref_value = ref_value.reshape(HEADS, head_dim, positions).astype(bf16)
    for f in range(frames_here):
        k_buf[f, positions:] = ref_key
        v_buf[f, :, :, positions:] = ref_value

    gain2_buf[...] = column(gain2_ref[...].reshape(1, width))
    factor = math.log2(math.e) / math.sqrt(head_dim)

    def spatial(half, carry):
        def score(f, head):
            low, high, first, last = head_span(head, head_dim, width)
            return jnp.dot(
                k_buf[f, :, first:last],
                q_buf[half, f, head, : last - first],
                preferred_element_type=jnp.float32,
            )

        units = [(f, head) for f in range(frames_here) for head in range(HEADS)]
        ahead = score(*units[0])
        for f in range(frames_here):
            done = []
            for head in range(HEADS):
                scores = ahead
                if f * HEADS + head + 1 < len(units):
                    ahead = score(*units[f * HEADS + head + 1])
                top = jnp.max(scores, axis=0, keepdims=True)
                exps = jnp.exp2((scores - top) * factor)
                inverse = 1.0 / jnp.sum(exps, axis=0, keepdims=True)
                probs = (exps * inverse).astype(bf16)
                done.append(jnp.dot(v_buf[f, head], probs, preferred_element_type=jnp.float32))
            attn = jnp.concatenate(done, axis=0).astype(bf16)
            mid = mid_buf[half, f] + project_down(spo_ref[...], attn, 0)
            mid_buf[half, f] = mid
            normed = layer_norm_down(mid, gain2_buf[...]) + pe_buf[f]
            fwd_out[half, :, f] = normed.T.astype(bf16).reshape(blocks, rows, width)
        for shift in range(1, blocks):
            fwd_copy(half, shift).start()
        fwd_in[half, me] = fwd_out[half, me]
        return carry

    lax.fori_loop(0, halves, spatial, 0)

    group = 8
    size = frames * group
    row_pos = lax.broadcasted_iota(jnp.int32, (size, size), 0) % group
    col_pos = lax.broadcasted_iota(jnp.int32, (size, size), 1) % group
    same = row_pos == col_pos

    def temporal(half, carry):
        for shift in range(1, blocks):
            fwd_copy(half, shift).wait_recv()
        normed = fwd_in[half].reshape(frames * rows, width)

        def grouped(weight_ref):
            full = jnp.dot(normed, weight_ref[...], preferred_element_type=jnp.float32)
            full = full.reshape(frames, rows // group, group, width)
            return [full[:, g].reshape(size, width).astype(bf16) for g in range(rows // group)]

        q2, k2, v2 = grouped(tmq_ref), grouped(tmk_ref), grouped(tmv_ref)
        done = []
        for g in range(rows // group):
            attn = attend_heads(
                q2[g],
                [lambda a, b: k2[g][:, a:b]],
                [lambda a, b: v2[g][:, a:b]],
                width,
                same,
            )
            done.append(attn.reshape(frames, 1, group, width))
        attn = jnp.concatenate(done, axis=1).reshape(blocks, frames_here, rows, width)
        bwd_out[half] = attn.astype(bf16)
        for shift in range(1, blocks):
            bwd_copy(half, shift).start()
        bwd_in[half, me] = bwd_out[half, me]
        return carry

    lax.fori_loop(0, halves, temporal, 0)

    for half in range(halves):
        for shift in range(1, blocks):
            bwd_copy(half, shift).wait_recv()
        for f in range(frames_here):
            attn = bwd_in[half, :, f].reshape(count, width)
            mixed = mid_buf[half, f] + project_down(tmo_ref[...], attn, 1)
            out_ref[f, :, half * count : (half + 1) * count] = mixed.astype(bf16)

    for shift in range(1, blocks):
        ref_copy(shift).wait_send()
        for half in range(halves):
            fwd_copy(half, shift).wait_send()
            bwd_copy(half, shift).wait_send()


def on_device_fused(
    hidden,
    ref_feats,
    frame_index,
    step_index,
    temb_table,
    norm_gain_1,
    norm_gain_2,
    *weights,
):
    frames_here, positions, width = hidden.shape
    blocks = lax.axis_size("frame")
    share = positions // blocks
    halves = 2
    rows = share // halves
    count = blocks * rows
    ref_rows = ref_feats.shape[0]
    bf16 = jnp.bfloat16
    dma = pltpu.SemaphoreType.DMA
    args = (
        step_index,
        frame_index,
        hidden.transpose(0, 2, 1),
        ref_feats,
        temb_table.T,
        norm_gain_1,
        norm_gain_2,
        *weights,
    )
    moved = (halves, blocks, frames_here, rows, width)
    out = pl.pallas_call(
        functools.partial(fused_kernel, blocks),
        out_shape=jax.ShapeDtypeStruct((frames_here, width, positions), bf16),
        in_specs=[pl.BlockSpec(memory_space=pltpu.HBM)] * len(args),
        out_specs=pl.BlockSpec(memory_space=pltpu.VMEM),
        scratch_shapes=[pltpu.SMEM(a.shape, a.dtype) for a in args[:2]]
        + [pltpu.VMEM(a.shape, a.dtype) for a in args[2:]]
        + [
            dma((len(args),)),
            pltpu.VMEM((blocks, ref_rows, width), bf16),
            pltpu.VMEM((halves, frames_here, HEADS, 256, count), bf16),
            pltpu.VMEM((frames_here, 2 * positions, width), bf16),
            pltpu.VMEM((frames_here, HEADS, width // HEADS, 2 * positions), bf16),
            pltpu.VMEM((halves, frames_here, width, count), jnp.float32),
            pltpu.VMEM((frames_here, width, count), jnp.float32),
            pltpu.VMEM((width, count), jnp.float32),
            pltpu.VMEM(moved, bf16),
            pltpu.VMEM(moved, bf16),
            pltpu.VMEM(moved, bf16),
            pltpu.VMEM(moved, bf16),
            dma((blocks - 1,)),
            dma((blocks - 1,)),
            dma((halves, blocks - 1)),
            dma((halves, blocks - 1)),
            dma((halves, blocks - 1)),
            dma((halves, blocks - 1)),
        ],
        compiler_params=pltpu.CompilerParams(
            collective_id=0, has_side_effects=True, vmem_limit_bytes=60 * 1024 * 1024
        ),
    )(*args)
    return out.transpose(0, 2, 1)


def on_device(hidden, ref_feats, frame_index, step_index, temb_table, *rest):
    blocks = lax.axis_size("frame")
    frames_here, positions, width = hidden.shape
    fits = (
        positions == 256 and positions % (32 * blocks) == 0
        and blocks * ref_feats.shape[0] == positions
        and ref_feats.shape[0] % 16 == 0
        and frames_here * blocks * 8 <= 128
    )
    body = on_device_fused if fits else on_device_plain
    return body(hidden, ref_feats, frame_index, step_index, temb_table, *rest)


def solution(mesh):
    in_specs = (
        P(("video", "frame"), None, None),
        P(("video", "frame"), None),
        P(("video", "frame")),
        P(),
        P(),
        P(),
        P(),
        P(),
        P(),
        P(),
        P(),
        P(),
        P(),
        P(),
        P(),
    )
    out_specs = P(("video", "frame"), None, None)
    return jax.shard_map(
        on_device, mesh=mesh, in_specs=in_specs, out_specs=out_specs, check_vma=False
    )
```

```python
import functools
import math

import jax
import jax.numpy as jnp
from jax import lax
from jax.experimental import pallas as pl
from jax.experimental.pallas import tpu as pltpu
from jax.sharding import PartitionSpec as P

HEADS = 8


def layer_norm(values, gain):
    mean = jnp.mean(values, axis=-1, keepdims=True)
    centered = values - mean
    var = jnp.mean(centered * centered, axis=-1, keepdims=True)
    return centered * lax.rsqrt(var + 1e-05) * gain


def positional(frame_index, width):
    chan = jnp.arange(width)
    freq = jnp.exp(-(chan // 2 * 2).astype(jnp.float32) / width * math.log(10000.0))
    phase = (chan % 2).astype(jnp.float32) * (math.pi / 2)
    return jnp.sin(frame_index.astype(jnp.float32)[:, None] * freq[None, :] + phase[None, :])


def project(rows, weight):
    return jnp.dot(rows, weight, preferred_element_type=jnp.float32).astype(jnp.bfloat16)


def temporal_attend(query, keys, values):
    frames, count, width = query.shape
    head_dim = width // HEADS
    q = query.reshape(frames, count, HEADS, head_dim)
    k = keys.reshape(frames, count, HEADS, head_dim)
    v = values.reshape(frames, count, HEADS, head_dim)
    scores = jnp.einsum("fnhd,gnhd->nhfg", q, k, preferred_element_type=jnp.float32) / math.sqrt(
        head_dim
    )
    probs = jax.nn.softmax(scores, axis=-1).astype(jnp.bfloat16)
    out = jnp.einsum("nhfg,gnhd->fnhd", probs, v, preferred_element_type=jnp.float32)
    return out.astype(jnp.bfloat16).reshape(frames, count, width)


def flatten_block(block):
    return block.reshape(block.shape[0], block.shape[2], block.shape[3])


def on_device_plain(
    hidden,
    ref_feats,
    frame_index,
    step_index,
    temb_table,
    norm_gain_1,
    norm_gain_2,
    sp_query,
    sp_key,
    sp_value,
    sp_out,
    tm_query,
    tm_key,
    tm_value,
    tm_out,
):
    frames_here, positions, width = hidden.shape
    head_dim = width // HEADS
    blocks = lax.axis_size("frame")
    share = positions // blocks
    temb = lax.dynamic_slice_in_dim(temb_table, step_index[0], 1, 0).astype(jnp.float32)
    base = hidden.astype(jnp.float32) + temb[None, :, :]
    normed_1 = layer_norm(base, norm_gain_1).astype(jnp.bfloat16)
    ref_local = layer_norm(ref_feats.astype(jnp.float32), norm_gain_1).astype(jnp.bfloat16)
    ref_all = lax.all_gather(ref_local, "frame", axis=0, tiled=True)
    ref_k = project(ref_all, sp_key)
    ref_v = project(ref_all, sp_value)
    q1 = project(normed_1, sp_query).reshape(frames_here, positions, HEADS, head_dim)
    k1 = project(normed_1, sp_key).reshape(frames_here, positions, HEADS, head_dim)
    v1 = project(normed_1, sp_value).reshape(frames_here, positions, HEADS, head_dim)
    ref_kh = ref_k.reshape(positions, HEADS, head_dim)
    ref_vh = ref_v.reshape(positions, HEADS, head_dim)
    scale = 1.0 / math.sqrt(head_dim)
    self_scores = jnp.einsum("fqhd,fkhd->fhqk", q1, k1, preferred_element_type=jnp.float32) * scale
    ref_scores = (
        jnp.einsum("fqhd,khd->fhqk", q1, ref_kh, preferred_element_type=jnp.float32) * scale
    )
    top = jnp.maximum(
        jnp.max(self_scores, axis=-1, keepdims=True), jnp.max(ref_scores, axis=-1, keepdims=True)
    )
    self_exp = jnp.exp(self_scores - top)
    ref_exp = jnp.exp(ref_scores - top)
    total = jnp.sum(self_exp, axis=-1, keepdims=True) + jnp.sum(ref_exp, axis=-1, keepdims=True)
    self_probs = (self_exp / total).astype(jnp.bfloat16)
    ref_probs = (ref_exp / total).astype(jnp.bfloat16)
    attn_1 = jnp.einsum("fhqk,fkhd->fqhd", self_probs, v1, preferred_element_type=jnp.float32)
    attn_1 = attn_1 + jnp.einsum(
        "fhqk,khd->fqhd", ref_probs, ref_vh, preferred_element_type=jnp.float32
    )
    attn_1 = attn_1.astype(jnp.bfloat16).reshape(frames_here, positions, width)
    mid = base + jnp.dot(attn_1, sp_out, preferred_element_type=jnp.float32)
    encoding = positional(frame_index, width)
    normed_2 = (layer_norm(mid, norm_gain_2) + encoding[:, None, :]).astype(jnp.bfloat16)
    moved = (
        project(normed_2, tm_query).reshape(frames_here, blocks, share, width),
        project(normed_2, tm_key).reshape(frames_here, blocks, share, width),
        project(normed_2, tm_value).reshape(frames_here, blocks, share, width),
    )
    result = temporal_attend(
        flatten_block(lax.all_to_all(moved[0], "frame", split_axis=1, concat_axis=0, tiled=True)),
        flatten_block(lax.all_to_all(moved[1], "frame", split_axis=1, concat_axis=0, tiled=True)),
        flatten_block(lax.all_to_all(moved[2], "frame", split_axis=1, concat_axis=0, tiled=True)),
    )
    attn_2 = result.reshape(result.shape[0], 1, result.shape[1], result.shape[2])
    returned = lax.all_to_all(attn_2, "frame", split_axis=0, concat_axis=1, tiled=True).reshape(
        frames_here, positions, width
    )
    return (mid + jnp.dot(returned, tm_out, preferred_element_type=jnp.float32)).astype(
        jnp.bfloat16
    )


def layer_norm_down(values, gain):
    mean = jnp.mean(values, axis=0, keepdims=True)
    centered = values - mean
    var = jnp.mean(centered * centered, axis=0, keepdims=True)
    return centered * lax.rsqrt(var + 1e-05) * gain


def project_down(weight, rows, contract):
    return lax.dot_general(
        weight, rows, (((0,), (contract,)), ((), ())), preferred_element_type=jnp.float32
    )


def head_span(head, head_dim, width):
    low = head * head_dim
    high = low + head_dim
    return low, high, low // 128 * 128, min(width, -(-high // 128) * 128)


def lane_mask(low, high, first, last):
    lane = lax.broadcasted_iota(jnp.int32, (1, last - first), 1) + first
    return jnp.where((lane >= low) & (lane < high), 1.0, 0.0).astype(jnp.bfloat16)


def attend_heads(q, key_parts, value_parts, width, allowed=None):
    head_dim = width // HEADS
    factor = math.log2(math.e) / math.sqrt(head_dim)
    columns = [None] * (-(-width // 128))
    for head in range(HEADS):
        low, high, first, last = head_span(head, head_dim, width)
        picked = q[:, first:last] * lane_mask(low, high, first, last)
        scores = [
            lax.dot_general(
                picked,
                keys(first, last),
                (((1,), (1,)), ((), ())),
                preferred_element_type=jnp.float32,
            )
            for keys in key_parts
        ]
        if allowed is not None:
            scores = [jnp.where(allowed, s, -1e30) for s in scores]
        top = functools.reduce(jnp.maximum, [jnp.max(s, axis=-1, keepdims=True) for s in scores])
        exps = [jnp.exp2((s - top) * factor) for s in scores]
        total = sum(jnp.sum(e, axis=-1, keepdims=True) for e in exps)
        inverse = 1.0 / total
        result = None
        for e, values in zip(exps, value_parts):
            probs = (e * inverse).astype(jnp.bfloat16)
            part = jnp.dot(probs, values(first, last), preferred_element_type=jnp.float32)
            result = part if result is None else result + part
        for block in range(first // 128, -(-last // 128)):
            start, end = block * 128, min(width, block * 128 + 128)
            piece = result[:, start - first : end - first]
            if columns[block] is not None:
                lane = lax.broadcasted_iota(jnp.int32, (1, end - start), 1) + start
                piece = jnp.where(lane >= low, piece, columns[block])
            columns[block] = piece
    return jnp.concatenate(columns, axis=-1)


def fused_kernel(
    blocks,
    step_hbm,
    frame_hbm,
    hidden_hbm,
    ref_hbm,
    temb_hbm,
    gain1_hbm,
    gain2_hbm,
    spq_hbm,
    spk_hbm,
    spv_hbm,
    spo_hbm,
    tmq_hbm,
    tmk_hbm,
    tmv_hbm,
    tmo_hbm,
    out_ref,
    step_ref,
    frame_ref,
    hidden_ref,
    ref_ref,
    temb_ref,
    gain1_ref,
    gain2_ref,
    spq_ref,
    spk_ref,
    spv_ref,
    spo_ref,
    tmq_ref,
    tmk_ref,
    tmv_ref,
    tmo_ref,
    load_sem,
    ref_buf,
    q_buf,
    k_buf,
    v_buf,
    mid_buf,
    pe_buf,
    gain2_buf,
    fwd_out,
    fwd_in,
    bwd_out,
    bwd_in,
    ref_send,
    ref_recv,
    fwd_send,
    fwd_recv,
    bwd_send,
    bwd_recv,
):
    me = lax.axis_index("frame")
    frames_here, width, positions = hidden_ref.shape
    halves, rows = fwd_out.shape[0], fwd_out.shape[2]
    count = blocks * rows
    frames = frames_here * blocks
    head_dim = width // HEADS
    bf16 = jnp.bfloat16

    def peer(shift):
        return lax.rem(me + shift, blocks)

    loads = [
        pltpu.make_async_copy(source, target, load_sem.at[place])
        for place, (source, target) in enumerate(
            (
                (ref_hbm, ref_ref),
                (gain1_hbm, gain1_ref),
                (step_hbm, step_ref),
                (frame_hbm, frame_ref),
                (temb_hbm, temb_ref),
                (hidden_hbm, hidden_ref),
                (spq_hbm, spq_ref),
                (spk_hbm, spk_ref),
                (spv_hbm, spv_ref),
                (gain2_hbm, gain2_ref),
                (spo_hbm, spo_ref),
                (tmq_hbm, tmq_ref),
                (tmk_hbm, tmk_ref),
                (tmv_hbm, tmv_ref),
                (tmo_hbm, tmo_ref),
            )
        )
    ]
    for load in loads:
        load.start()

    barrier = pltpu.get_barrier_semaphore()
    for shift in range(1, blocks):
        pl.semaphore_signal(
            barrier, inc=1, device_id={"frame": peer(shift)}, device_id_type=pl.DeviceIdType.MESH
        )

    for load in loads[:2]:
        load.wait()
    gain1 = gain1_ref[...].reshape(1, width)
    ref_buf[me] = layer_norm(ref_ref[...].astype(jnp.float32), gain1).astype(bf16)
    pl.semaphore_wait(barrier, blocks - 1)

    def ref_copy(shift):
        return pltpu.make_async_remote_copy(
            src_ref=ref_buf.at[me],
            dst_ref=ref_buf.at[me],
            send_sem=ref_send.at[shift - 1],
            recv_sem=ref_recv.at[shift - 1],
            device_id={"frame": peer(shift)},
            device_id_type=pl.DeviceIdType.MESH,
        )

    whole = width // 128 * 128
    lanes = (pl.ds(0, whole), pl.ds(whole, 2 * width - whole))

    def fwd_copy(half, f, shift):
        return pltpu.make_async_remote_copy(
            src_ref=fwd_out.at[half, peer(shift), :, lanes[f]],
            dst_ref=fwd_in.at[half, me, :, lanes[f]],
            send_sem=fwd_send.at[half, f, shift - 1],
            recv_sem=fwd_recv.at[half, f, shift - 1],
            device_id={"frame": peer(shift)},
            device_id_type=pl.DeviceIdType.MESH,
        )

    def pack(first, second):
        return jnp.concatenate([first, second[..., whole:], second[..., :whole]], axis=-1)

    def unpack(both):
        second = [both[..., 2 * width - whole :], both[..., width : 2 * width - whole]]
        return both[..., :width], jnp.concatenate(second, axis=-1)

    def bwd_copy(half, shift):
        return pltpu.make_async_remote_copy(
            src_ref=bwd_out.at[half, peer(shift)],
            dst_ref=bwd_in.at[half, me],
            send_sem=bwd_send.at[half, shift - 1],
            recv_sem=bwd_recv.at[half, shift - 1],
            device_id={"frame": peer(shift)},
            device_id_type=pl.DeviceIdType.MESH,
        )

    for shift in range(1, blocks):
        ref_copy(shift).start()

    def column(row):
        return jnp.broadcast_to(row, (count, width)).T

    for load in loads[2:]:
        load.wait()
    steps = temb_ref.shape[1]
    chosen = lax.broadcasted_iota(jnp.int32, (steps, count), 0) == step_ref[0]
    temb = jnp.dot(
        temb_ref[...],
        jnp.where(chosen, 1.0, 0.0).astype(bf16),
        preferred_element_type=jnp.float32,
    )

    chan = lax.broadcasted_iota(jnp.int32, (1, width), 1)
    freq = jnp.exp(-(chan // 2 * 2).astype(jnp.float32) / width * math.log(10000.0))
    phase = (chan % 2).astype(jnp.float32) * (math.pi / 2)
    for f in range(frames_here):
        pe_buf[f] = column(jnp.sin(frame_ref[f].astype(jnp.float32) * freq + phase))

    gain1 = column(gain1)
    for f in range(frames_here):
        normed = []
        for half in range(halves):
            base = hidden_ref[f, :, half * count : (half + 1) * count].astype(jnp.float32) + temb
            mid_buf[half, f] = base
            normed.append(layer_norm_down(base, gain1).astype(bf16))
        normed = jnp.concatenate(normed, axis=1)
        query = project_down(spq_ref[...], normed, 0)
        for half in range(halves):
            for head in range(HEADS):
                low, high, first, last = head_span(head, head_dim, width)
                piece = query[first:last, half * count : (half + 1) * count]
                row = lax.broadcasted_iota(jnp.int32, piece.shape, 0) + first
                piece = jnp.where((row >= low) & (row < high), piece, 0.0)
                q_buf[half, f, head, : last - first] = piece.astype(bf16)
        k_buf[f, :positions] = project(normed.T, spk_ref[...])
        value = project_down(spv_ref[...], normed, 0)
        v_buf[f, :, :, :positions] = value.reshape(HEADS, head_dim, positions).astype(bf16)

    for shift in range(1, blocks):
        ref_copy(shift).wait_recv()
    ref_all = ref_buf[...].reshape(-1, width)
    ref_key = project(ref_all, spk_ref[...])
    ref_value = project_down(spv_ref[...], ref_all, 1)
    ref_value = ref_value.reshape(HEADS, head_dim, positions).astype(bf16)
    for f in range(frames_here):
        k_buf[f, positions:] = ref_key
        v_buf[f, :, :, positions:] = ref_value

    gain2_buf[...] = column(gain2_ref[...].reshape(1, width))
    factor = math.log2(math.e) / math.sqrt(head_dim)

    def spatial(half, carry):
        def score(f, head):
            low, high, first, last = head_span(head, head_dim, width)
            return jnp.dot(
                k_buf[f, :, first:last],
                q_buf[half, f, head, : last - first],
                preferred_element_type=jnp.float32,
            )

        units = [(f, head) for f in range(frames_here) for head in range(HEADS)]
        ahead = score(*units[0])
        for f in range(frames_here):
            done = []
            for head in range(HEADS):
                scores = ahead
                if f * HEADS + head + 1 < len(units):
                    ahead = score(*units[f * HEADS + head + 1])
                top = jnp.max(scores, axis=0, keepdims=True)
                exps = jnp.exp2((scores - top) * factor)
                inverse = 1.0 / jnp.sum(exps, axis=0, keepdims=True)
                probs = (exps * inverse).astype(bf16)
                done.append(jnp.dot(v_buf[f, head], probs, preferred_element_type=jnp.float32))
            attn = jnp.concatenate(done, axis=0).astype(bf16)
            mid = mid_buf[half, f] + project_down(spo_ref[...], attn, 0)
            mid_buf[half, f] = mid
            normed = layer_norm_down(mid, gain2_buf[...]) + pe_buf[f]
            normed = normed.T.astype(bf16).reshape(blocks, rows, width)
            if f == 0:
                first_tail = normed[:, :, whole:]
                fwd_out[half, :, :, :whole] = normed[:, :, :whole]
            else:
                fwd_out[half, :, :, whole:] = jnp.concatenate(
                    [first_tail, normed[:, :, whole:], normed[:, :, :whole]], axis=-1
                )
            for shift in range(1, blocks):
                fwd_copy(half, f, shift).start()
        fwd_in[half, me] = fwd_out[half, me]
        return carry

    lax.fori_loop(0, halves, spatial, 0)

    group = 8
    size = frames * group
    row_pos = lax.broadcasted_iota(jnp.int32, (size, size), 0) % group
    col_pos = lax.broadcasted_iota(jnp.int32, (size, size), 1) % group
    same = row_pos == col_pos

    def temporal(half, carry):
        for shift in range(1, blocks):
            for f in range(frames_here):
                fwd_copy(half, f, shift).wait_recv()
        normed = jnp.concatenate(unpack(fwd_in[half]), axis=0).reshape(frames * rows, width)

        def grouped(weight_ref):
            full = jnp.dot(normed, weight_ref[...], preferred_element_type=jnp.float32)
            full = full.reshape(frames, rows // group, group, width)
            return [full[:, g].reshape(size, width).astype(bf16) for g in range(rows // group)]

        q2, k2, v2 = grouped(tmq_ref), grouped(tmk_ref), grouped(tmv_ref)
        done = []
        for g in range(rows // group):
            attn = attend_heads(
                q2[g],
                [lambda a, b: k2[g][:, a:b]],
                [lambda a, b: v2[g][:, a:b]],
                width,
                same,
            )
            done.append(attn.reshape(frames, 1, group, width))
        attn = jnp.concatenate(done, axis=1).reshape(frames, rows, width).astype(bf16)
        bwd_out[half] = pack(attn[:blocks], attn[blocks:])
        for shift in range(1, blocks):
            bwd_copy(half, shift).start()
        bwd_in[half, me] = bwd_out[half, me]
        return carry

    lax.fori_loop(0, halves, temporal, 0)

    for half in range(halves):
        for shift in range(1, blocks):
            bwd_copy(half, shift).wait_recv()
        for f, attn in enumerate(unpack(bwd_in[half])):
            attn = attn.reshape(count, width)
            mixed = mid_buf[half, f] + project_down(tmo_ref[...], attn, 1)
            out_ref[f, :, half * count : (half + 1) * count] = mixed.astype(bf16)

    for shift in range(1, blocks):
        ref_copy(shift).wait_send()
        for half in range(halves):
            for f in range(frames_here):
                fwd_copy(half, f, shift).wait_send()
            bwd_copy(half, shift).wait_send()


def on_device_fused(
    hidden,
    ref_feats,
    frame_index,
    step_index,
    temb_table,
    norm_gain_1,
    norm_gain_2,
    *weights,
):
    frames_here, positions, width = hidden.shape
    blocks = lax.axis_size("frame")
    share = positions // blocks
    halves = 2
    rows = share // halves
    count = blocks * rows
    ref_rows = ref_feats.shape[0]
    bf16 = jnp.bfloat16
    dma = pltpu.SemaphoreType.DMA
    args = (
        step_index,
        frame_index,
        hidden.transpose(0, 2, 1),
        ref_feats,
        temb_table.T,
        norm_gain_1,
        norm_gain_2,
        *weights,
    )
    moved = (halves, blocks, rows, frames_here * width)
    out = pl.pallas_call(
        functools.partial(fused_kernel, blocks),
        out_shape=jax.ShapeDtypeStruct((frames_here, width, positions), bf16),
        in_specs=[pl.BlockSpec(memory_space=pltpu.HBM)] * len(args),
        out_specs=pl.BlockSpec(memory_space=pltpu.VMEM),
        scratch_shapes=[pltpu.SMEM(a.shape, a.dtype) for a in args[:2]]
        + [pltpu.VMEM(a.shape, a.dtype) for a in args[2:]]
        + [
            dma((len(args),)),
            pltpu.VMEM((blocks, ref_rows, width), bf16),
            pltpu.VMEM((halves, frames_here, HEADS, 256, count), bf16),
            pltpu.VMEM((frames_here, 2 * positions, width), bf16),
            pltpu.VMEM((frames_here, HEADS, width // HEADS, 2 * positions), bf16),
            pltpu.VMEM((halves, frames_here, width, count), jnp.float32),
            pltpu.VMEM((frames_here, width, count), jnp.float32),
            pltpu.VMEM((width, count), jnp.float32),
            pltpu.VMEM(moved, bf16),
            pltpu.VMEM(moved, bf16),
            pltpu.VMEM(moved, bf16),
            pltpu.VMEM(moved, bf16),
            dma((blocks - 1,)),
            dma((blocks - 1,)),
            dma((halves, frames_here, blocks - 1)),
            dma((halves, frames_here, blocks - 1)),
            dma((halves, blocks - 1)),
            dma((halves, blocks - 1)),
        ],
        compiler_params=pltpu.CompilerParams(
            collective_id=0, has_side_effects=True, vmem_limit_bytes=60 * 1024 * 1024
        ),
    )(*args)
    return out.transpose(0, 2, 1)


def on_device(hidden, ref_feats, frame_index, step_index, temb_table, *rest):
    blocks = lax.axis_size("frame")
    frames_here, positions, width = hidden.shape
    fits = (
        positions == 256
        and positions % (32 * blocks) == 0
        and frames_here == 2
        and 2 * width % 128 == 0
        and blocks * ref_feats.shape[0] == positions
        and ref_feats.shape[0] % 16 == 0
        and frames_here * blocks * 8 <= 128
    )
    body = on_device_fused if fits else on_device_plain
    return body(hidden, ref_feats, frame_index, step_index, temb_table, *rest)


def solution(mesh):
    in_specs = (
        P(("video", "frame"), None, None),
        P(("video", "frame"), None),
        P(("video", "frame")),
        P(),
        P(),
        P(),
        P(),
        P(),
        P(),
        P(),
        P(),
        P(),
        P(),
        P(),
        P(),
    )
    out_specs = P(("video", "frame"), None, None)
    return jax.shard_map(
        on_device, mesh=mesh, in_specs=in_specs, out_specs=out_specs, check_vma=False
    )
```

```python
import functools
import math

import jax
import jax.numpy as jnp
from jax import lax
from jax.experimental import pallas as pl
from jax.experimental.pallas import tpu as pltpu
from jax.sharding import PartitionSpec as P

HEADS = 8


def layer_norm(values, gain):
    mean = jnp.mean(values, axis=-1, keepdims=True)
    centered = values - mean
    var = jnp.mean(centered * centered, axis=-1, keepdims=True)
    return centered * lax.rsqrt(var + 1e-05) * gain


def positional(frame_index, width):
    chan = jnp.arange(width)
    freq = jnp.exp(-(chan // 2 * 2).astype(jnp.float32) / width * math.log(10000.0))
    phase = (chan % 2).astype(jnp.float32) * (math.pi / 2)
    return jnp.sin(frame_index.astype(jnp.float32)[:, None] * freq[None, :] + phase[None, :])


def project(rows, weight):
    return jnp.dot(rows, weight, preferred_element_type=jnp.float32).astype(jnp.bfloat16)


def temporal_attend(query, keys, values):
    frames, count, width = query.shape
    head_dim = width // HEADS
    q = query.reshape(frames, count, HEADS, head_dim)
    k = keys.reshape(frames, count, HEADS, head_dim)
    v = values.reshape(frames, count, HEADS, head_dim)
    scores = jnp.einsum("fnhd,gnhd->nhfg", q, k, preferred_element_type=jnp.float32) / math.sqrt(
        head_dim
    )
    probs = jax.nn.softmax(scores, axis=-1).astype(jnp.bfloat16)
    out = jnp.einsum("nhfg,gnhd->fnhd", probs, v, preferred_element_type=jnp.float32)
    return out.astype(jnp.bfloat16).reshape(frames, count, width)


def flatten_block(block):
    return block.reshape(block.shape[0], block.shape[2], block.shape[3])


def on_device_plain(
    hidden,
    ref_feats,
    frame_index,
    step_index,
    temb_table,
    norm_gain_1,
    norm_gain_2,
    sp_query,
    sp_key,
    sp_value,
    sp_out,
    tm_query,
    tm_key,
    tm_value,
    tm_out,
):
    frames_here, positions, width = hidden.shape
    head_dim = width // HEADS
    blocks = lax.axis_size("frame")
    share = positions // blocks
    temb = lax.dynamic_slice_in_dim(temb_table, step_index[0], 1, 0).astype(jnp.float32)
    base = hidden.astype(jnp.float32) + temb[None, :, :]
    normed_1 = layer_norm(base, norm_gain_1).astype(jnp.bfloat16)
    ref_local = layer_norm(ref_feats.astype(jnp.float32), norm_gain_1).astype(jnp.bfloat16)
    ref_all = lax.all_gather(ref_local, "frame", axis=0, tiled=True)
    ref_k = project(ref_all, sp_key)
    ref_v = project(ref_all, sp_value)
    q1 = project(normed_1, sp_query).reshape(frames_here, positions, HEADS, head_dim)
    k1 = project(normed_1, sp_key).reshape(frames_here, positions, HEADS, head_dim)
    v1 = project(normed_1, sp_value).reshape(frames_here, positions, HEADS, head_dim)
    ref_kh = ref_k.reshape(positions, HEADS, head_dim)
    ref_vh = ref_v.reshape(positions, HEADS, head_dim)
    scale = 1.0 / math.sqrt(head_dim)
    self_scores = jnp.einsum("fqhd,fkhd->fhqk", q1, k1, preferred_element_type=jnp.float32) * scale
    ref_scores = (
        jnp.einsum("fqhd,khd->fhqk", q1, ref_kh, preferred_element_type=jnp.float32) * scale
    )
    top = jnp.maximum(
        jnp.max(self_scores, axis=-1, keepdims=True), jnp.max(ref_scores, axis=-1, keepdims=True)
    )
    self_exp = jnp.exp(self_scores - top)
    ref_exp = jnp.exp(ref_scores - top)
    total = jnp.sum(self_exp, axis=-1, keepdims=True) + jnp.sum(ref_exp, axis=-1, keepdims=True)
    self_probs = (self_exp / total).astype(jnp.bfloat16)
    ref_probs = (ref_exp / total).astype(jnp.bfloat16)
    attn_1 = jnp.einsum("fhqk,fkhd->fqhd", self_probs, v1, preferred_element_type=jnp.float32)
    attn_1 = attn_1 + jnp.einsum(
        "fhqk,khd->fqhd", ref_probs, ref_vh, preferred_element_type=jnp.float32
    )
    attn_1 = attn_1.astype(jnp.bfloat16).reshape(frames_here, positions, width)
    mid = base + jnp.dot(attn_1, sp_out, preferred_element_type=jnp.float32)
    encoding = positional(frame_index, width)
    normed_2 = (layer_norm(mid, norm_gain_2) + encoding[:, None, :]).astype(jnp.bfloat16)
    moved = (
        project(normed_2, tm_query).reshape(frames_here, blocks, share, width),
        project(normed_2, tm_key).reshape(frames_here, blocks, share, width),
        project(normed_2, tm_value).reshape(frames_here, blocks, share, width),
    )
    result = temporal_attend(
        flatten_block(lax.all_to_all(moved[0], "frame", split_axis=1, concat_axis=0, tiled=True)),
        flatten_block(lax.all_to_all(moved[1], "frame", split_axis=1, concat_axis=0, tiled=True)),
        flatten_block(lax.all_to_all(moved[2], "frame", split_axis=1, concat_axis=0, tiled=True)),
    )
    attn_2 = result.reshape(result.shape[0], 1, result.shape[1], result.shape[2])
    returned = lax.all_to_all(attn_2, "frame", split_axis=0, concat_axis=1, tiled=True).reshape(
        frames_here, positions, width
    )
    return (mid + jnp.dot(returned, tm_out, preferred_element_type=jnp.float32)).astype(
        jnp.bfloat16
    )


def layer_norm_down(values, gain):
    mean = jnp.mean(values, axis=0, keepdims=True)
    centered = values - mean
    var = jnp.mean(centered * centered, axis=0, keepdims=True)
    return centered * lax.rsqrt(var + 1e-05) * gain


def project_down(weight, rows, contract):
    return lax.dot_general(
        weight, rows, (((0,), (contract,)), ((), ())), preferred_element_type=jnp.float32
    )


def head_span(head, head_dim, width):
    low = head * head_dim
    high = low + head_dim
    return low, high, low // 128 * 128, min(width, -(-high // 128) * 128)


def lane_mask(low, high, first, last):
    lane = lax.broadcasted_iota(jnp.int32, (1, last - first), 1) + first
    return jnp.where((lane >= low) & (lane < high), 1.0, 0.0).astype(jnp.bfloat16)


def attend_heads(q, key_parts, value_parts, width, allowed=None):
    head_dim = width // HEADS
    factor = math.log2(math.e) / math.sqrt(head_dim)
    columns = [None] * (-(-width // 128))
    for head in range(HEADS):
        low, high, first, last = head_span(head, head_dim, width)
        picked = q[:, first:last] * lane_mask(low, high, first, last)
        scores = [
            lax.dot_general(
                picked,
                keys(first, last),
                (((1,), (1,)), ((), ())),
                preferred_element_type=jnp.float32,
            )
            for keys in key_parts
        ]
        if allowed is not None:
            scores = [jnp.where(allowed, s, -1e30) for s in scores]
        top = functools.reduce(jnp.maximum, [jnp.max(s, axis=-1, keepdims=True) for s in scores])
        exps = [jnp.exp2((s - top) * factor) for s in scores]
        total = sum(jnp.sum(e, axis=-1, keepdims=True) for e in exps)
        inverse = 1.0 / total
        result = None
        for e, values in zip(exps, value_parts):
            probs = (e * inverse).astype(jnp.bfloat16)
            part = jnp.dot(probs, values(first, last), preferred_element_type=jnp.float32)
            result = part if result is None else result + part
        for block in range(first // 128, -(-last // 128)):
            start, end = block * 128, min(width, block * 128 + 128)
            piece = result[:, start - first : end - first]
            if columns[block] is not None:
                lane = lax.broadcasted_iota(jnp.int32, (1, end - start), 1) + start
                piece = jnp.where(lane >= low, piece, columns[block])
            columns[block] = piece
    return jnp.concatenate(columns, axis=-1)


def fused_kernel(
    blocks,
    step_hbm,
    frame_hbm,
    hidden_hbm,
    ref_hbm,
    temb_hbm,
    gain1_hbm,
    gain2_hbm,
    spq_hbm,
    spk_hbm,
    spv_hbm,
    spo_hbm,
    tmq_hbm,
    tmk_hbm,
    tmv_hbm,
    tmo_hbm,
    out_hbm,
    out_ref,
    store_sem,
    step_ref,
    frame_ref,
    hidden_ref,
    ref_ref,
    temb_ref,
    gain1_ref,
    gain2_ref,
    spq_ref,
    spk_ref,
    spv_ref,
    spo_ref,
    tmq_ref,
    tmk_ref,
    tmv_ref,
    tmo_ref,
    load_sem,
    ref_buf,
    q_buf,
    k_buf,
    v_buf,
    mid_buf,
    pe_buf,
    gain2_buf,
    fwd_out,
    fwd_in,
    bwd_out,
    bwd_in,
    ref_send,
    ref_recv,
    fwd_send,
    fwd_recv,
    bwd_send,
    bwd_recv,
):
    me = lax.axis_index("frame")
    frames_here, width, positions = hidden_ref.shape
    halves, rows = fwd_out.shape[0], fwd_out.shape[2]
    count = blocks * rows
    frames = frames_here * blocks
    head_dim = width // HEADS
    bf16 = jnp.bfloat16

    def peer(shift):
        return lax.rem(me + shift, blocks)

    loads = [
        pltpu.make_async_copy(source, target, load_sem.at[place])
        for place, (source, target) in enumerate(
            (
                (ref_hbm, ref_ref),
                (gain1_hbm, gain1_ref),
                (step_hbm, step_ref),
                (frame_hbm, frame_ref),
                (temb_hbm, temb_ref),
                (hidden_hbm, hidden_ref),
                (spq_hbm, spq_ref),
                (spk_hbm, spk_ref),
                (spv_hbm, spv_ref),
                (gain2_hbm, gain2_ref),
                (spo_hbm, spo_ref),
                (tmq_hbm, tmq_ref),
                (tmk_hbm, tmk_ref),
                (tmv_hbm, tmv_ref),
                (tmo_hbm, tmo_ref),
            )
        )
    ]
    for load in loads:
        load.start()

    barrier = pltpu.get_barrier_semaphore()
    for shift in range(1, blocks):
        pl.semaphore_signal(
            barrier, inc=1, device_id={"frame": peer(shift)}, device_id_type=pl.DeviceIdType.MESH
        )

    for load in loads[:2]:
        load.wait()
    gain1 = gain1_ref[...].reshape(1, width)
    ref_buf[me] = layer_norm(ref_ref[...].astype(jnp.float32), gain1).astype(bf16)
    pl.semaphore_wait(barrier, blocks - 1)

    def ref_copy(shift):
        return pltpu.make_async_remote_copy(
            src_ref=ref_buf.at[me],
            dst_ref=ref_buf.at[me],
            send_sem=ref_send.at[shift - 1],
            recv_sem=ref_recv.at[shift - 1],
            device_id={"frame": peer(shift)},
            device_id_type=pl.DeviceIdType.MESH,
        )

    whole = width // 128 * 128
    lanes = (pl.ds(0, whole), pl.ds(whole, 2 * width - whole))

    def fwd_copy(half, f, shift):
        return pltpu.make_async_remote_copy(
            src_ref=fwd_out.at[half, peer(shift), :, lanes[f]],
            dst_ref=fwd_in.at[half, me, :, lanes[f]],
            send_sem=fwd_send.at[half, f, shift - 1],
            recv_sem=fwd_recv.at[half, f, shift - 1],
            device_id={"frame": peer(shift)},
            device_id_type=pl.DeviceIdType.MESH,
        )

    def pack(first, second):
        return jnp.concatenate([first, second[..., whole:], second[..., :whole]], axis=-1)

    def unpack(both):
        second = [both[..., 2 * width - whole :], both[..., width : 2 * width - whole]]
        return both[..., :width], jnp.concatenate(second, axis=-1)

    def bwd_copy(half, shift):
        return pltpu.make_async_remote_copy(
            src_ref=bwd_out.at[half, peer(shift)],
            dst_ref=bwd_in.at[half, me],
            send_sem=bwd_send.at[half, shift - 1],
            recv_sem=bwd_recv.at[half, shift - 1],
            device_id={"frame": peer(shift)},
            device_id_type=pl.DeviceIdType.MESH,
        )

    for shift in range(1, blocks):
        ref_copy(shift).start()

    def column(row):
        return jnp.broadcast_to(row, (count, width)).T

    for load in loads[2:]:
        load.wait()
    steps = temb_ref.shape[1]
    chosen = lax.broadcasted_iota(jnp.int32, (steps, count), 0) == step_ref[0]
    temb = jnp.dot(
        temb_ref[...],
        jnp.where(chosen, 1.0, 0.0).astype(bf16),
        preferred_element_type=jnp.float32,
    )

    chan = lax.broadcasted_iota(jnp.int32, (1, width), 1)
    freq = jnp.exp(-(chan // 2 * 2).astype(jnp.float32) / width * math.log(10000.0))
    phase = (chan % 2).astype(jnp.float32) * (math.pi / 2)
    for f in range(frames_here):
        pe_buf[f] = column(jnp.sin(frame_ref[f].astype(jnp.float32) * freq + phase))

    pair_shape = (HEADS // 2, 2 * head_dim, positions)

    def pair_span(pair):
        _, _, first, _ = head_span(2 * pair, head_dim, width)
        _, _, _, last = head_span(2 * pair + 1, head_dim, width)
        return first, last

    def by_head(pair, piece):
        row = lax.broadcasted_iota(jnp.int32, piece.shape, 0) + pair_span(pair)[0]
        start = 2 * pair * head_dim
        middle, end = start + head_dim, start + 2 * head_dim
        one = jnp.where((row >= start) & (row < middle), piece, 0.0)
        two = jnp.where((row >= middle) & (row < end), piece, 0.0)
        return jnp.concatenate([one, two], axis=1).astype(bf16)

    def weigh(scores):
        top = jnp.max(scores, axis=0, keepdims=True)
        exps = jnp.exp2((scores - top) * factor)
        inverse = 1.0 / jnp.sum(exps, axis=0, keepdims=True)
        return (exps * inverse).astype(bf16)

    def own_rows(values, probs):
        both = jnp.dot(values, probs, preferred_element_type=jnp.float32)
        return [both[:head_dim, :count], both[head_dim:, count:]]

    factor = math.log2(math.e) / math.sqrt(head_dim)
    gain1 = column(gain1)
    for f in range(frames_here):
        normed = []
        for half in range(halves):
            base = hidden_ref[f, :, half * count : (half + 1) * count].astype(jnp.float32) + temb
            mid_buf[half, f] = base
            normed.append(layer_norm_down(base, gain1).astype(bf16))
        normed = jnp.concatenate(normed, axis=1)
        query = project_down(spq_ref[...], normed, 0)
        for half in range(halves):
            for pair in range(HEADS // 2):
                first, last = pair_span(pair)
                piece = query[first:last, half * count : (half + 1) * count]
                q_buf[half, f, pair, : last - first] = by_head(pair, piece)
        k_buf[f, :positions] = project(normed.T, spk_ref[...])
        value = project_down(spv_ref[...], normed, 0)
        v_buf[f, :, :, :positions] = value.reshape(pair_shape).astype(bf16)

    for shift in range(1, blocks):
        ref_copy(shift).wait_recv()
    ref_all = ref_buf[...].reshape(-1, width)
    ref_key = project(ref_all, spk_ref[...])
    ref_value = project_down(spv_ref[...], ref_all, 1)
    ref_value = ref_value.reshape(pair_shape).astype(bf16)
    for f in range(frames_here):
        k_buf[f, positions:] = ref_key
        v_buf[f, :, :, positions:] = ref_value

    gain2_buf[...] = column(gain2_ref[...].reshape(1, width))

    def spatial(half, carry):
        def score(f, pair):
            first, last = pair_span(pair)
            return jnp.dot(
                k_buf[f, :, first:last],
                q_buf[half, f, pair, : last - first],
                preferred_element_type=jnp.float32,
            )

        units = [(f, pair) for f in range(frames_here) for pair in range(HEADS // 2)]
        ahead = score(*units[0])
        for f in range(frames_here):
            done = []
            for pair in range(HEADS // 2):
                scores = ahead
                place = units.index((f, pair)) + 1
                if place < len(units):
                    ahead = score(*units[place])
                done += own_rows(v_buf[f, pair], weigh(scores))
            attn = jnp.concatenate(done, axis=0).astype(bf16)
            mid = mid_buf[half, f] + project_down(spo_ref[...], attn, 0)
            mid_buf[half, f] = mid
            normed = layer_norm_down(mid, gain2_buf[...]) + pe_buf[f]
            normed = normed.T.astype(bf16).reshape(blocks, rows, width)
            if f == 0:
                first_tail = normed[:, :, whole:]
                fwd_out[half, :, :, :whole] = normed[:, :, :whole]
            else:
                fwd_out[half, :, :, whole:] = jnp.concatenate(
                    [first_tail, normed[:, :, whole:], normed[:, :, :whole]], axis=-1
                )
            for shift in range(1, blocks):
                fwd_copy(half, f, shift).start()
        fwd_in[half, me] = fwd_out[half, me]
        return carry

    lax.fori_loop(0, halves, spatial, 0)

    group = 8
    size = frames * group
    row_pos = lax.broadcasted_iota(jnp.int32, (size, size), 0) % group
    col_pos = lax.broadcasted_iota(jnp.int32, (size, size), 1) % group
    same = row_pos == col_pos

    def temporal(half, carry):
        for shift in range(1, blocks):
            for f in range(frames_here):
                fwd_copy(half, f, shift).wait_recv()
        normed = jnp.concatenate(unpack(fwd_in[half]), axis=0).reshape(frames * rows, width)

        def grouped(weight_ref):
            full = jnp.dot(normed, weight_ref[...], preferred_element_type=jnp.float32)
            full = full.reshape(frames, rows // group, group, width)
            return [full[:, g].reshape(size, width).astype(bf16) for g in range(rows // group)]

        q2, k2, v2 = grouped(tmq_ref), grouped(tmk_ref), grouped(tmv_ref)
        done = []
        for g in range(rows // group):
            attn = attend_heads(
                q2[g],
                [lambda a, b: k2[g][:, a:b]],
                [lambda a, b: v2[g][:, a:b]],
                width,
                same,
            )
            done.append(attn.reshape(frames, 1, group, width))
        attn = jnp.concatenate(done, axis=1).reshape(frames, rows, width).astype(bf16)
        bwd_out[half] = pack(attn[:blocks], attn[blocks:])
        for shift in range(1, blocks):
            bwd_copy(half, shift).start()
        bwd_in[half, me] = bwd_out[half, me]
        return carry

    lax.fori_loop(0, halves, temporal, 0)

    stores = []
    for half in range(halves):
        for shift in range(1, blocks):
            bwd_copy(half, shift).wait_recv()
        for f, attn in enumerate(unpack(bwd_in[half])):
            attn = attn.reshape(count, width)
            mixed = mid_buf[half, f] + project_down(tmo_ref[...], attn, 1)
            out_ref[f, :, half * count : (half + 1) * count] = mixed.astype(bf16)
            stores.append(
                pltpu.make_async_copy(
                    out_ref.at[f, :, pl.ds(half * count, count)],
                    out_hbm.at[f, :, pl.ds(half * count, count)],
                    store_sem.at[half, f],
                )
            )
            stores[-1].start()

    for store in stores:
        store.wait()
    for shift in range(1, blocks):
        ref_copy(shift).wait_send()
        for half in range(halves):
            for f in range(frames_here):
                fwd_copy(half, f, shift).wait_send()
            bwd_copy(half, shift).wait_send()


def hand_over(parts, source, target, sem):
    size = source.shape[1] // parts
    copies = []
    for part in range(parts):
        rows = pl.ds(part * size, size)
        copies.append(
            pltpu.make_async_copy(source.at[:, rows], target.at[:, rows], sem.at[part])
        )
        copies[-1].start()
    for copy in copies:
        copy.wait()


def on_device_fused(
    hidden,
    ref_feats,
    frame_index,
    step_index,
    temb_table,
    norm_gain_1,
    norm_gain_2,
    *weights,
):
    frames_here, positions, width = hidden.shape
    blocks = lax.axis_size("frame")
    share = positions // blocks
    halves = 2
    rows = share // halves
    count = blocks * rows
    ref_rows = ref_feats.shape[0]
    bf16 = jnp.bfloat16
    dma = pltpu.SemaphoreType.DMA
    args = (
        step_index,
        frame_index,
        hidden.transpose(0, 2, 1),
        ref_feats,
        temb_table.T,
        norm_gain_1,
        norm_gain_2,
        *weights,
    )
    moved = (halves, blocks, rows, frames_here * width)
    out = pl.pallas_call(
        functools.partial(fused_kernel, blocks),
        out_shape=jax.ShapeDtypeStruct((frames_here, width, positions), bf16),
        in_specs=[pl.BlockSpec(memory_space=pltpu.HBM)] * len(args),
        out_specs=pl.BlockSpec(memory_space=pltpu.HBM),
        scratch_shapes=[pltpu.VMEM((frames_here, width, positions), bf16), dma((halves, frames_here))]
        + [pltpu.SMEM(a.shape, a.dtype) for a in args[:2]]
        + [pltpu.VMEM(a.shape, a.dtype) for a in args[2:]]
        + [
            dma((len(args),)),
            pltpu.VMEM((blocks, ref_rows, width), bf16),
            pltpu.VMEM((halves, frames_here, HEADS // 2, 256, 2 * count), bf16),
            pltpu.VMEM((frames_here, 2 * positions, width), bf16),
            pltpu.VMEM((frames_here, HEADS // 2, 2 * width // HEADS, 2 * positions), bf16),
            pltpu.VMEM((halves, frames_here, width, count), jnp.float32),
            pltpu.VMEM((frames_here, width, count), jnp.float32),
            pltpu.VMEM((width, count), jnp.float32),
            pltpu.VMEM(moved, bf16),
            pltpu.VMEM(moved, bf16),
            pltpu.VMEM(moved, bf16),
            pltpu.VMEM(moved, bf16),
            dma((blocks - 1,)),
            dma((blocks - 1,)),
            dma((halves, frames_here, blocks - 1)),
            dma((halves, frames_here, blocks - 1)),
            dma((halves, blocks - 1)),
            dma((halves, blocks - 1)),
        ],
        compiler_params=pltpu.CompilerParams(
            collective_id=0, has_side_effects=True, vmem_limit_bytes=60 * 1024 * 1024
        ),
    )(*args)
    parts = 4
    out = pl.pallas_call(
        functools.partial(hand_over, parts),
        out_shape=jax.ShapeDtypeStruct(out.shape, out.dtype),
        in_specs=[pl.BlockSpec(memory_space=pltpu.HBM)],
        out_specs=pl.BlockSpec(memory_space=pltpu.HBM),
        scratch_shapes=[dma((parts,))],
        compiler_params=pltpu.CompilerParams(vmem_limit_bytes=60 * 1024 * 1024),
    )(out)
    return out.transpose(0, 2, 1)


def on_device(hidden, ref_feats, frame_index, step_index, temb_table, *rest):
    blocks = lax.axis_size("frame")
    frames_here, positions, width = hidden.shape
    fits = (
        positions == 256
        and positions % (32 * blocks) == 0
        and frames_here == 2
        and 2 * width % 128 == 0
        and blocks * ref_feats.shape[0] == positions
        and ref_feats.shape[0] % 16 == 0
        and frames_here * blocks * 8 <= 128
    )
    body = on_device_fused if fits else on_device_plain
    return body(hidden, ref_feats, frame_index, step_index, temb_table, *rest)


def solution(mesh):
    in_specs = (
        P(("video", "frame"), None, None),
        P(("video", "frame"), None),
        P(("video", "frame")),
        P(),
        P(),
        P(),
        P(),
        P(),
        P(),
        P(),
        P(),
        P(),
        P(),
        P(),
        P(),
    )
    out_specs = P(("video", "frame"), None, None)
    return jax.shard_map(
        on_device, mesh=mesh, in_specs=in_specs, out_specs=out_specs, check_vma=False
    )
```

```python
import functools
import math

import jax
import jax.numpy as jnp
from jax import lax
from jax.experimental import pallas as pl
from jax.experimental.pallas import tpu as pltpu
from jax.sharding import PartitionSpec as P

HEADS = 8


def layer_norm(values, gain):
    mean = jnp.mean(values, axis=-1, keepdims=True)
    centered = values - mean
    var = jnp.mean(centered * centered, axis=-1, keepdims=True)
    return centered * lax.rsqrt(var + 1e-05) * gain


def positional(frame_index, width):
    chan = jnp.arange(width)
    freq = jnp.exp(-(chan // 2 * 2).astype(jnp.float32) / width * math.log(10000.0))
    phase = (chan % 2).astype(jnp.float32) * (math.pi / 2)
    return jnp.sin(frame_index.astype(jnp.float32)[:, None] * freq[None, :] + phase[None, :])


def project(rows, weight):
    return jnp.dot(rows, weight, preferred_element_type=jnp.float32).astype(jnp.bfloat16)


def temporal_attend(query, keys, values):
    frames, count, width = query.shape
    head_dim = width // HEADS
    q = query.reshape(frames, count, HEADS, head_dim)
    k = keys.reshape(frames, count, HEADS, head_dim)
    v = values.reshape(frames, count, HEADS, head_dim)
    scores = jnp.einsum("fnhd,gnhd->nhfg", q, k, preferred_element_type=jnp.float32) / math.sqrt(
        head_dim
    )
    probs = jax.nn.softmax(scores, axis=-1).astype(jnp.bfloat16)
    out = jnp.einsum("nhfg,gnhd->fnhd", probs, v, preferred_element_type=jnp.float32)
    return out.astype(jnp.bfloat16).reshape(frames, count, width)


def flatten_block(block):
    return block.reshape(block.shape[0], block.shape[2], block.shape[3])


def on_device_plain(
    hidden,
    ref_feats,
    frame_index,
    step_index,
    temb_table,
    norm_gain_1,
    norm_gain_2,
    sp_query,
    sp_key,
    sp_value,
    sp_out,
    tm_query,
    tm_key,
    tm_value,
    tm_out,
):
    frames_here, positions, width = hidden.shape
    head_dim = width // HEADS
    blocks = lax.axis_size("frame")
    share = positions // blocks
    temb = lax.dynamic_slice_in_dim(temb_table, step_index[0], 1, 0).astype(jnp.float32)
    base = hidden.astype(jnp.float32) + temb[None, :, :]
    normed_1 = layer_norm(base, norm_gain_1).astype(jnp.bfloat16)
    ref_local = layer_norm(ref_feats.astype(jnp.float32), norm_gain_1).astype(jnp.bfloat16)
    ref_all = lax.all_gather(ref_local, "frame", axis=0, tiled=True)
    ref_k = project(ref_all, sp_key)
    ref_v = project(ref_all, sp_value)
    q1 = project(normed_1, sp_query).reshape(frames_here, positions, HEADS, head_dim)
    k1 = project(normed_1, sp_key).reshape(frames_here, positions, HEADS, head_dim)
    v1 = project(normed_1, sp_value).reshape(frames_here, positions, HEADS, head_dim)
    ref_kh = ref_k.reshape(positions, HEADS, head_dim)
    ref_vh = ref_v.reshape(positions, HEADS, head_dim)
    scale = 1.0 / math.sqrt(head_dim)
    self_scores = jnp.einsum("fqhd,fkhd->fhqk", q1, k1, preferred_element_type=jnp.float32) * scale
    ref_scores = (
        jnp.einsum("fqhd,khd->fhqk", q1, ref_kh, preferred_element_type=jnp.float32) * scale
    )
    top = jnp.maximum(
        jnp.max(self_scores, axis=-1, keepdims=True), jnp.max(ref_scores, axis=-1, keepdims=True)
    )
    self_exp = jnp.exp(self_scores - top)
    ref_exp = jnp.exp(ref_scores - top)
    total = jnp.sum(self_exp, axis=-1, keepdims=True) + jnp.sum(ref_exp, axis=-1, keepdims=True)
    self_probs = (self_exp / total).astype(jnp.bfloat16)
    ref_probs = (ref_exp / total).astype(jnp.bfloat16)
    attn_1 = jnp.einsum("fhqk,fkhd->fqhd", self_probs, v1, preferred_element_type=jnp.float32)
    attn_1 = attn_1 + jnp.einsum(
        "fhqk,khd->fqhd", ref_probs, ref_vh, preferred_element_type=jnp.float32
    )
    attn_1 = attn_1.astype(jnp.bfloat16).reshape(frames_here, positions, width)
    mid = base + jnp.dot(attn_1, sp_out, preferred_element_type=jnp.float32)
    encoding = positional(frame_index, width)
    normed_2 = (layer_norm(mid, norm_gain_2) + encoding[:, None, :]).astype(jnp.bfloat16)
    moved = (
        project(normed_2, tm_query).reshape(frames_here, blocks, share, width),
        project(normed_2, tm_key).reshape(frames_here, blocks, share, width),
        project(normed_2, tm_value).reshape(frames_here, blocks, share, width),
    )
    result = temporal_attend(
        flatten_block(lax.all_to_all(moved[0], "frame", split_axis=1, concat_axis=0, tiled=True)),
        flatten_block(lax.all_to_all(moved[1], "frame", split_axis=1, concat_axis=0, tiled=True)),
        flatten_block(lax.all_to_all(moved[2], "frame", split_axis=1, concat_axis=0, tiled=True)),
    )
    attn_2 = result.reshape(result.shape[0], 1, result.shape[1], result.shape[2])
    returned = lax.all_to_all(attn_2, "frame", split_axis=0, concat_axis=1, tiled=True).reshape(
        frames_here, positions, width
    )
    return (mid + jnp.dot(returned, tm_out, preferred_element_type=jnp.float32)).astype(
        jnp.bfloat16
    )


def layer_norm_down(values, gain):
    mean = jnp.mean(values, axis=0, keepdims=True)
    centered = values - mean
    var = jnp.mean(centered * centered, axis=0, keepdims=True)
    return centered * lax.rsqrt(var + 1e-05) * gain


def project_down(weight, rows, contract):
    return lax.dot_general(
        weight, rows, (((0,), (contract,)), ((), ())), preferred_element_type=jnp.float32
    )


def head_span(head, head_dim, width):
    low = head * head_dim
    high = low + head_dim
    return low, high, low // 128 * 128, min(width, -(-high // 128) * 128)


def fused_kernel(
    blocks,
    step_hbm,
    frame_hbm,
    hidden_hbm,
    ref_hbm,
    temb_hbm,
    gain1_hbm,
    gain2_hbm,
    spq_hbm,
    spk_hbm,
    spv_hbm,
    spo_hbm,
    tmq_hbm,
    tmk_hbm,
    tmv_hbm,
    tmo_hbm,
    out_hbm,
    out_ref,
    store_sem,
    step_ref,
    frame_ref,
    hidden_ref,
    ref_ref,
    temb_ref,
    gain1_ref,
    gain2_ref,
    spq_ref,
    spk_ref,
    spv_ref,
    spo_ref,
    tmq_ref,
    tmk_ref,
    tmv_ref,
    tmo_ref,
    load_sem,
    ref_buf,
    q_buf,
    k_buf,
    self_buf,
    v_buf,
    mid_buf,
    pe_buf,
    gain2_buf,
    fwd_out,
    fwd_in,
    bwd_out,
    bwd_in,
    ref_send,
    ref_recv,
    fwd_send,
    fwd_recv,
    bwd_send,
    bwd_recv,
):
    me = lax.axis_index("frame")
    frames_here, width, positions = hidden_ref.shape
    halves, rows = fwd_out.shape[0], fwd_out.shape[2]
    count = blocks * rows
    frames = frames_here * blocks
    head_dim = width // HEADS
    bf16 = jnp.bfloat16

    def peer(shift):
        return lax.rem(me + shift, blocks)

    loads = [
        pltpu.make_async_copy(source, target, load_sem.at[place])
        for place, (source, target) in enumerate(
            (
                (ref_hbm, ref_ref),
                (gain1_hbm, gain1_ref),
                (step_hbm, step_ref),
                (frame_hbm, frame_ref),
                (temb_hbm, temb_ref),
                (hidden_hbm, hidden_ref),
                (spq_hbm, spq_ref),
                (spk_hbm, spk_ref),
                (spv_hbm, spv_ref),
                (gain2_hbm, gain2_ref),
                (spo_hbm, spo_ref),
                (tmq_hbm, tmq_ref),
                (tmk_hbm, tmk_ref),
                (tmv_hbm, tmv_ref),
                (tmo_hbm, tmo_ref),
            )
        )
    ]
    for load in loads:
        load.start()

    barrier = pltpu.get_barrier_semaphore()
    for shift in range(1, blocks):
        pl.semaphore_signal(
            barrier, inc=1, device_id={"frame": peer(shift)}, device_id_type=pl.DeviceIdType.MESH
        )

    for load in loads[:2]:
        load.wait()
    gain1 = gain1_ref[...].reshape(1, width)
    ref_buf[me] = layer_norm(ref_ref[...].astype(jnp.float32), gain1).astype(bf16)
    pl.semaphore_wait(barrier, blocks - 1)

    def ref_copy(shift):
        return pltpu.make_async_remote_copy(
            src_ref=ref_buf.at[me],
            dst_ref=ref_buf.at[me],
            send_sem=ref_send.at[shift - 1],
            recv_sem=ref_recv.at[shift - 1],
            device_id={"frame": peer(shift)},
            device_id_type=pl.DeviceIdType.MESH,
        )

    whole = width // 128 * 128
    lanes = (pl.ds(0, whole), pl.ds(whole, 2 * width - whole))

    def fwd_copy(half, f, shift):
        return pltpu.make_async_remote_copy(
            src_ref=fwd_out.at[half, peer(shift), :, lanes[f]],
            dst_ref=fwd_in.at[half, me, :, lanes[f]],
            send_sem=fwd_send.at[half, f, shift - 1],
            recv_sem=fwd_recv.at[half, f, shift - 1],
            device_id={"frame": peer(shift)},
            device_id_type=pl.DeviceIdType.MESH,
        )

    def pack(first, second):
        return jnp.concatenate([first, second[..., whole:], second[..., :whole]], axis=-1)

    def unpack(both):
        second = [both[..., 2 * width - whole :], both[..., width : 2 * width - whole]]
        return both[..., :width], jnp.concatenate(second, axis=-1)

    def bwd_copy(half, shift):
        return pltpu.make_async_remote_copy(
            src_ref=bwd_out.at[half, peer(shift)],
            dst_ref=bwd_in.at[half, me],
            send_sem=bwd_send.at[half, shift - 1],
            recv_sem=bwd_recv.at[half, shift - 1],
            device_id={"frame": peer(shift)},
            device_id_type=pl.DeviceIdType.MESH,
        )

    for shift in range(1, blocks):
        ref_copy(shift).start()

    def column(row):
        return jnp.broadcast_to(row, (count, width)).T

    for load in loads[2:9]:
        load.wait()
    steps = temb_ref.shape[1]
    chosen = lax.broadcasted_iota(jnp.int32, (steps, count), 0) == step_ref[0]
    temb = jnp.dot(
        temb_ref[...],
        jnp.where(chosen, 1.0, 0.0).astype(bf16),
        preferred_element_type=jnp.float32,
    )

    chan = lax.broadcasted_iota(jnp.int32, (1, width), 1)
    freq = jnp.exp(-(chan // 2 * 2).astype(jnp.float32) / width * math.log(10000.0))
    phase = (chan % 2).astype(jnp.float32) * (math.pi / 2)
    for f in range(frames_here):
        pe_buf[f] = column(jnp.sin(frame_ref[f].astype(jnp.float32) * freq + phase))

    pair_shape = (HEADS // 2, 2 * head_dim, positions)

    def pair_span(pair):
        _, _, first, _ = head_span(2 * pair, head_dim, width)
        _, _, _, last = head_span(2 * pair + 1, head_dim, width)
        return first, last

    def by_head(pair, piece):
        row = lax.broadcasted_iota(jnp.int32, piece.shape, 0) + pair_span(pair)[0]
        start = 2 * pair * head_dim
        middle, end = start + head_dim, start + 2 * head_dim
        one = jnp.where((row >= start) & (row < middle), piece, 0.0)
        two = jnp.where((row >= middle) & (row < end), piece, 0.0)
        return jnp.concatenate([one, two], axis=1).astype(bf16)

    def weigh(scores):
        tops = [jnp.max(s, axis=0, keepdims=True) for s in scores]
        top = functools.reduce(jnp.maximum, tops)
        exps = [jnp.exp2((s - top) * factor) for s in scores]
        inverse = 1.0 / sum(jnp.sum(e, axis=0, keepdims=True) for e in exps)
        return jnp.concatenate([(e * inverse).astype(bf16) for e in exps], axis=0)

    def own_rows(values, probs):
        both = jnp.dot(values, probs, preferred_element_type=jnp.float32)
        return [both[:head_dim, :count], both[head_dim:, count:]]

    factor = math.log2(math.e) / math.sqrt(head_dim)
    gain1 = column(gain1)
    for f in range(frames_here):
        normed = []
        for half in range(halves):
            base = hidden_ref[f, :, half * count : (half + 1) * count].astype(jnp.float32) + temb
            mid_buf[half, f] = base
            normed.append(layer_norm_down(base, gain1).astype(bf16))
        normed = jnp.concatenate(normed, axis=1)
        query = project_down(spq_ref[...], normed, 0)
        key = project(normed.T, spk_ref[...])
        for half in range(halves):
            for pair in range(HEADS // 2):
                first, last = pair_span(pair)
                picked = by_head(pair, query[first:last, half * count : (half + 1) * count])
                q_buf[half, f, pair, : last - first] = picked
                self_buf[half, f, pair] = jnp.dot(
                    key[:, first:last], picked, preferred_element_type=jnp.float32
                )
        value = project_down(spv_ref[...], normed, 0)
        v_buf[f, :, :, :positions] = value.reshape(pair_shape).astype(bf16)

    for load in loads[9:11]:
        load.wait()
    gain2_buf[...] = column(gain2_ref[...].reshape(1, width))
    for shift in range(1, blocks):
        ref_copy(shift).wait_recv()
    ref_all = ref_buf[...].reshape(-1, width)
    k_buf[...] = project(ref_all, spk_ref[...])
    ref_value = project_down(spv_ref[...], ref_all, 1)
    ref_value = ref_value.reshape(pair_shape).astype(bf16)
    for f in range(frames_here):
        v_buf[f, :, :, positions:] = ref_value


    def spatial(half, carry):
        def score(f, pair):
            first, last = pair_span(pair)
            return jnp.dot(
                k_buf[:, first:last],
                q_buf[half, f, pair, : last - first],
                preferred_element_type=jnp.float32,
            )

        units = [(f, pair) for f in range(frames_here) for pair in range(HEADS // 2)]
        ahead = score(*units[0])
        for f in range(frames_here):
            done = []
            for pair in range(HEADS // 2):
                scores = ahead
                place = units.index((f, pair)) + 1
                if place < len(units):
                    ahead = score(*units[place])
                done += own_rows(v_buf[f, pair], weigh([self_buf[half, f, pair], scores]))
            attn = jnp.concatenate(done, axis=0).astype(bf16)
            mid = mid_buf[half, f] + project_down(spo_ref[...], attn, 0)
            mid_buf[half, f] = mid
            normed = layer_norm_down(mid, gain2_buf[...]) + pe_buf[f]
            normed = normed.T.astype(bf16).reshape(blocks, rows, width)
            if f == 0:
                first_tail = normed[:, :, whole:]
                fwd_out[half, :, :, :whole] = normed[:, :, :whole]
            else:
                fwd_out[half, :, :, whole:] = jnp.concatenate(
                    [first_tail, normed[:, :, whole:], normed[:, :, :whole]], axis=-1
                )
            for shift in range(1, blocks):
                fwd_copy(half, f, shift).start()
        fwd_in[half, me] = fwd_out[half, me]
        return carry

    lax.fori_loop(0, halves, spatial, 0)

    for load in loads[11:]:
        load.wait()
    group = 8
    row_pos = lax.broadcasted_iota(jnp.int32, (count, 2 * count), 0) % group
    col_pos = lax.broadcasted_iota(jnp.int32, (count, 2 * count), 1) % group
    same = row_pos == col_pos

    def temporal(half, carry):
        for shift in range(1, blocks):
            for f in range(frames_here):
                fwd_copy(half, f, shift).wait_recv()
        normed = jnp.concatenate(unpack(fwd_in[half]), axis=0).astype(jnp.float32)
        normed = normed.reshape(frames, rows // group, group, width)
        normed = jnp.concatenate(
            [normed[:, g].reshape(count, width) for g in range(rows // group)], axis=0
        ).astype(bf16)
        query = project_down(tmq_ref[...], normed, 1)
        key = project(normed, tmk_ref[...])
        value = project_down(tmv_ref[...], normed, 1).reshape(HEADS // 2, 2 * head_dim, -1)
        value = value.astype(bf16)

        def score(g, pair):
            first, last = pair_span(pair)
            columns = slice(g * count, (g + 1) * count)
            picked = by_head(pair, query[first:last, columns])
            found = jnp.dot(
                key[columns, first:last], picked, preferred_element_type=jnp.float32
            )
            return jnp.where(same, found, -1e30)

        done = []
        for g in range(rows // group):
            attn = []
            for pair in range(HEADS // 2):
                probs = weigh([score(g, pair)])
                attn += own_rows(value[pair, :, g * count : (g + 1) * count], probs)
            attn = jnp.concatenate(attn, axis=0).T
            done.append(attn.reshape(frames, 1, group, width))
        attn = jnp.concatenate(done, axis=1).reshape(frames, rows, width).astype(bf16)
        bwd_out[half] = pack(attn[:blocks], attn[blocks:])
        for shift in range(1, blocks):
            bwd_copy(half, shift).start()
        bwd_in[half, me] = bwd_out[half, me]
        return carry

    lax.fori_loop(0, halves, temporal, 0)

    stores = []
    for half in range(halves):
        for shift in range(1, blocks):
            bwd_copy(half, shift).wait_recv()
        for f, attn in enumerate(unpack(bwd_in[half])):
            attn = attn.reshape(count, width)
            mixed = mid_buf[half, f] + project_down(tmo_ref[...], attn, 1)
            out_ref[f, :, half * count : (half + 1) * count] = mixed.astype(bf16)
            stores.append(
                pltpu.make_async_copy(
                    out_ref.at[f, :, pl.ds(half * count, count)],
                    out_hbm.at[f, :, pl.ds(half * count, count)],
                    store_sem.at[half, f],
                )
            )
            stores[-1].start()

    for store in stores:
        store.wait()
    for shift in range(1, blocks):
        ref_copy(shift).wait_send()
        for half in range(halves):
            for f in range(frames_here):
                fwd_copy(half, f, shift).wait_send()
            bwd_copy(half, shift).wait_send()


def on_device_fused(
    hidden,
    ref_feats,
    frame_index,
    step_index,
    temb_table,
    norm_gain_1,
    norm_gain_2,
    *weights,
):
    frames_here, positions, width = hidden.shape
    blocks = lax.axis_size("frame")
    share = positions // blocks
    halves = 2
    rows = share // halves
    count = blocks * rows
    ref_rows = ref_feats.shape[0]
    bf16 = jnp.bfloat16
    dma = pltpu.SemaphoreType.DMA
    args = (
        step_index,
        frame_index,
        hidden.transpose(0, 2, 1),
        ref_feats,
        temb_table.T,
        norm_gain_1,
        norm_gain_2,
        *weights,
    )
    moved = (halves, blocks, rows, frames_here * width)
    out = pl.pallas_call(
        functools.partial(fused_kernel, blocks),
        out_shape=jax.ShapeDtypeStruct((frames_here, width, positions), bf16),
        in_specs=[pl.BlockSpec(memory_space=pltpu.HBM)] * len(args),
        out_specs=pl.BlockSpec(memory_space=pltpu.HBM),
        scratch_shapes=[pltpu.VMEM((frames_here, width, positions), bf16), dma((halves, frames_here))]
        + [pltpu.SMEM(a.shape, a.dtype) for a in args[:2]]
        + [pltpu.VMEM(a.shape, a.dtype) for a in args[2:]]
        + [
            dma((len(args),)),
            pltpu.VMEM((blocks, ref_rows, width), bf16),
            pltpu.VMEM((halves, frames_here, HEADS // 2, 256, 2 * count), bf16),
            pltpu.VMEM((blocks * ref_rows, width), bf16),
            pltpu.VMEM((halves, frames_here, HEADS // 2, positions, 2 * count), jnp.float32),
            pltpu.VMEM((frames_here, HEADS // 2, 2 * width // HEADS, 2 * positions), bf16),
            pltpu.VMEM((halves, frames_here, width, count), jnp.float32),
            pltpu.VMEM((frames_here, width, count), jnp.float32),
            pltpu.VMEM((width, count), jnp.float32),
            pltpu.VMEM(moved, bf16),
            pltpu.VMEM(moved, bf16),
            pltpu.VMEM(moved, bf16),
            pltpu.VMEM(moved, bf16),
            dma((blocks - 1,)),
            dma((blocks - 1,)),
            dma((halves, frames_here, blocks - 1)),
            dma((halves, frames_here, blocks - 1)),
            dma((halves, blocks - 1)),
            dma((halves, blocks - 1)),
        ],
        compiler_params=pltpu.CompilerParams(
            collective_id=0, has_side_effects=True, vmem_limit_bytes=60 * 1024 * 1024
        ),
    )(*args)
    return out.transpose(0, 2, 1)


def on_device(hidden, ref_feats, frame_index, step_index, temb_table, *rest):
    blocks = lax.axis_size("frame")
    frames_here, positions, width = hidden.shape
    fits = (
        positions == 256
        and positions % (32 * blocks) == 0
        and frames_here == 2
        and 2 * width % 128 == 0
        and blocks * ref_feats.shape[0] == positions
        and ref_feats.shape[0] % 16 == 0
        and frames_here * blocks * 8 == positions // 2
    )
    body = on_device_fused if fits else on_device_plain
    return body(hidden, ref_feats, frame_index, step_index, temb_table, *rest)


def solution(mesh):
    in_specs = (
        P(("video", "frame"), None, None),
        P(("video", "frame"), None),
        P(("video", "frame")),
        P(),
        P(),
        P(),
        P(),
        P(),
        P(),
        P(),
        P(),
        P(),
        P(),
        P(),
        P(),
    )
    out_specs = P(("video", "frame"), None, None)
    return jax.shard_map(
        on_device, mesh=mesh, in_specs=in_specs, out_specs=out_specs, check_vma=False
    )
```

```python
import functools
import math

import jax
import jax.numpy as jnp
from jax import lax
from jax.experimental import pallas as pl
from jax.experimental.pallas import tpu as pltpu
from jax.sharding import PartitionSpec as P

HEADS = 8


def layer_norm(values, gain):
    mean = jnp.mean(values, axis=-1, keepdims=True)
    centered = values - mean
    var = jnp.mean(centered * centered, axis=-1, keepdims=True)
    return centered * lax.rsqrt(var + 1e-05) * gain


def positional(frame_index, width):
    chan = jnp.arange(width)
    freq = jnp.exp(-(chan // 2 * 2).astype(jnp.float32) / width * math.log(10000.0))
    phase = (chan % 2).astype(jnp.float32) * (math.pi / 2)
    return jnp.sin(frame_index.astype(jnp.float32)[:, None] * freq[None, :] + phase[None, :])


def project(rows, weight):
    return jnp.dot(rows, weight, preferred_element_type=jnp.float32).astype(jnp.bfloat16)


def temporal_attend(query, keys, values):
    frames, count, width = query.shape
    head_dim = width // HEADS
    q = query.reshape(frames, count, HEADS, head_dim)
    k = keys.reshape(frames, count, HEADS, head_dim)
    v = values.reshape(frames, count, HEADS, head_dim)
    scores = jnp.einsum("fnhd,gnhd->nhfg", q, k, preferred_element_type=jnp.float32) / math.sqrt(
        head_dim
    )
    probs = jax.nn.softmax(scores, axis=-1).astype(jnp.bfloat16)
    out = jnp.einsum("nhfg,gnhd->fnhd", probs, v, preferred_element_type=jnp.float32)
    return out.astype(jnp.bfloat16).reshape(frames, count, width)


def flatten_block(block):
    return block.reshape(block.shape[0], block.shape[2], block.shape[3])


def on_device_plain(
    hidden,
    ref_feats,
    frame_index,
    step_index,
    temb_table,
    norm_gain_1,
    norm_gain_2,
    sp_query,
    sp_key,
    sp_value,
    sp_out,
    tm_query,
    tm_key,
    tm_value,
    tm_out,
):
    frames_here, positions, width = hidden.shape
    head_dim = width // HEADS
    blocks = lax.axis_size("frame")
    share = positions // blocks
    temb = lax.dynamic_slice_in_dim(temb_table, step_index[0], 1, 0).astype(jnp.float32)
    base = hidden.astype(jnp.float32) + temb[None, :, :]
    normed_1 = layer_norm(base, norm_gain_1).astype(jnp.bfloat16)
    ref_local = layer_norm(ref_feats.astype(jnp.float32), norm_gain_1).astype(jnp.bfloat16)
    ref_all = lax.all_gather(ref_local, "frame", axis=0, tiled=True)
    ref_k = project(ref_all, sp_key)
    ref_v = project(ref_all, sp_value)
    q1 = project(normed_1, sp_query).reshape(frames_here, positions, HEADS, head_dim)
    k1 = project(normed_1, sp_key).reshape(frames_here, positions, HEADS, head_dim)
    v1 = project(normed_1, sp_value).reshape(frames_here, positions, HEADS, head_dim)
    ref_kh = ref_k.reshape(positions, HEADS, head_dim)
    ref_vh = ref_v.reshape(positions, HEADS, head_dim)
    scale = 1.0 / math.sqrt(head_dim)
    self_scores = jnp.einsum("fqhd,fkhd->fhqk", q1, k1, preferred_element_type=jnp.float32) * scale
    ref_scores = (
        jnp.einsum("fqhd,khd->fhqk", q1, ref_kh, preferred_element_type=jnp.float32) * scale
    )
    top = jnp.maximum(
        jnp.max(self_scores, axis=-1, keepdims=True), jnp.max(ref_scores, axis=-1, keepdims=True)
    )
    self_exp = jnp.exp(self_scores - top)
    ref_exp = jnp.exp(ref_scores - top)
    total = jnp.sum(self_exp, axis=-1, keepdims=True) + jnp.sum(ref_exp, axis=-1, keepdims=True)
    self_probs = (self_exp / total).astype(jnp.bfloat16)
    ref_probs = (ref_exp / total).astype(jnp.bfloat16)
    attn_1 = jnp.einsum("fhqk,fkhd->fqhd", self_probs, v1, preferred_element_type=jnp.float32)
    attn_1 = attn_1 + jnp.einsum(
        "fhqk,khd->fqhd", ref_probs, ref_vh, preferred_element_type=jnp.float32
    )
    attn_1 = attn_1.astype(jnp.bfloat16).reshape(frames_here, positions, width)
    mid = base + jnp.dot(attn_1, sp_out, preferred_element_type=jnp.float32)
    encoding = positional(frame_index, width)
    normed_2 = (layer_norm(mid, norm_gain_2) + encoding[:, None, :]).astype(jnp.bfloat16)
    moved = (
        project(normed_2, tm_query).reshape(frames_here, blocks, share, width),
        project(normed_2, tm_key).reshape(frames_here, blocks, share, width),
        project(normed_2, tm_value).reshape(frames_here, blocks, share, width),
    )
    result = temporal_attend(
        flatten_block(lax.all_to_all(moved[0], "frame", split_axis=1, concat_axis=0, tiled=True)),
        flatten_block(lax.all_to_all(moved[1], "frame", split_axis=1, concat_axis=0, tiled=True)),
        flatten_block(lax.all_to_all(moved[2], "frame", split_axis=1, concat_axis=0, tiled=True)),
    )
    attn_2 = result.reshape(result.shape[0], 1, result.shape[1], result.shape[2])
    returned = lax.all_to_all(attn_2, "frame", split_axis=0, concat_axis=1, tiled=True).reshape(
        frames_here, positions, width
    )
    return (mid + jnp.dot(returned, tm_out, preferred_element_type=jnp.float32)).astype(
        jnp.bfloat16
    )


def layer_norm_down(values, gain):
    mean = jnp.mean(values, axis=0, keepdims=True)
    centered = values - mean
    var = jnp.mean(centered * centered, axis=0, keepdims=True)
    return centered * lax.rsqrt(var + 1e-05) * gain


def project_down(weight, rows, contract):
    return lax.dot_general(
        weight, rows, (((0,), (contract,)), ((), ())), preferred_element_type=jnp.float32
    )


def head_span(head, head_dim, width):
    low = head * head_dim
    high = low + head_dim
    return low, high, low // 128 * 128, min(width, -(-high // 128) * 128)


def unpack(both, width):
    split = 2 * width - width // 128 * 128
    return both[..., :width], jnp.concatenate([both[..., split:], both[..., width:split]], axis=-1)


def finish_kernel(attn_hbm, mid_hbm, tmo_hbm, out_hbm, attn_ref, mid_ref, tmo_ref, out_ref, load_sem, store_sem):
    halves, frames_here, width, count = mid_ref.shape
    weight = pltpu.make_async_copy(tmo_hbm, tmo_ref, load_sem.at[halves, 0])
    weight.start()
    loads = []
    for half in range(halves):
        pair = (
            pltpu.make_async_copy(attn_hbm.at[half], attn_ref.at[half], load_sem.at[half, 0]),
            pltpu.make_async_copy(mid_hbm.at[half], mid_ref.at[half], load_sem.at[half, 1]),
        )
        for load in pair:
            load.start()
        loads.append(pair)
    weight.wait()
    stores = []
    for half in range(halves):
        for load in loads[half]:
            load.wait()
        columns = pl.ds(half * count, count)
        for f, attn in enumerate(unpack(attn_ref[half], width)):
            attn = attn.reshape(count, width)
            mixed = mid_ref[half, f] + project_down(tmo_ref[...], attn, 1)
            out_ref[f, :, half * count : (half + 1) * count] = mixed.astype(jnp.bfloat16)
            stores.append(
                pltpu.make_async_copy(
                    out_ref.at[f, :, columns], out_hbm.at[f, :, columns], store_sem.at[half, f]
                )
            )
            stores[-1].start()
    for store in stores:
        store.wait()


def fused_kernel(
    blocks,
    step_hbm,
    frame_hbm,
    hidden_hbm,
    ref_hbm,
    temb_hbm,
    gain1_hbm,
    gain2_hbm,
    spq_hbm,
    spk_hbm,
    spv_hbm,
    spo_hbm,
    tmq_hbm,
    tmk_hbm,
    tmv_hbm,
    attn_hbm,
    mid_hbm,
    own_sem,
    mid_sem,
    step_ref,
    frame_ref,
    hidden_ref,
    ref_ref,
    temb_ref,
    gain1_ref,
    gain2_ref,
    spq_ref,
    spk_ref,
    spv_ref,
    spo_ref,
    tmq_ref,
    tmk_ref,
    tmv_ref,
    load_sem,
    ref_buf,
    q_buf,
    k_buf,
    self_buf,
    top_buf,
    sum_buf,
    v_buf,
    mid_buf,
    pe_buf,
    gain2_buf,
    fwd_out,
    fwd_in,
    bwd_out,
    ref_send,
    ref_recv,
    fwd_send,
    fwd_recv,
    bwd_send,
    bwd_recv,
):
    me = lax.axis_index("frame")
    frames_here, width, positions = hidden_ref.shape
    halves, rows = fwd_out.shape[0], fwd_out.shape[2]
    count = blocks * rows
    frames = frames_here * blocks
    head_dim = width // HEADS
    bf16 = jnp.bfloat16

    def peer(shift):
        return lax.rem(me + shift, blocks)

    loads = [
        pltpu.make_async_copy(source, target, load_sem.at[place])
        for place, (source, target) in enumerate(
            (
                (ref_hbm, ref_ref),
                (gain1_hbm, gain1_ref),
                (step_hbm, step_ref),
                (frame_hbm, frame_ref),
                (temb_hbm, temb_ref),
                (hidden_hbm, hidden_ref),
                (spq_hbm, spq_ref),
                (spk_hbm, spk_ref),
                (spv_hbm, spv_ref),
                (gain2_hbm, gain2_ref),
                (spo_hbm, spo_ref),
                (tmq_hbm, tmq_ref),
                (tmk_hbm, tmk_ref),
                (tmv_hbm, tmv_ref),
            )
        )
    ]
    for load in loads:
        load.start()

    barrier = pltpu.get_barrier_semaphore()
    for shift in range(1, blocks):
        pl.semaphore_signal(
            barrier, inc=1, device_id={"frame": peer(shift)}, device_id_type=pl.DeviceIdType.MESH
        )

    for load in loads[:2]:
        load.wait()
    gain1 = gain1_ref[...].reshape(1, width)
    ref_buf[me] = layer_norm(ref_ref[...].astype(jnp.float32), gain1).astype(bf16)
    pl.semaphore_wait(barrier, blocks - 1)

    def ref_copy(shift):
        return pltpu.make_async_remote_copy(
            src_ref=ref_buf.at[me],
            dst_ref=ref_buf.at[me],
            send_sem=ref_send.at[shift - 1],
            recv_sem=ref_recv.at[shift - 1],
            device_id={"frame": peer(shift)},
            device_id_type=pl.DeviceIdType.MESH,
        )

    whole = width // 128 * 128
    lanes = (pl.ds(0, whole), pl.ds(whole, 2 * width - whole))

    def fwd_copy(half, f, shift):
        return pltpu.make_async_remote_copy(
            src_ref=fwd_out.at[half, peer(shift), :, lanes[f]],
            dst_ref=fwd_in.at[half, me, :, lanes[f]],
            send_sem=fwd_send.at[half, f, shift - 1],
            recv_sem=fwd_recv.at[half, f, shift - 1],
            device_id={"frame": peer(shift)},
            device_id_type=pl.DeviceIdType.MESH,
        )

    def own_copy(half):
        return pltpu.make_async_copy(
            bwd_out.at[half, me], attn_hbm.at[half, me], own_sem.at[half]
        )

    def mid_copy(half, f):
        return pltpu.make_async_copy(
            mid_buf.at[half, f], mid_hbm.at[half, f], mid_sem.at[half, f]
        )

    def pack(first, second):
        return jnp.concatenate([first, second[..., whole:], second[..., :whole]], axis=-1)

    def bwd_copy(half, shift):
        return pltpu.make_async_remote_copy(
            src_ref=bwd_out.at[half, peer(shift)],
            dst_ref=attn_hbm.at[half, me],
            send_sem=bwd_send.at[half, shift - 1],
            recv_sem=bwd_recv.at[half, shift - 1],
            device_id={"frame": peer(shift)},
            device_id_type=pl.DeviceIdType.MESH,
        )

    for shift in range(1, blocks):
        ref_copy(shift).start()

    def column(row):
        return jnp.broadcast_to(row, (count, width)).T

    for load in loads[2:9]:
        load.wait()
    steps = temb_ref.shape[1]
    chosen = lax.broadcasted_iota(jnp.int32, (steps, count), 0) == step_ref[0]
    temb = jnp.dot(
        temb_ref[...],
        jnp.where(chosen, 1.0, 0.0).astype(bf16),
        preferred_element_type=jnp.float32,
    )

    chan = lax.broadcasted_iota(jnp.int32, (1, width), 1)
    freq = jnp.exp(-(chan // 2 * 2).astype(jnp.float32) / width * math.log(10000.0))
    phase = (chan % 2).astype(jnp.float32) * (math.pi / 2)
    for f in range(frames_here):
        pe_buf[f] = column(jnp.sin(frame_ref[f].astype(jnp.float32) * freq + phase))

    pair_shape = (HEADS // 2, 2 * head_dim, positions)

    def pair_span(pair):
        _, _, first, _ = head_span(2 * pair, head_dim, width)
        _, _, _, last = head_span(2 * pair + 1, head_dim, width)
        return first, last

    def by_head(pair, piece):
        row = lax.broadcasted_iota(jnp.int32, piece.shape, 0) + pair_span(pair)[0]
        start = 2 * pair * head_dim
        middle, end = start + head_dim, start + 2 * head_dim
        one = jnp.where((row >= start) & (row < middle), piece, 0.0)
        two = jnp.where((row >= middle) & (row < end), piece, 0.0)
        return jnp.concatenate([one, two], axis=1).astype(bf16)

    def raised(scores):
        top = jnp.max(scores, axis=0, keepdims=True)
        exps = jnp.exp2((scores - top) * factor)
        return top, exps, jnp.sum(exps, axis=0, keepdims=True)

    def own_rows(values, probs):
        both = jnp.dot(values, probs, preferred_element_type=jnp.float32)
        return [both[:head_dim, :count], both[head_dim:, count:]]

    factor = math.log2(math.e) / math.sqrt(head_dim)
    gain1 = column(gain1)
    for f in range(frames_here):
        normed = []
        for half in range(halves):
            base = hidden_ref[f, :, half * count : (half + 1) * count].astype(jnp.float32) + temb
            mid_buf[half, f] = base
            normed.append(layer_norm_down(base, gain1).astype(bf16))
        normed = jnp.concatenate(normed, axis=1)
        query = project_down(spq_ref[...], normed, 0)
        key = project(normed.T, spk_ref[...])
        for half in range(halves):
            for pair in range(HEADS // 2):
                first, last = pair_span(pair)
                picked = by_head(pair, query[first:last, half * count : (half + 1) * count])
                q_buf[half, f, pair, : last - first] = picked
                top, exps, total = raised(
                    jnp.dot(key[:, first:last], picked, preferred_element_type=jnp.float32)
                )
                self_buf[half, f, pair] = exps
                top_buf[half, f, pair] = top
                sum_buf[half, f, pair] = total
        value = project_down(spv_ref[...], normed, 0)
        v_buf[f, :, :, :positions] = value.reshape(pair_shape).astype(bf16)

    for load in loads[9:11]:
        load.wait()
    gain2_buf[...] = column(gain2_ref[...].reshape(1, width))
    for shift in range(1, blocks):
        ref_copy(shift).wait_recv()
    ref_all = ref_buf[...].reshape(-1, width)
    k_buf[...] = project(ref_all, spk_ref[...])
    ref_value = project_down(spv_ref[...], ref_all, 1)
    ref_value = ref_value.reshape(pair_shape).astype(bf16)
    for f in range(frames_here):
        v_buf[f, :, :, positions:] = ref_value


    def spatial(half, carry):
        def score(f, pair):
            first, last = pair_span(pair)
            return jnp.dot(
                k_buf[:, first:last],
                q_buf[half, f, pair, : last - first],
                preferred_element_type=jnp.float32,
            )

        units = [(f, pair) for f in range(frames_here) for pair in range(HEADS // 2)]
        ahead = score(*units[0])
        for f in range(frames_here):
            done = []
            for pair in range(HEADS // 2):
                scores = ahead
                place = units.index((f, pair)) + 1
                if place < len(units):
                    ahead = score(*units[place])
                ref_top, exps, total = raised(scores)
                self_top = top_buf[half, f, pair]
                top = jnp.maximum(self_top, ref_top)
                self_part = jnp.exp2((self_top - top) * factor)
                ref_part = jnp.exp2((ref_top - top) * factor)
                inverse = 1.0 / (sum_buf[half, f, pair] * self_part + total * ref_part)
                probs = [
                    (self_buf[half, f, pair] * (self_part * inverse)).astype(bf16),
                    (exps * (ref_part * inverse)).astype(bf16),
                ]
                done += own_rows(v_buf[f, pair], jnp.concatenate(probs, axis=0))
            attn = jnp.concatenate(done, axis=0).astype(bf16)
            mid = mid_buf[half, f] + project_down(spo_ref[...], attn, 0)
            mid_buf[half, f] = mid
            mid_copy(half, f).start()
            normed = layer_norm_down(mid, gain2_buf[...]) + pe_buf[f]
            normed = normed.T.astype(bf16).reshape(blocks, rows, width)
            if f == 0:
                first_tail = normed[:, :, whole:]
                fwd_out[half, :, :, :whole] = normed[:, :, :whole]
            else:
                fwd_out[half, :, :, whole:] = jnp.concatenate(
                    [first_tail, normed[:, :, whole:], normed[:, :, :whole]], axis=-1
                )
            for shift in range(1, blocks):
                fwd_copy(half, f, shift).start()
        fwd_in[half, me] = fwd_out[half, me]
        return carry

    lax.fori_loop(0, halves, spatial, 0)

    for load in loads[11:]:
        load.wait()
    group = 8
    row_pos = lax.broadcasted_iota(jnp.int32, (count, 2 * count), 0) % group
    col_pos = lax.broadcasted_iota(jnp.int32, (count, 2 * count), 1) % group
    same = row_pos == col_pos

    def temporal(half, carry):
        for shift in range(1, blocks):
            for f in range(frames_here):
                fwd_copy(half, f, shift).wait_recv()
        normed = jnp.concatenate(unpack(fwd_in[half], width), axis=0).astype(jnp.float32)
        normed = normed.reshape(frames, rows // group, group, width)
        normed = jnp.concatenate(
            [normed[:, g].reshape(count, width) for g in range(rows // group)], axis=0
        ).astype(bf16)
        query = project_down(tmq_ref[...], normed, 1)
        key = project(normed, tmk_ref[...])
        value = project_down(tmv_ref[...], normed, 1).reshape(HEADS // 2, 2 * head_dim, -1)
        value = value.astype(bf16)

        def score(g, pair):
            first, last = pair_span(pair)
            columns = slice(g * count, (g + 1) * count)
            picked = by_head(pair, query[first:last, columns])
            found = jnp.dot(
                key[columns, first:last], picked, preferred_element_type=jnp.float32
            )
            return jnp.where(same, found, -1e30)

        done = []
        for g in range(rows // group):
            attn = []
            for pair in range(HEADS // 2):
                _, exps, total = raised(score(g, pair))
                probs = (exps * (1.0 / total)).astype(bf16)
                attn += own_rows(value[pair, :, g * count : (g + 1) * count], probs)
            attn = jnp.concatenate(attn, axis=0).T
            done.append(attn.reshape(frames, 1, group, width))
        attn = jnp.concatenate(done, axis=1).reshape(frames, rows, width).astype(bf16)
        bwd_out[half] = pack(attn[:blocks], attn[blocks:])
        for shift in range(1, blocks):
            bwd_copy(half, shift).start()
        own_copy(half).start()
        return carry

    lax.fori_loop(0, halves, temporal, 0)

    for half in range(halves):
        own_copy(half).wait()
        for f in range(frames_here):
            mid_copy(half, f).wait()
        for shift in range(1, blocks):
            bwd_copy(half, shift).wait_recv()
    for shift in range(1, blocks):
        ref_copy(shift).wait_send()
        for half in range(halves):
            for f in range(frames_here):
                fwd_copy(half, f, shift).wait_send()
            bwd_copy(half, shift).wait_send()


def on_device_fused(
    hidden,
    ref_feats,
    frame_index,
    step_index,
    temb_table,
    norm_gain_1,
    norm_gain_2,
    *weights,
):
    frames_here, positions, width = hidden.shape
    blocks = lax.axis_size("frame")
    share = positions // blocks
    halves = 2
    rows = share // halves
    count = blocks * rows
    ref_rows = ref_feats.shape[0]
    bf16 = jnp.bfloat16
    dma = pltpu.SemaphoreType.DMA
    args = (
        step_index,
        frame_index,
        hidden.transpose(0, 2, 1),
        ref_feats,
        temb_table.T,
        norm_gain_1,
        norm_gain_2,
        *weights[:-1],
    )
    hbm = pl.BlockSpec(memory_space=pltpu.HBM)
    moved = (halves, blocks, rows, frames_here * width)
    params = pltpu.CompilerParams(vmem_limit_bytes=60 * 1024 * 1024)
    attn, mid = pl.pallas_call(
        functools.partial(fused_kernel, blocks),
        out_shape=(
            jax.ShapeDtypeStruct(moved, bf16),
            jax.ShapeDtypeStruct((halves, frames_here, width, count), jnp.float32),
        ),
        in_specs=[hbm] * len(args),
        out_specs=(hbm, hbm),
        scratch_shapes=[dma((halves,)), dma((halves, frames_here))]
        + [pltpu.SMEM(a.shape, a.dtype) for a in args[:2]]
        + [pltpu.VMEM(a.shape, a.dtype) for a in args[2:]]
        + [
            dma((len(args),)),
            pltpu.VMEM((blocks, ref_rows, width), bf16),
            pltpu.VMEM((halves, frames_here, HEADS // 2, 256, 2 * count), bf16),
            pltpu.VMEM((blocks * ref_rows, width), bf16),
            pltpu.VMEM((halves, frames_here, HEADS // 2, positions, 2 * count), jnp.float32),
            pltpu.VMEM((halves, frames_here, HEADS // 2, 1, 2 * count), jnp.float32),
            pltpu.VMEM((halves, frames_here, HEADS // 2, 1, 2 * count), jnp.float32),
            pltpu.VMEM((frames_here, HEADS // 2, 2 * width // HEADS, 2 * positions), bf16),
            pltpu.VMEM((halves, frames_here, width, count), jnp.float32),
            pltpu.VMEM((frames_here, width, count), jnp.float32),
            pltpu.VMEM((width, count), jnp.float32),
            pltpu.VMEM(moved, bf16),
            pltpu.VMEM(moved, bf16),
            pltpu.VMEM(moved, bf16),
            dma((blocks - 1,)),
            dma((blocks - 1,)),
            dma((halves, frames_here, blocks - 1)),
            dma((halves, frames_here, blocks - 1)),
            dma((halves, blocks - 1)),
            dma((halves, blocks - 1)),
        ],
        compiler_params=pltpu.CompilerParams(
            collective_id=0, has_side_effects=True, vmem_limit_bytes=60 * 1024 * 1024
        ),
    )(*args)
    out_shape = (frames_here, width, positions)
    out = pl.pallas_call(
        finish_kernel,
        out_shape=jax.ShapeDtypeStruct(out_shape, bf16),
        in_specs=[hbm] * 3,
        out_specs=hbm,
        scratch_shapes=[
            pltpu.VMEM(moved, bf16),
            pltpu.VMEM(mid.shape, jnp.float32),
            pltpu.VMEM(weights[-1].shape, bf16),
            pltpu.VMEM(out_shape, bf16),
            dma((halves + 1, 2)),
            dma((halves, frames_here)),
        ],
        compiler_params=params,
    )(attn, mid, weights[-1])
    return out.transpose(0, 2, 1)


def on_device(hidden, ref_feats, frame_index, step_index, temb_table, *rest):
    blocks = lax.axis_size("frame")
    frames_here, positions, width = hidden.shape
    fits = (
        positions == 256
        and positions % (32 * blocks) == 0
        and frames_here == 2
        and 2 * width % 128 == 0
        and blocks * ref_feats.shape[0] == positions
        and ref_feats.shape[0] % 16 == 0
        and frames_here * blocks * 8 == positions // 2
    )
    body = on_device_fused if fits else on_device_plain
    return body(hidden, ref_feats, frame_index, step_index, temb_table, *rest)


def solution(mesh):
    in_specs = (
        P(("video", "frame"), None, None),
        P(("video", "frame"), None),
        P(("video", "frame")),
        P(),
        P(),
        P(),
        P(),
        P(),
        P(),
        P(),
        P(),
        P(),
        P(),
        P(),
        P(),
    )
    out_specs = P(("video", "frame"), None, None)
    return jax.shard_map(
        on_device, mesh=mesh, in_specs=in_specs, out_specs=out_specs, check_vma=False
    )
```

```python
import functools
import math

import jax
import jax.numpy as jnp
from jax import lax
from jax.experimental import pallas as pl
from jax.experimental.pallas import tpu as pltpu
from jax.sharding import PartitionSpec as P

HEADS = 8


def layer_norm(values, gain):
    mean = jnp.mean(values, axis=-1, keepdims=True)
    centered = values - mean
    var = jnp.mean(centered * centered, axis=-1, keepdims=True)
    return centered * lax.rsqrt(var + 1e-05) * gain


def positional(frame_index, width):
    chan = jnp.arange(width)
    freq = jnp.exp(-(chan // 2 * 2).astype(jnp.float32) / width * math.log(10000.0))
    phase = (chan % 2).astype(jnp.float32) * (math.pi / 2)
    return jnp.sin(frame_index.astype(jnp.float32)[:, None] * freq[None, :] + phase[None, :])


def project(rows, weight):
    return jnp.dot(rows, weight, preferred_element_type=jnp.float32).astype(jnp.bfloat16)


def temporal_attend(query, keys, values):
    frames, count, width = query.shape
    head_dim = width // HEADS
    q = query.reshape(frames, count, HEADS, head_dim)
    k = keys.reshape(frames, count, HEADS, head_dim)
    v = values.reshape(frames, count, HEADS, head_dim)
    scores = jnp.einsum("fnhd,gnhd->nhfg", q, k, preferred_element_type=jnp.float32) / math.sqrt(
        head_dim
    )
    probs = jax.nn.softmax(scores, axis=-1).astype(jnp.bfloat16)
    out = jnp.einsum("nhfg,gnhd->fnhd", probs, v, preferred_element_type=jnp.float32)
    return out.astype(jnp.bfloat16).reshape(frames, count, width)


def flatten_block(block):
    return block.reshape(block.shape[0], block.shape[2], block.shape[3])


def on_device_plain(
    hidden,
    ref_feats,
    frame_index,
    step_index,
    temb_table,
    norm_gain_1,
    norm_gain_2,
    sp_query,
    sp_key,
    sp_value,
    sp_out,
    tm_query,
    tm_key,
    tm_value,
    tm_out,
):
    frames_here, positions, width = hidden.shape
    head_dim = width // HEADS
    blocks = lax.axis_size("frame")
    share = positions // blocks
    temb = lax.dynamic_slice_in_dim(temb_table, step_index[0], 1, 0).astype(jnp.float32)
    base = hidden.astype(jnp.float32) + temb[None, :, :]
    normed_1 = layer_norm(base, norm_gain_1).astype(jnp.bfloat16)
    ref_local = layer_norm(ref_feats.astype(jnp.float32), norm_gain_1).astype(jnp.bfloat16)
    ref_all = lax.all_gather(ref_local, "frame", axis=0, tiled=True)
    ref_k = project(ref_all, sp_key)
    ref_v = project(ref_all, sp_value)
    q1 = project(normed_1, sp_query).reshape(frames_here, positions, HEADS, head_dim)
    k1 = project(normed_1, sp_key).reshape(frames_here, positions, HEADS, head_dim)
    v1 = project(normed_1, sp_value).reshape(frames_here, positions, HEADS, head_dim)
    ref_kh = ref_k.reshape(positions, HEADS, head_dim)
    ref_vh = ref_v.reshape(positions, HEADS, head_dim)
    scale = 1.0 / math.sqrt(head_dim)
    self_scores = jnp.einsum("fqhd,fkhd->fhqk", q1, k1, preferred_element_type=jnp.float32) * scale
    ref_scores = (
        jnp.einsum("fqhd,khd->fhqk", q1, ref_kh, preferred_element_type=jnp.float32) * scale
    )
    top = jnp.maximum(
        jnp.max(self_scores, axis=-1, keepdims=True), jnp.max(ref_scores, axis=-1, keepdims=True)
    )
    self_exp = jnp.exp(self_scores - top)
    ref_exp = jnp.exp(ref_scores - top)
    total = jnp.sum(self_exp, axis=-1, keepdims=True) + jnp.sum(ref_exp, axis=-1, keepdims=True)
    self_probs = (self_exp / total).astype(jnp.bfloat16)
    ref_probs = (ref_exp / total).astype(jnp.bfloat16)
    attn_1 = jnp.einsum("fhqk,fkhd->fqhd", self_probs, v1, preferred_element_type=jnp.float32)
    attn_1 = attn_1 + jnp.einsum(
        "fhqk,khd->fqhd", ref_probs, ref_vh, preferred_element_type=jnp.float32
    )
    attn_1 = attn_1.astype(jnp.bfloat16).reshape(frames_here, positions, width)
    mid = base + jnp.dot(attn_1, sp_out, preferred_element_type=jnp.float32)
    encoding = positional(frame_index, width)
    normed_2 = (layer_norm(mid, norm_gain_2) + encoding[:, None, :]).astype(jnp.bfloat16)
    moved = (
        project(normed_2, tm_query).reshape(frames_here, blocks, share, width),
        project(normed_2, tm_key).reshape(frames_here, blocks, share, width),
        project(normed_2, tm_value).reshape(frames_here, blocks, share, width),
    )
    result = temporal_attend(
        flatten_block(lax.all_to_all(moved[0], "frame", split_axis=1, concat_axis=0, tiled=True)),
        flatten_block(lax.all_to_all(moved[1], "frame", split_axis=1, concat_axis=0, tiled=True)),
        flatten_block(lax.all_to_all(moved[2], "frame", split_axis=1, concat_axis=0, tiled=True)),
    )
    attn_2 = result.reshape(result.shape[0], 1, result.shape[1], result.shape[2])
    returned = lax.all_to_all(attn_2, "frame", split_axis=0, concat_axis=1, tiled=True).reshape(
        frames_here, positions, width
    )
    return (mid + jnp.dot(returned, tm_out, preferred_element_type=jnp.float32)).astype(
        jnp.bfloat16
    )


def layer_norm_down(values, gain):
    mean = jnp.mean(values, axis=0, keepdims=True)
    centered = values - mean
    var = jnp.mean(centered * centered, axis=0, keepdims=True)
    return centered * lax.rsqrt(var + 1e-05) * gain


def project_down(weight, rows, contract):
    return lax.dot_general(
        weight, rows, (((0,), (contract,)), ((), ())), preferred_element_type=jnp.float32
    )


def head_span(head, head_dim, width):
    low = head * head_dim
    high = low + head_dim
    return low, high, low // 128 * 128, min(width, -(-high // 128) * 128)


def unpack(both, width):
    split = 2 * width - width // 128 * 128
    return both[..., :width], jnp.concatenate([both[..., split:], both[..., width:split]], axis=-1)


def finish_kernel(attn_hbm, mid_hbm, tmo_hbm, out_hbm, attn_ref, mid_ref, tmo_ref, out_ref, load_sem, store_sem):
    halves, frames_here, width, count = mid_ref.shape
    weight = pltpu.make_async_copy(tmo_hbm, tmo_ref, load_sem.at[halves, 0])
    weight.start()
    loads = []
    for half in range(halves):
        pair = (
            pltpu.make_async_copy(attn_hbm.at[half], attn_ref.at[half], load_sem.at[half, 0]),
            pltpu.make_async_copy(mid_hbm.at[half], mid_ref.at[half], load_sem.at[half, 1]),
        )
        for load in pair:
            load.start()
        loads.append(pair)
    weight.wait()
    stores = []
    for half in range(halves):
        for load in loads[half]:
            load.wait()
        columns = pl.ds(half * count, count)
        for f, attn in enumerate(unpack(attn_ref[half], width)):
            attn = attn.reshape(count, width)
            mixed = mid_ref[half, f] + project_down(tmo_ref[...], attn, 1)
            out_ref[f, :, half * count : (half + 1) * count] = mixed.astype(jnp.bfloat16)
            stores.append(
                pltpu.make_async_copy(
                    out_ref.at[f, :, columns], out_hbm.at[f, :, columns], store_sem.at[half, f]
                )
            )
            stores[-1].start()
    for store in stores:
        store.wait()


def fused_kernel(
    blocks,
    step_hbm,
    frame_hbm,
    hidden_hbm,
    ref_hbm,
    temb_hbm,
    gain1_hbm,
    gain2_hbm,
    spq_hbm,
    spk_hbm,
    spv_hbm,
    spo_hbm,
    tmq_hbm,
    tmk_hbm,
    tmv_hbm,
    attn_hbm,
    mid_hbm,
    own_sem,
    mid_sem,
    step_ref,
    frame_ref,
    hidden_ref,
    ref_ref,
    temb_ref,
    gain1_ref,
    gain2_ref,
    spq_ref,
    spk_ref,
    spv_ref,
    spo_ref,
    tmq_ref,
    tmk_ref,
    tmv_ref,
    load_sem,
    ref_buf,
    q_buf,
    k_buf,
    self_buf,
    top_buf,
    sum_buf,
    v_buf,
    mid_buf,
    pe_buf,
    gain2_buf,
    fwd_out,
    fwd_in,
    bwd_out,
    ref_send,
    ref_recv,
    fwd_send,
    fwd_recv,
    bwd_send,
    bwd_recv,
):
    me = lax.axis_index("frame")
    frames_here, width, positions = hidden_ref.shape
    halves, rows = fwd_out.shape[0], fwd_out.shape[2]
    count = blocks * rows
    frames = frames_here * blocks
    head_dim = width // HEADS
    bf16 = jnp.bfloat16

    order = sorted(range(1, blocks), key=lambda shift: abs(2 * shift - blocks))

    def peer(shift):
        return lax.rem(me + shift, blocks)

    loads = [
        pltpu.make_async_copy(source, target, load_sem.at[place])
        for place, (source, target) in enumerate(
            (
                (ref_hbm, ref_ref),
                (gain1_hbm, gain1_ref),
                (step_hbm, step_ref),
                (frame_hbm, frame_ref),
                (temb_hbm, temb_ref),
                (hidden_hbm, hidden_ref),
                (spq_hbm, spq_ref),
                (spk_hbm, spk_ref),
                (spv_hbm, spv_ref),
                (gain2_hbm, gain2_ref),
                (spo_hbm, spo_ref),
                (tmq_hbm, tmq_ref),
                (tmk_hbm, tmk_ref),
                (tmv_hbm, tmv_ref),
            )
        )
    ]
    for load in loads:
        load.start()

    barrier = pltpu.get_barrier_semaphore()
    for shift in range(1, blocks):
        pl.semaphore_signal(
            barrier, inc=1, device_id={"frame": peer(shift)}, device_id_type=pl.DeviceIdType.MESH
        )

    for load in loads[:2]:
        load.wait()
    gain1 = gain1_ref[...].reshape(1, width)
    ref_buf[me] = layer_norm(ref_ref[...].astype(jnp.float32), gain1).astype(bf16)
    pl.semaphore_wait(barrier, blocks - 1)

    def ref_copy(shift):
        return pltpu.make_async_remote_copy(
            src_ref=ref_buf.at[me],
            dst_ref=ref_buf.at[me],
            send_sem=ref_send.at[shift - 1],
            recv_sem=ref_recv.at[shift - 1],
            device_id={"frame": peer(shift)},
            device_id_type=pl.DeviceIdType.MESH,
        )

    whole = width // 128 * 128
    lanes = (pl.ds(0, whole), pl.ds(whole, 2 * width - whole))

    def fwd_copy(half, f, shift):
        return pltpu.make_async_remote_copy(
            src_ref=fwd_out.at[half, peer(shift), :, lanes[f]],
            dst_ref=fwd_in.at[half, me, :, lanes[f]],
            send_sem=fwd_send.at[half, f, shift - 1],
            recv_sem=fwd_recv.at[half, f, shift - 1],
            device_id={"frame": peer(shift)},
            device_id_type=pl.DeviceIdType.MESH,
        )

    def own_copy(half):
        return pltpu.make_async_copy(
            bwd_out.at[half, me], attn_hbm.at[half, me], own_sem.at[half]
        )

    def mid_copy(half, f):
        return pltpu.make_async_copy(
            mid_buf.at[half, f], mid_hbm.at[half, f], mid_sem.at[half, f]
        )

    def pack(first, second):
        return jnp.concatenate([first, second[..., whole:], second[..., :whole]], axis=-1)

    def bwd_copy(half, shift):
        return pltpu.make_async_remote_copy(
            src_ref=bwd_out.at[half, peer(shift)],
            dst_ref=attn_hbm.at[half, me],
            send_sem=bwd_send.at[half, shift - 1],
            recv_sem=bwd_recv.at[half, shift - 1],
            device_id={"frame": peer(shift)},
            device_id_type=pl.DeviceIdType.MESH,
        )

    for shift in order:
        ref_copy(shift).start()

    def column(row):
        return jnp.broadcast_to(row, (count, width)).T

    for load in loads[2:9]:
        load.wait()
    steps = temb_ref.shape[1]
    chosen = lax.broadcasted_iota(jnp.int32, (steps, count), 0) == step_ref[0]
    temb = jnp.dot(
        temb_ref[...],
        jnp.where(chosen, 1.0, 0.0).astype(bf16),
        preferred_element_type=jnp.float32,
    )

    chan = lax.broadcasted_iota(jnp.int32, (1, width), 1)
    freq = jnp.exp(-(chan // 2 * 2).astype(jnp.float32) / width * math.log(10000.0))
    phase = (chan % 2).astype(jnp.float32) * (math.pi / 2)
    for f in range(frames_here):
        pe_buf[f] = column(jnp.sin(frame_ref[f].astype(jnp.float32) * freq + phase))

    pair_shape = (HEADS // 2, 2 * head_dim, positions)

    def pair_span(pair):
        _, _, first, _ = head_span(2 * pair, head_dim, width)
        _, _, _, last = head_span(2 * pair + 1, head_dim, width)
        return first, last

    def by_head(pair, piece):
        row = lax.broadcasted_iota(jnp.int32, piece.shape, 0) + pair_span(pair)[0]
        start = 2 * pair * head_dim
        middle, end = start + head_dim, start + 2 * head_dim
        one = jnp.where((row >= start) & (row < middle), piece, 0.0)
        two = jnp.where((row >= middle) & (row < end), piece, 0.0)
        return jnp.concatenate([one, two], axis=1).astype(bf16)

    def raised(scores):
        top = jnp.max(scores, axis=0, keepdims=True)
        exps = jnp.exp2((scores - top) * factor)
        return top, exps, jnp.sum(exps, axis=0, keepdims=True)

    def own_rows(values, probs):
        both = jnp.dot(values, probs, preferred_element_type=jnp.float32)
        return [both[:head_dim, :count], both[head_dim:, count:]]

    factor = math.log2(math.e) / math.sqrt(head_dim)
    gain1 = column(gain1)
    for f in range(frames_here):
        normed = []
        for half in range(halves):
            base = hidden_ref[f, :, half * count : (half + 1) * count].astype(jnp.float32) + temb
            mid_buf[half, f] = base
            normed.append(layer_norm_down(base, gain1).astype(bf16))
        normed = jnp.concatenate(normed, axis=1)
        query = project_down(spq_ref[...], normed, 0)
        key = project(normed.T, spk_ref[...])
        for half in range(halves):
            for pair in range(HEADS // 2):
                first, last = pair_span(pair)
                picked = by_head(pair, query[first:last, half * count : (half + 1) * count])
                q_buf[half, f, pair, : last - first] = picked
                top, exps, total = raised(
                    jnp.dot(key[:, first:last], picked, preferred_element_type=jnp.float32)
                )
                self_buf[half, f, pair] = exps
                top_buf[half, f, pair] = top
                sum_buf[half, f, pair] = total
        value = project_down(spv_ref[...], normed, 0)
        v_buf[f, :, :, :positions] = value.reshape(pair_shape).astype(bf16)

    for load in loads[9:11]:
        load.wait()
    gain2_buf[...] = column(gain2_ref[...].reshape(1, width))
    for shift in range(1, blocks):
        ref_copy(shift).wait_recv()
    ref_all = ref_buf[...].reshape(-1, width)
    k_buf[...] = project(ref_all, spk_ref[...])
    ref_value = project_down(spv_ref[...], ref_all, 1)
    ref_value = ref_value.reshape(pair_shape).astype(bf16)
    for f in range(frames_here):
        v_buf[f, :, :, positions:] = ref_value


    def spatial(half, carry):
        def score(f, pair):
            first, last = pair_span(pair)
            return jnp.dot(
                k_buf[:, first:last],
                q_buf[half, f, pair, : last - first],
                preferred_element_type=jnp.float32,
            )

        units = [(f, pair) for f in range(frames_here) for pair in range(HEADS // 2)]
        ahead = score(*units[0])
        for f in range(frames_here):
            done = []
            for pair in range(HEADS // 2):
                scores = ahead
                place = units.index((f, pair)) + 1
                if place < len(units):
                    ahead = score(*units[place])
                ref_top, exps, total = raised(scores)
                self_top = top_buf[half, f, pair]
                top = jnp.maximum(self_top, ref_top)
                self_part = jnp.exp2((self_top - top) * factor)
                ref_part = jnp.exp2((ref_top - top) * factor)
                inverse = 1.0 / (sum_buf[half, f, pair] * self_part + total * ref_part)
                probs = [
                    (self_buf[half, f, pair] * (self_part * inverse)).astype(bf16),
                    (exps * (ref_part * inverse)).astype(bf16),
                ]
                done += own_rows(v_buf[f, pair], jnp.concatenate(probs, axis=0))
            attn = jnp.concatenate(done, axis=0).astype(bf16)
            mid = mid_buf[half, f] + project_down(spo_ref[...], attn, 0)
            mid_buf[half, f] = mid
            mid_copy(half, f).start()
            normed = layer_norm_down(mid, gain2_buf[...]) + pe_buf[f]
            normed = normed.T.astype(bf16).reshape(blocks, rows, width)
            if f == 0:
                first_tail = normed[:, :, whole:]
                fwd_out[half, :, :, :whole] = normed[:, :, :whole]
            else:
                fwd_out[half, :, :, whole:] = jnp.concatenate(
                    [first_tail, normed[:, :, whole:], normed[:, :, :whole]], axis=-1
                )
            for shift in order:
                fwd_copy(half, f, shift).start()
        fwd_in[half, me] = fwd_out[half, me]
        return carry

    lax.fori_loop(0, halves, spatial, 0)

    for load in loads[11:]:
        load.wait()
    group = 8
    row_pos = lax.broadcasted_iota(jnp.int32, (count, 2 * count), 0) % group
    col_pos = lax.broadcasted_iota(jnp.int32, (count, 2 * count), 1) % group
    same = row_pos == col_pos

    def temporal(half, carry):
        for shift in range(1, blocks):
            for f in range(frames_here):
                fwd_copy(half, f, shift).wait_recv()
        normed = jnp.concatenate(unpack(fwd_in[half], width), axis=0).astype(jnp.float32)
        normed = normed.reshape(frames, rows // group, group, width)
        normed = jnp.concatenate(
            [normed[:, g].reshape(count, width) for g in range(rows // group)], axis=0
        ).astype(bf16)
        query = project_down(tmq_ref[...], normed, 1)
        key = project(normed, tmk_ref[...])
        value = project_down(tmv_ref[...], normed, 1).reshape(HEADS // 2, 2 * head_dim, -1)
        value = value.astype(bf16)

        def score(g, pair):
            first, last = pair_span(pair)
            columns = slice(g * count, (g + 1) * count)
            picked = by_head(pair, query[first:last, columns])
            found = jnp.dot(
                key[columns, first:last], picked, preferred_element_type=jnp.float32
            )
            return jnp.where(same, found, -1e30)

        done = []
        for g in range(rows // group):
            attn = []
            for pair in range(HEADS // 2):
                _, exps, total = raised(score(g, pair))
                probs = (exps * (1.0 / total)).astype(bf16)
                attn += own_rows(value[pair, :, g * count : (g + 1) * count], probs)
            attn = jnp.concatenate(attn, axis=0).T
            done.append(attn.reshape(frames, 1, group, width))
        attn = jnp.concatenate(done, axis=1).reshape(frames, rows, width).astype(bf16)
        bwd_out[half] = pack(attn[:blocks], attn[blocks:])
        for shift in order:
            bwd_copy(half, shift).start()
        own_copy(half).start()
        return carry

    lax.fori_loop(0, halves, temporal, 0)

    for half in range(halves):
        own_copy(half).wait()
        for f in range(frames_here):
            mid_copy(half, f).wait()
        for shift in range(1, blocks):
            bwd_copy(half, shift).wait_recv()
    for shift in range(1, blocks):
        ref_copy(shift).wait_send()
        for half in range(halves):
            for f in range(frames_here):
                fwd_copy(half, f, shift).wait_send()
            bwd_copy(half, shift).wait_send()


def on_device_fused(
    hidden,
    ref_feats,
    frame_index,
    step_index,
    temb_table,
    norm_gain_1,
    norm_gain_2,
    *weights,
):
    frames_here, positions, width = hidden.shape
    blocks = lax.axis_size("frame")
    share = positions // blocks
    halves = 2
    rows = share // halves
    count = blocks * rows
    ref_rows = ref_feats.shape[0]
    bf16 = jnp.bfloat16
    dma = pltpu.SemaphoreType.DMA
    args = (
        step_index,
        frame_index,
        hidden.transpose(0, 2, 1),
        ref_feats,
        temb_table.T,
        norm_gain_1,
        norm_gain_2,
        *weights[:-1],
    )
    hbm = pl.BlockSpec(memory_space=pltpu.HBM)
    moved = (halves, blocks, rows, frames_here * width)
    params = pltpu.CompilerParams(vmem_limit_bytes=60 * 1024 * 1024)
    attn, mid = pl.pallas_call(
        functools.partial(fused_kernel, blocks),
        out_shape=(
            jax.ShapeDtypeStruct(moved, bf16),
            jax.ShapeDtypeStruct((halves, frames_here, width, count), jnp.float32),
        ),
        in_specs=[hbm] * len(args),
        out_specs=(hbm, hbm),
        scratch_shapes=[dma((halves,)), dma((halves, frames_here))]
        + [pltpu.SMEM(a.shape, a.dtype) for a in args[:2]]
        + [pltpu.VMEM(a.shape, a.dtype) for a in args[2:]]
        + [
            dma((len(args),)),
            pltpu.VMEM((blocks, ref_rows, width), bf16),
            pltpu.VMEM((halves, frames_here, HEADS // 2, 256, 2 * count), bf16),
            pltpu.VMEM((blocks * ref_rows, width), bf16),
            pltpu.VMEM((halves, frames_here, HEADS // 2, positions, 2 * count), jnp.float32),
            pltpu.VMEM((halves, frames_here, HEADS // 2, 1, 2 * count), jnp.float32),
            pltpu.VMEM((halves, frames_here, HEADS // 2, 1, 2 * count), jnp.float32),
            pltpu.VMEM((frames_here, HEADS // 2, 2 * width // HEADS, 2 * positions), bf16),
            pltpu.VMEM((halves, frames_here, width, count), jnp.float32),
            pltpu.VMEM((frames_here, width, count), jnp.float32),
            pltpu.VMEM((width, count), jnp.float32),
            pltpu.VMEM(moved, bf16),
            pltpu.VMEM(moved, bf16),
            pltpu.VMEM(moved, bf16),
            dma((blocks - 1,)),
            dma((blocks - 1,)),
            dma((halves, frames_here, blocks - 1)),
            dma((halves, frames_here, blocks - 1)),
            dma((halves, blocks - 1)),
            dma((halves, blocks - 1)),
        ],
        compiler_params=pltpu.CompilerParams(
            collective_id=0, has_side_effects=True, vmem_limit_bytes=60 * 1024 * 1024
        ),
    )(*args)
    out_shape = (frames_here, width, positions)
    out = pl.pallas_call(
        finish_kernel,
        out_shape=jax.ShapeDtypeStruct(out_shape, bf16),
        in_specs=[hbm] * 3,
        out_specs=hbm,
        scratch_shapes=[
            pltpu.VMEM(moved, bf16),
            pltpu.VMEM(mid.shape, jnp.float32),
            pltpu.VMEM(weights[-1].shape, bf16),
            pltpu.VMEM(out_shape, bf16),
            dma((halves + 1, 2)),
            dma((halves, frames_here)),
        ],
        compiler_params=params,
    )(attn, mid, weights[-1])
    return out.transpose(0, 2, 1)


def on_device(hidden, ref_feats, frame_index, step_index, temb_table, *rest):
    blocks = lax.axis_size("frame")
    frames_here, positions, width = hidden.shape
    fits = (
        positions == 256
        and positions % (32 * blocks) == 0
        and frames_here == 2
        and 2 * width % 128 == 0
        and blocks * ref_feats.shape[0] == positions
        and ref_feats.shape[0] % 16 == 0
        and frames_here * blocks * 8 == positions // 2
    )
    body = on_device_fused if fits else on_device_plain
    return body(hidden, ref_feats, frame_index, step_index, temb_table, *rest)


def solution(mesh):
    in_specs = (
        P(("video", "frame"), None, None),
        P(("video", "frame"), None),
        P(("video", "frame")),
        P(),
        P(),
        P(),
        P(),
        P(),
        P(),
        P(),
        P(),
        P(),
        P(),
        P(),
        P(),
    )
    out_specs = P(("video", "frame"), None, None)
    return jax.shard_map(
        on_device, mesh=mesh, in_specs=in_specs, out_specs=out_specs, check_vma=False
    )
```

```python
import functools
import math

import jax
import jax.numpy as jnp
from jax import lax
from jax.experimental import pallas as pl
from jax.experimental.pallas import tpu as pltpu
from jax.sharding import PartitionSpec as P

HEADS = 8


def layer_norm(values, gain):
    mean = jnp.mean(values, axis=-1, keepdims=True)
    centered = values - mean
    var = jnp.mean(centered * centered, axis=-1, keepdims=True)
    return centered * lax.rsqrt(var + 1e-05) * gain


def positional(frame_index, width):
    chan = jnp.arange(width)
    freq = jnp.exp(-(chan // 2 * 2).astype(jnp.float32) / width * math.log(10000.0))
    phase = (chan % 2).astype(jnp.float32) * (math.pi / 2)
    return jnp.sin(frame_index.astype(jnp.float32)[:, None] * freq[None, :] + phase[None, :])


def project(rows, weight):
    return jnp.dot(rows, weight, preferred_element_type=jnp.float32).astype(jnp.bfloat16)


def temporal_attend(query, keys, values):
    frames, count, width = query.shape
    head_dim = width // HEADS
    q = query.reshape(frames, count, HEADS, head_dim)
    k = keys.reshape(frames, count, HEADS, head_dim)
    v = values.reshape(frames, count, HEADS, head_dim)
    scores = jnp.einsum("fnhd,gnhd->nhfg", q, k, preferred_element_type=jnp.float32) / math.sqrt(
        head_dim
    )
    probs = jax.nn.softmax(scores, axis=-1).astype(jnp.bfloat16)
    out = jnp.einsum("nhfg,gnhd->fnhd", probs, v, preferred_element_type=jnp.float32)
    return out.astype(jnp.bfloat16).reshape(frames, count, width)


def flatten_block(block):
    return block.reshape(block.shape[0], block.shape[2], block.shape[3])


def on_device_plain(
    hidden,
    ref_feats,
    frame_index,
    step_index,
    temb_table,
    norm_gain_1,
    norm_gain_2,
    sp_query,
    sp_key,
    sp_value,
    sp_out,
    tm_query,
    tm_key,
    tm_value,
    tm_out,
):
    frames_here, positions, width = hidden.shape
    head_dim = width // HEADS
    blocks = lax.axis_size("frame")
    share = positions // blocks
    temb = lax.dynamic_slice_in_dim(temb_table, step_index[0], 1, 0).astype(jnp.float32)
    base = hidden.astype(jnp.float32) + temb[None, :, :]
    normed_1 = layer_norm(base, norm_gain_1).astype(jnp.bfloat16)
    ref_local = layer_norm(ref_feats.astype(jnp.float32), norm_gain_1).astype(jnp.bfloat16)
    ref_all = lax.all_gather(ref_local, "frame", axis=0, tiled=True)
    ref_k = project(ref_all, sp_key)
    ref_v = project(ref_all, sp_value)
    q1 = project(normed_1, sp_query).reshape(frames_here, positions, HEADS, head_dim)
    k1 = project(normed_1, sp_key).reshape(frames_here, positions, HEADS, head_dim)
    v1 = project(normed_1, sp_value).reshape(frames_here, positions, HEADS, head_dim)
    ref_kh = ref_k.reshape(positions, HEADS, head_dim)
    ref_vh = ref_v.reshape(positions, HEADS, head_dim)
    scale = 1.0 / math.sqrt(head_dim)
    self_scores = jnp.einsum("fqhd,fkhd->fhqk", q1, k1, preferred_element_type=jnp.float32) * scale
    ref_scores = (
        jnp.einsum("fqhd,khd->fhqk", q1, ref_kh, preferred_element_type=jnp.float32) * scale
    )
    top = jnp.maximum(
        jnp.max(self_scores, axis=-1, keepdims=True), jnp.max(ref_scores, axis=-1, keepdims=True)
    )
    self_exp = jnp.exp(self_scores - top)
    ref_exp = jnp.exp(ref_scores - top)
    total = jnp.sum(self_exp, axis=-1, keepdims=True) + jnp.sum(ref_exp, axis=-1, keepdims=True)
    self_probs = (self_exp / total).astype(jnp.bfloat16)
    ref_probs = (ref_exp / total).astype(jnp.bfloat16)
    attn_1 = jnp.einsum("fhqk,fkhd->fqhd", self_probs, v1, preferred_element_type=jnp.float32)
    attn_1 = attn_1 + jnp.einsum(
        "fhqk,khd->fqhd", ref_probs, ref_vh, preferred_element_type=jnp.float32
    )
    attn_1 = attn_1.astype(jnp.bfloat16).reshape(frames_here, positions, width)
    mid = base + jnp.dot(attn_1, sp_out, preferred_element_type=jnp.float32)
    encoding = positional(frame_index, width)
    normed_2 = (layer_norm(mid, norm_gain_2) + encoding[:, None, :]).astype(jnp.bfloat16)
    moved = (
        project(normed_2, tm_query).reshape(frames_here, blocks, share, width),
        project(normed_2, tm_key).reshape(frames_here, blocks, share, width),
        project(normed_2, tm_value).reshape(frames_here, blocks, share, width),
    )
    result = temporal_attend(
        flatten_block(lax.all_to_all(moved[0], "frame", split_axis=1, concat_axis=0, tiled=True)),
        flatten_block(lax.all_to_all(moved[1], "frame", split_axis=1, concat_axis=0, tiled=True)),
        flatten_block(lax.all_to_all(moved[2], "frame", split_axis=1, concat_axis=0, tiled=True)),
    )
    attn_2 = result.reshape(result.shape[0], 1, result.shape[1], result.shape[2])
    returned = lax.all_to_all(attn_2, "frame", split_axis=0, concat_axis=1, tiled=True).reshape(
        frames_here, positions, width
    )
    return (mid + jnp.dot(returned, tm_out, preferred_element_type=jnp.float32)).astype(
        jnp.bfloat16
    )


def layer_norm_down(values, gain):
    mean = jnp.mean(values, axis=0, keepdims=True)
    centered = values - mean
    var = jnp.mean(centered * centered, axis=0, keepdims=True)
    return centered * lax.rsqrt(var + 1e-05) * gain


def project_down(weight, rows, contract):
    return lax.dot_general(
        weight, rows, (((0,), (contract,)), ((), ())), preferred_element_type=jnp.float32
    )


def head_span(head, head_dim, width):
    low = head * head_dim
    high = low + head_dim
    return low, high, low // 128 * 128, min(width, -(-high // 128) * 128)


def fused_kernel(
    blocks,
    step_hbm,
    frame_hbm,
    hidden_hbm,
    ref_hbm,
    temb_hbm,
    gain1_hbm,
    gain2_hbm,
    spq_hbm,
    spk_hbm,
    spv_hbm,
    spo_hbm,
    tmq_hbm,
    tmk_hbm,
    tmv_hbm,
    tmo_hbm,
    out_hbm,
    out_ref,
    store_sem,
    step_ref,
    frame_ref,
    hidden_ref,
    ref_ref,
    temb_ref,
    gain1_ref,
    gain2_ref,
    spq_ref,
    spk_ref,
    spv_ref,
    spo_ref,
    tmq_ref,
    tmk_ref,
    tmv_ref,
    tmo_ref,
    load_sem,
    ref_buf,
    q_buf,
    k_buf,
    self_buf,
    top_buf,
    sum_buf,
    v_buf,
    mid_buf,
    pe_buf,
    gain2_buf,
    fwd_out,
    fwd_in,
    bwd_out,
    bwd_in,
    ref_send,
    ref_recv,
    fwd_send,
    fwd_recv,
    bwd_send,
    bwd_recv,
):
    me = lax.axis_index("frame")
    frames_here, width, positions = hidden_ref.shape
    halves, rows = fwd_out.shape[0], fwd_out.shape[2]
    count = blocks * rows
    frames = frames_here * blocks
    head_dim = width // HEADS
    bf16 = jnp.bfloat16

    def peer(shift):
        return lax.rem(me + shift, blocks)

    loads = [
        pltpu.make_async_copy(source, target, load_sem.at[place])
        for place, (source, target) in enumerate(
            (
                (ref_hbm, ref_ref),
                (gain1_hbm, gain1_ref),
                (step_hbm, step_ref),
                (frame_hbm, frame_ref),
                (temb_hbm, temb_ref),
                (hidden_hbm, hidden_ref),
                (spq_hbm, spq_ref),
                (spk_hbm, spk_ref),
                (spv_hbm, spv_ref),
                (gain2_hbm, gain2_ref),
                (spo_hbm, spo_ref),
                (tmq_hbm, tmq_ref),
                (tmk_hbm, tmk_ref),
                (tmv_hbm, tmv_ref),
                (tmo_hbm, tmo_ref),
            )
        )
    ]
    for load in loads:
        load.start()

    barrier = pltpu.get_barrier_semaphore()
    for shift in range(1, blocks):
        pl.semaphore_signal(
            barrier, inc=1, device_id={"frame": peer(shift)}, device_id_type=pl.DeviceIdType.MESH
        )

    for load in loads[:2]:
        load.wait()
    gain1 = gain1_ref[...].reshape(1, width)
    ref_buf[me] = layer_norm(ref_ref[...].astype(jnp.float32), gain1).astype(bf16)
    pl.semaphore_wait(barrier, blocks - 1)

    def ref_copy(shift):
        return pltpu.make_async_remote_copy(
            src_ref=ref_buf.at[me],
            dst_ref=ref_buf.at[me],
            send_sem=ref_send.at[shift - 1],
            recv_sem=ref_recv.at[shift - 1],
            device_id={"frame": peer(shift)},
            device_id_type=pl.DeviceIdType.MESH,
        )

    whole = width // 128 * 128
    lanes = (pl.ds(0, whole), pl.ds(whole, 2 * width - whole))

    def fwd_copy(half, f, shift):
        return pltpu.make_async_remote_copy(
            src_ref=fwd_out.at[half, peer(shift), :, lanes[f]],
            dst_ref=fwd_in.at[half, me, :, lanes[f]],
            send_sem=fwd_send.at[half, f, shift - 1],
            recv_sem=fwd_recv.at[half, f, shift - 1],
            device_id={"frame": peer(shift)},
            device_id_type=pl.DeviceIdType.MESH,
        )

    def pack(first, second):
        return jnp.concatenate([first, second[..., whole:], second[..., :whole]], axis=-1)

    def unpack(both):
        second = [both[..., 2 * width - whole :], both[..., width : 2 * width - whole]]
        return both[..., :width], jnp.concatenate(second, axis=-1)

    def bwd_copy(half, shift):
        return pltpu.make_async_remote_copy(
            src_ref=bwd_out.at[half, peer(shift)],
            dst_ref=bwd_in.at[half, me],
            send_sem=bwd_send.at[half, shift - 1],
            recv_sem=bwd_recv.at[half, shift - 1],
            device_id={"frame": peer(shift)},
            device_id_type=pl.DeviceIdType.MESH,
        )

    for shift in range(1, blocks):
        ref_copy(shift).start()

    def column(row):
        return jnp.broadcast_to(row, (count, width)).T

    for load in loads[2:9]:
        load.wait()
    steps = temb_ref.shape[1]
    chosen = lax.broadcasted_iota(jnp.int32, (steps, count), 0) == step_ref[0]
    temb = jnp.dot(
        temb_ref[...],
        jnp.where(chosen, 1.0, 0.0).astype(bf16),
        preferred_element_type=jnp.float32,
    )

    chan = lax.broadcasted_iota(jnp.int32, (1, width), 1)
    freq = jnp.exp(-(chan // 2 * 2).astype(jnp.float32) / width * math.log(10000.0))
    phase = (chan % 2).astype(jnp.float32) * (math.pi / 2)
    for f in range(frames_here):
        pe_buf[f] = column(jnp.sin(frame_ref[f].astype(jnp.float32) * freq + phase))

    pair_shape = (HEADS // 2, 2 * head_dim, positions)

    def pair_span(pair):
        _, _, first, _ = head_span(2 * pair, head_dim, width)
        _, _, _, last = head_span(2 * pair + 1, head_dim, width)
        return first, last

    def by_head(pair, piece):
        row = lax.broadcasted_iota(jnp.int32, piece.shape, 0) + pair_span(pair)[0]
        start = 2 * pair * head_dim
        middle, end = start + head_dim, start + 2 * head_dim
        one = jnp.where((row >= start) & (row < middle), piece, 0.0)
        two = jnp.where((row >= middle) & (row < end), piece, 0.0)
        return jnp.concatenate([one, two], axis=1).astype(bf16)

    def raised(scores):
        top = jnp.max(scores, axis=0, keepdims=True)
        exps = jnp.exp2((scores - top) * factor)
        return top, exps, jnp.sum(exps, axis=0, keepdims=True)

    def own_rows(values, probs):
        both = jnp.dot(values, probs, preferred_element_type=jnp.float32)
        return [both[:head_dim, :count], both[head_dim:, count:]]

    factor = math.log2(math.e) / math.sqrt(head_dim)
    gain1 = column(gain1)
    for f in range(frames_here):
        normed = []
        for half in range(halves):
            base = hidden_ref[f, :, half * count : (half + 1) * count].astype(jnp.float32) + temb
            mid_buf[half, f] = base
            normed.append(layer_norm_down(base, gain1).astype(bf16))
        normed = jnp.concatenate(normed, axis=1)
        query = project_down(spq_ref[...], normed, 0)
        key = project(normed.T, spk_ref[...])
        for half in range(halves):
            for pair in range(HEADS // 2):
                first, last = pair_span(pair)
                picked = by_head(pair, query[first:last, half * count : (half + 1) * count])
                q_buf[half, f, pair, : last - first] = picked
                top, exps, total = raised(
                    jnp.dot(key[:, first:last], picked, preferred_element_type=jnp.float32)
                )
                self_buf[half, f, pair] = exps
                top_buf[half, f, pair] = top
                sum_buf[half, f, pair] = total
        value = project_down(spv_ref[...], normed, 0)
        v_buf[f, :, :, :positions] = value.reshape(pair_shape).astype(bf16)

    for load in loads[9:11]:
        load.wait()
    gain2_buf[...] = column(gain2_ref[...].reshape(1, width))
    for shift in range(1, blocks):
        ref_copy(shift).wait_recv()
    ref_all = ref_buf[...].reshape(-1, width)
    k_buf[...] = project(ref_all, spk_ref[...])
    ref_value = project_down(spv_ref[...], ref_all, 1)
    ref_value = ref_value.reshape(pair_shape).astype(bf16)
    for f in range(frames_here):
        v_buf[f, :, :, positions:] = ref_value


    def spatial(half, carry):
        def score(f, pair):
            first, last = pair_span(pair)
            return jnp.dot(
                k_buf[:, first:last],
                q_buf[half, f, pair, : last - first],
                preferred_element_type=jnp.float32,
            )

        units = [(f, pair) for f in range(frames_here) for pair in range(HEADS // 2)]
        ahead = score(*units[0])
        for f in range(frames_here):
            done = []
            for pair in range(HEADS // 2):
                scores = ahead
                place = units.index((f, pair)) + 1
                if place < len(units):
                    ahead = score(*units[place])
                ref_top, exps, total = raised(scores)
                self_top = top_buf[half, f, pair]
                top = jnp.maximum(self_top, ref_top)
                self_part = jnp.exp2((self_top - top) * factor)
                ref_part = jnp.exp2((ref_top - top) * factor)
                inverse = 1.0 / (sum_buf[half, f, pair] * self_part + total * ref_part)
                probs = [
                    (self_buf[half, f, pair] * (self_part * inverse)).astype(bf16),
                    (exps * (ref_part * inverse)).astype(bf16),
                ]
                done += own_rows(v_buf[f, pair], jnp.concatenate(probs, axis=0))
            attn = jnp.concatenate(done, axis=0).astype(bf16)
            mid = mid_buf[half, f] + project_down(spo_ref[...], attn, 0)
            mid_buf[half, f] = mid
            normed = layer_norm_down(mid, gain2_buf[...]) + pe_buf[f]
            normed = normed.T.astype(bf16).reshape(blocks, rows, width)
            if f == 0:
                first_tail = normed[:, :, whole:]
                fwd_out[half, :, :, :whole] = normed[:, :, :whole]
            else:
                fwd_out[half, :, :, whole:] = jnp.concatenate(
                    [first_tail, normed[:, :, whole:], normed[:, :, :whole]], axis=-1
                )
            for shift in range(1, blocks):
                fwd_copy(half, f, shift).start()
        fwd_in[half, me] = fwd_out[half, me]
        return carry

    lax.fori_loop(0, halves, spatial, 0)

    for load in loads[11:]:
        load.wait()
    group = 8
    row_pos = lax.broadcasted_iota(jnp.int32, (count, 2 * count), 0) % group
    col_pos = lax.broadcasted_iota(jnp.int32, (count, 2 * count), 1) % group
    same = row_pos == col_pos

    def temporal(half, carry):
        for shift in range(1, blocks):
            for f in range(frames_here):
                fwd_copy(half, f, shift).wait_recv()
        normed = jnp.concatenate(unpack(fwd_in[half]), axis=0).astype(jnp.float32)
        normed = normed.reshape(frames, rows // group, group, width)
        normed = jnp.concatenate(
            [normed[:, g].reshape(count, width) for g in range(rows // group)], axis=0
        ).astype(bf16)
        query = project_down(tmq_ref[...], normed, 1)
        key = project(normed, tmk_ref[...])
        value = project_down(tmv_ref[...], normed, 1).reshape(HEADS // 2, 2 * head_dim, -1)
        value = value.astype(bf16)

        def score(g, pair):
            first, last = pair_span(pair)
            columns = slice(g * count, (g + 1) * count)
            picked = by_head(pair, query[first:last, columns])
            found = jnp.dot(
                key[columns, first:last], picked, preferred_element_type=jnp.float32
            )
            return jnp.where(same, found, -1e30)

        done = []
        for g in range(rows // group):
            attn = []
            for pair in range(HEADS // 2):
                _, exps, total = raised(score(g, pair))
                probs = (exps * (1.0 / total)).astype(bf16)
                attn += own_rows(value[pair, :, g * count : (g + 1) * count], probs)
            attn = jnp.concatenate(attn, axis=0).T
            done.append(attn.reshape(frames, 1, group, width))
        attn = jnp.concatenate(done, axis=1).reshape(frames, rows, width).astype(bf16)
        bwd_out[half] = pack(attn[:blocks], attn[blocks:])
        for shift in range(1, blocks):
            bwd_copy(half, shift).start()
        bwd_in[half, me] = bwd_out[half, me]
        return carry

    lax.fori_loop(0, halves, temporal, 0)

    stores = []
    for half in range(halves):
        for shift in range(1, blocks):
            bwd_copy(half, shift).wait_recv()
        for f, attn in enumerate(unpack(bwd_in[half])):
            attn = attn.reshape(count, width)
            mixed = mid_buf[half, f] + project_down(tmo_ref[...], attn, 1)
            out_ref[f, :, half * count : (half + 1) * count] = mixed.astype(bf16)
            stores.append(
                pltpu.make_async_copy(
                    out_ref.at[f, :, pl.ds(half * count, count)],
                    out_hbm.at[f, :, pl.ds(half * count, count)],
                    store_sem.at[half, f],
                )
            )
            stores[-1].start()

    for store in stores:
        store.wait()
    for shift in range(1, blocks):
        ref_copy(shift).wait_send()
        for half in range(halves):
            for f in range(frames_here):
                fwd_copy(half, f, shift).wait_send()
            bwd_copy(half, shift).wait_send()


def on_device_fused(
    hidden,
    ref_feats,
    frame_index,
    step_index,
    temb_table,
    norm_gain_1,
    norm_gain_2,
    *weights,
):
    frames_here, positions, width = hidden.shape
    blocks = lax.axis_size("frame")
    share = positions // blocks
    halves = 2
    rows = share // halves
    count = blocks * rows
    ref_rows = ref_feats.shape[0]
    bf16 = jnp.bfloat16
    dma = pltpu.SemaphoreType.DMA
    args = (
        step_index,
        frame_index,
        hidden.transpose(0, 2, 1),
        ref_feats,
        temb_table.T,
        norm_gain_1,
        norm_gain_2,
        *weights,
    )
    moved = (halves, blocks, rows, frames_here * width)
    out = pl.pallas_call(
        functools.partial(fused_kernel, blocks),
        out_shape=jax.ShapeDtypeStruct((frames_here, width, positions), bf16),
        in_specs=[pl.BlockSpec(memory_space=pltpu.HBM)] * len(args),
        out_specs=pl.BlockSpec(memory_space=pltpu.HBM),
        scratch_shapes=[pltpu.VMEM((frames_here, width, positions), bf16), dma((halves, frames_here))]
        + [pltpu.SMEM(a.shape, a.dtype) for a in args[:2]]
        + [pltpu.VMEM(a.shape, a.dtype) for a in args[2:]]
        + [
            dma((len(args),)),
            pltpu.VMEM((blocks, ref_rows, width), bf16),
            pltpu.VMEM((halves, frames_here, HEADS // 2, 256, 2 * count), bf16),
            pltpu.VMEM((blocks * ref_rows, width), bf16),
            pltpu.VMEM((halves, frames_here, HEADS // 2, positions, 2 * count), jnp.float32),
            pltpu.VMEM((halves, frames_here, HEADS // 2, 1, 2 * count), jnp.float32),
            pltpu.VMEM((halves, frames_here, HEADS // 2, 1, 2 * count), jnp.float32),
            pltpu.VMEM((frames_here, HEADS // 2, 2 * width // HEADS, 2 * positions), bf16),
            pltpu.VMEM((halves, frames_here, width, count), jnp.float32),
            pltpu.VMEM((frames_here, width, count), jnp.float32),
            pltpu.VMEM((width, count), jnp.float32),
            pltpu.VMEM(moved, bf16),
            pltpu.VMEM(moved, bf16),
            pltpu.VMEM(moved, bf16),
            pltpu.VMEM(moved, bf16),
            dma((blocks - 1,)),
            dma((blocks - 1,)),
            dma((halves, frames_here, blocks - 1)),
            dma((halves, frames_here, blocks - 1)),
            dma((halves, blocks - 1)),
            dma((halves, blocks - 1)),
        ],
        compiler_params=pltpu.CompilerParams(
            collective_id=0, has_side_effects=True, vmem_limit_bytes=60 * 1024 * 1024
        ),
    )(*args)
    return out.transpose(0, 2, 1)


def on_device(hidden, ref_feats, frame_index, step_index, temb_table, *rest):
    blocks = lax.axis_size("frame")
    frames_here, positions, width = hidden.shape
    fits = (
        positions == 256
        and positions % (32 * blocks) == 0
        and frames_here == 2
        and 2 * width % 128 == 0
        and blocks * ref_feats.shape[0] == positions
        and ref_feats.shape[0] % 16 == 0
        and frames_here * blocks * 8 == positions // 2
    )
    body = on_device_fused if fits else on_device_plain
    return body(hidden, ref_feats, frame_index, step_index, temb_table, *rest)


def solution(mesh):
    in_specs = (
        P(("video", "frame"), None, None),
        P(("video", "frame"), None),
        P(("video", "frame")),
        P(),
        P(),
        P(),
        P(),
        P(),
        P(),
        P(),
        P(),
        P(),
        P(),
        P(),
        P(),
    )
    out_specs = P(("video", "frame"), None, None)
    return jax.shard_map(
        on_device, mesh=mesh, in_specs=in_specs, out_specs=out_specs, check_vma=False
    )
```
